128 devices in a mesh: dp: 8 (over x, core), expert: 16 (over z, y).
Axes of the slice: x: 4, y: 4, z: 4, core: 2. Of those that a mesh axis runs over, the one named last changes fastest.
Arguments:
- tokens: bfloat16 [4096, 2048], P(('dp', 'expert')), may hold values from -6 to 6
- self_query: bfloat16 [4096, 2048], P(('dp', 'expert')), may hold values from -160 to 160
- new_kv: bfloat16 [4096, 4096], P(('dp', 'expert')), may hold values from -7 to 7
- kv_cache: bfloat16 [4096, 8, 4096], P(('dp', 'expert')), may hold values from -6 to 6
- parents: int32 [4096], P(('dp', 'expert')), may hold values from 0 to 3, as said below
- dec_len: int32 [1024], P('dp'), may hold values from 1 to 8
- cross_query: bfloat16 [4096, 2048], P(('dp', 'expert')), may hold values from -160 to 160
- memory: bfloat16 [1024, 64, 4096], P(('dp', 'expert')), may hold values from -7 to 7
- src_len: int32 [1024], P(('dp', 'expert')), may hold values from 2 to 64
- norm_gain: float32 [2048], replicated, may hold values from 0.1 to 1.9
- routes: int32 [4096, 2], P(('dp', 'expert')), may hold values from 0 to 15, all different within a row; in each aligned block of 32 rows (0 to 31, 32 to 63, ...) at most 8 rows name the same one
- gate_weights: float32 [4096, 2], P(('dp', 'expert')), may hold values from 0.2 to 1
- expert_in: bfloat16 [16, 2048, 8192], P('expert', None, 'dp'), may hold values from -0.125 to 0.125
- expert_out: bfloat16 [16, 8192, 2048], P('expert', 'dp'), may hold values from -0.0625 to 0.0625
Outputs:
- mixed: bfloat16 [4096, 2048], P(('dp', 'expert'))
- new_cache: bfloat16 [4096, 8, 4096], P(('dp', 'expert'))
The draws below stay inside these ranges and needn't reach their ends.
Inputs may be any that keep to these rules, and one draw needn't show every extreme that they name: `parents`: within the rows of one device at most 16 name the same parent beam, and one beam is named by exactly 16 of them. `routes`: A row names two different experts; within the rows of one device no expert is named more than 8 times.
All inputs are finite; a program needn't handle non-finite values.
Results may differ from the reference program's by a relative error of at most 0.014.
Values may be sent and summed in bfloat16 or wider, within the bound.
A program may use at most 128 MiB of HBM per device.

```python
import math
import jax
import jax.numpy as jnp
import numpy as np
from jax import lax

D = 2048
HEADS = 16
HEAD = 128
FF = 8192
BEAM = 4
ROW_DEV = 32
DEC_LEN = 8
SRC_LEN = 64
EXPERTS = 16
EG = 4
CAP_SRC = 8
PAGE_CAP = 16
ROWS = 4096
SENTS = 1024
N_EXPERT = 16


def parent_values(key):
    key = jax.random.fold_in(key, 101)
    key_top, key_order, key_other = jax.random.split(key, 3)
    blocks = ROWS // ROW_DEV
    favored = jax.random.randint(key_top, (blocks, 1), 0, BEAM)
    orders = jax.vmap(lambda single: jax.random.permutation(single, ROW_DEV))(jax.random.split(key_order, blocks))
    others = (favored + 1 + jax.random.randint(key_other, (blocks, ROW_DEV), 0, BEAM - 1)) % BEAM
    return jnp.where(orders < PAGE_CAP, favored, others).reshape(ROWS).astype(jnp.int32)


def cache_values(key):
    key = jax.random.fold_in(key, 102)
    return jax.random.truncated_normal(key, -6.0, 6.0, (ROWS, DEC_LEN, 2 * D), jnp.float32)


def memory_values(key):
    key = jax.random.fold_in(key, 104)
    return jax.random.truncated_normal(key, -6.0, 6.0, (SENTS, SRC_LEN, 2 * D), jnp.float32)


def draw_parents(key, part):
    values = parent_values(key)
    return values


def draw_kv_cache(key, part):
    values = cache_values(key)
    return values.astype(jnp.bfloat16)


def draw_new_kv(key, part):
    key = jax.random.fold_in(key, 3)
    values = jax.random.truncated_normal(key, -6.0, 6.0, (ROWS, 2 * D), jnp.float32)
    return values.astype(jnp.bfloat16)


def draw_self_query(key, part):
    key = jax.random.fold_in(key, 4)
    values = jax.random.truncated_normal(key, -6.0, 6.0, (ROWS, D), jnp.float32)
    return values.astype(jnp.bfloat16)


def draw_memory(key, part):
    values = memory_values(key)
    return values.astype(jnp.bfloat16)


def draw_cross_query(key, part):
    key = jax.random.fold_in(key, 6)
    values = jax.random.truncated_normal(key, -6.0, 6.0, (ROWS, D), jnp.float32)
    return values.astype(jnp.bfloat16)


def with_ends(values, rng, smallest, high):
    extent = values.shape
    index_at = [jax.random.randint(jax.random.fold_in(rng, axis), (), 0, extent[axis]) for axis in range(len(extent))]
    values = values.at[tuple(index_at)].set(smallest)
    longest = extent.index(max(extent))
    index_at[longest] = (index_at[longest] + 1) % extent[longest]
    return values.at[tuple(index_at)].set(high)


def steps_of(key, dims, cuts, smallest, top_value):
    def one(position, shards_of):
        heights = jax.random.uniform(jax.random.fold_in(jax.random.fold_in(key, 6), position), (shards_of,), jnp.float32, smallest / len(cuts), top_value / len(cuts))
        return jnp.repeat(jnp.exp(heights), dims[position] // shards_of).reshape((-1,) + (1,) * (len(dims) - position - 1))

    factor_of = one(*cuts[0])
    for cut in cuts[1:]:
        factor_of = factor_of * one(*cut)
    return factor_of


def shared_out(key, own, number, rows, amount, top, bound, lean):
    ranking = jax.random.permutation(key, amount)
    crowded, common = load_shares(amount, rows * top, bound, lean, True), load_shares(amount, rows * top, bound, lean, False)
    places = jnp.arange(amount)

    def named(sizes, rotation):
        used = int((sizes > 0).sum())
        fixed = max(1, used // 4)
        moved = fixed + (places - fixed + rotation * (used - fixed)) % max(1, amount - fixed)
        return jnp.zeros((amount,), jnp.int32).at[ranking[jnp.where(places < fixed, places, moved)]].set(jnp.asarray(sizes, jnp.int32))

    sizes = jnp.where(number % 4 == 0, named(crowded, number // 4), named(common, number - number // 4 - 1))
    mixed = jax.random.permutation(jax.random.fold_in(own, 3), amount)
    donor, sink = mixed[0:amount // 2 * 2:2], mixed[1:amount // 2 * 2:2]
    slack = jnp.minimum(sizes[donor] - 1, bound - sizes[sink]) // 2
    slack = jnp.where((donor == ranking[0]) | (sink == ranking[0]) | (sizes[sink] == 0), 0, jnp.maximum(slack, 0))
    moved = jax.random.randint(jax.random.fold_in(own, 4), (amount // 2,), 0, 1 << 20) % (slack + 1)
    sizes = sizes.at[donor].add(-moved).at[sink].add(moved)
    labels = jnp.searchsorted(jnp.cumsum(sizes), jnp.arange(rows * top), side="right").astype(jnp.int32)
    table = labels.reshape(top, rows).T
    table = table[jax.random.permutation(jax.random.fold_in(own, 1), rows)]
    rotation = jax.random.randint(jax.random.fold_in(own, 2), (rows, 1), 0, top)
    return jnp.take_along_axis(table, (jnp.arange(top)[None, :] + rotation) % top, axis=1)


def load_shares(count, total, most, skew, full):
    weights = [(1 << 20) // math.isqrt(standing ** skew) + 1 for standing in range(1, count + 1)]
    largest = most if full else min(most, max(-(-total // count), total * weights[0] // sum(weights)))
    least = 1 if total - largest >= count - 1 else 0
    given, rest = [largest] + [least] * (count - 1), total - largest - least * (count - 1)
    while rest > 0:
        movable = [i for i in range(1, count) if given[i] < largest] or [i for i in range(1, count) if given[i] < most]
        mass, remaining = sum([weights[i] for i in movable]), rest
        for i in movable:
            more = min(most - given[i], max(1, remaining * weights[i] // mass), rest)
            given[i] = given[i] + more
            rest = rest - more
    return np.array(given)


def normal_values(rng, dims, scale, bound, cuts=(), kind=jnp.bfloat16):
    loudness = steps_of(rng, dims, cuts, -0.22, 0.18) if cuts else 1.0
    values = jax.random.normal(rng, dims, jnp.float32) * scale * loudness
    return jnp.minimum(jnp.maximum(values, -bound), bound).astype(kind)


def setup_inputs(seed: int = 0) -> dict:
    splits = jax.random.split(jax.random.key(seed), 15)
    tokens = normal_values(splits[0], (ROWS, D), 1.0, 6.0, ((0, 128),))
    self_query = draw_self_query(jax.random.fold_in(splits[14], 71), 0)
    new_kv = draw_new_kv(jax.random.fold_in(splits[14], 71), 0)
    kv_cache = draw_kv_cache(jax.random.fold_in(splits[14], 71), 0)
    parents = draw_parents(jax.random.fold_in(splits[14], 71), 0)
    dec_len = with_ends(jax.random.randint(splits[5], (SENTS,), 1, DEC_LEN + 1), jax.random.fold_in(splits[5], 1), 1, DEC_LEN).astype(jnp.int32)
    cross_query = draw_cross_query(jax.random.fold_in(splits[14], 71), 0)
    memory = draw_memory(jax.random.fold_in(splits[14], 71), 0)
    src_len = with_ends(jax.random.randint(splits[8], (SENTS,), 2, SRC_LEN + 1), jax.random.fold_in(splits[8], 1), 2, SRC_LEN).astype(jnp.int32)
    norm_gain = jnp.clip(1.0 + 0.18 * jax.random.normal(splits[9], (D,), jnp.float32), 0.1, 1.9)
    routes_keys = jax.random.split(jax.random.fold_in(splits[10], 1), ROWS // ROW_DEV)
    routes_turns = jax.random.permutation(jax.random.fold_in(splits[10], 3), ROWS // ROW_DEV)
    routes = jax.vmap(lambda own, number: shared_out(jax.random.fold_in(splits[10], 2), own, number, ROW_DEV, EXPERTS, 2, CAP_SRC, 2))(routes_keys, routes_turns).reshape((ROWS, 2))
    gate_weights = jnp.clip(0.2 + 0.8 * jax.random.uniform(splits[11], (ROWS, 2), jnp.float32) ** steps_of(splits[11], (ROWS, 2), ((0, 128),), -0.2, 0.2), 0.2, 1.0)
    expert_in = normal_values(splits[12], (EXPERTS, D, FF), D ** -0.5, 0.125, ((0, 16), (2, 8)))
    expert_out = normal_values(splits[13], (EXPERTS, FF, D), FF ** -0.5, 0.0625, ((0, 16), (1, 8)))
    return {"tokens": tokens, "self_query": self_query, "new_kv": new_kv, "kv_cache": kv_cache, "parents": parents, "dec_len": dec_len, "cross_query": cross_query, "memory": memory, "src_len": src_len, "norm_gain": norm_gain, "routes": routes, "gate_weights": gate_weights, "expert_in": expert_in, "expert_out": expert_out}


def row_layout():
    row_ids = jnp.arange(ROWS, dtype=jnp.int32)
    block_ids = row_ids // ROW_DEV
    expert_pos = block_ids % N_EXPERT
    dp_pos = block_ids // N_EXPERT
    beam_ids = expert_pos // EG
    sentence = (dp_pos * EG + expert_pos % EG) * ROW_DEV + row_ids % ROW_DEV
    return (row_ids, beam_ids, sentence)

def self_attention(self_query, new_kv, new_cache, lengths):
    scale = 1.0 / math.sqrt(HEAD)
    queries = self_query.astype(jnp.float32).reshape(ROWS, HEADS, HEAD)
    keys = new_cache[:, :, :D].astype(jnp.float32).reshape(ROWS, DEC_LEN, HEADS, HEAD)
    values = new_cache[:, :, D:].astype(jnp.float32).reshape(ROWS, DEC_LEN, HEADS, HEAD)
    own_key = new_kv[:, :D].astype(jnp.float32).reshape(ROWS, HEADS, HEAD)
    own_value = new_kv[:, D:].astype(jnp.float32).reshape(ROWS, HEADS, HEAD)
    scores = jnp.einsum('rhk,rphk->rhp', queries, keys) * scale
    own = lax.optimization_barrier(jnp.sum(queries * own_key, -1)) * scale
    valid = (jnp.arange(DEC_LEN, dtype=jnp.int32)[None, :] < lengths[:, None])[:, None, :]
    peak = jnp.maximum(lax.optimization_barrier(jnp.max(jnp.where(valid, scores, -1e+30), -1)), own)
    cache_terms = jnp.where(valid, jnp.exp(scores - peak[..., None]), 0.0)
    own_term = jnp.exp(own - peak)
    total = lax.optimization_barrier(jnp.sum(cache_terms, -1)) + own_term
    cache_weights = (cache_terms / total[..., None]).astype(jnp.bfloat16)
    own_weight = (own_term / total).astype(jnp.bfloat16)
    result = jnp.einsum('rhp,rphk->rhk', cache_weights.astype(jnp.float32), values)
    result = result + own_weight.astype(jnp.float32)[..., None] * own_value
    return result.reshape(ROWS, D)

def cross_attention(cross_query, memory, src_len):
    scale = 1.0 / math.sqrt(HEAD)
    dp_count = ROWS // (N_EXPERT * ROW_DEV)
    queries = cross_query.reshape(dp_count, BEAM, EG, ROW_DEV, HEADS, HEAD)
    queries = queries.transpose(0, 2, 3, 1, 4, 5).reshape(dp_count * EG, ROW_DEV, BEAM, HEADS, HEAD)
    blocks = memory.reshape(dp_count * EG, ROW_DEV, SRC_LEN, 2 * D)
    lengths = src_len.reshape(dp_count * EG, ROW_DEV)

    def one_block(operands):
        block_q, block_m, block_l = operands
        keys = block_m[..., :D].astype(jnp.float32).reshape(ROW_DEV, SRC_LEN, HEADS, HEAD)
        values = block_m[..., D:].astype(jnp.float32).reshape(ROW_DEV, SRC_LEN, HEADS, HEAD)
        scores = jnp.einsum('sbhk,sphk->sbhp', block_q.astype(jnp.float32), keys) * scale
        valid = (jnp.arange(SRC_LEN, dtype=jnp.int32)[None, :] < block_l[:, None])[:, None, None, :]
        peak = lax.optimization_barrier(jnp.max(jnp.where(valid, scores, -1e+30), -1))
        terms = jnp.where(valid, jnp.exp(scores - peak[..., None]), 0.0)
        weights = terms / lax.optimization_barrier(jnp.sum(terms, -1))[..., None]
        return jnp.einsum('sbhp,sphk->sbhk', weights, values).reshape(ROW_DEV, BEAM, D)
    outputs = lax.map(one_block, (queries, blocks, lengths))
    outputs = outputs.reshape(dp_count, EG, ROW_DEV, BEAM, D).transpose(0, 3, 1, 2, 4)
    return outputs.reshape(ROWS, D)

def expert_outputs(moe_in, routes, expert_in, expert_out):
    flat_routes = routes.reshape(-1)
    most = ROWS // ROW_DEV * CAP_SRC

    def one_expert(operands):
        index, first_w, second_w = operands
        hits = flat_routes == index
        slots = jnp.nonzero(hits, size=most, fill_value=0)[0].astype(jnp.int32)
        filled = jnp.sum(hits.astype(jnp.int32))
        picked = moe_in[slots // 2]
        inner = jax.nn.relu(jnp.dot(picked, first_w, preferred_element_type=jnp.float32)).astype(jnp.bfloat16)
        result = jnp.dot(inner, second_w, preferred_element_type=jnp.float32).astype(jnp.bfloat16)
        target = jnp.where(jnp.arange(most, dtype=jnp.int32) < filled, slots, 2 * ROWS).astype(jnp.int32)
        return (result, target)
    results, targets = lax.map(one_expert, (jnp.arange(EXPERTS, dtype=jnp.int32), expert_in, expert_out))
    placed = jnp.zeros((2 * ROWS, D), jnp.float32)
    placed = placed.at[targets.reshape(-1)].set(results.reshape(-1, D).astype(jnp.float32), mode='drop')
    return placed.reshape(ROWS, 2, D)

def reference(tokens, self_query, new_kv, kv_cache, parents, dec_len, cross_query, memory, src_len, norm_gain, routes, gate_weights, expert_in, expert_out):
    row_ids, beam_ids, sentence = row_layout()
    parent_rows = (row_ids + (parents - beam_ids) * (EG * ROW_DEV)).astype(jnp.int32)
    new_cache = kv_cache[parent_rows]
    self_out = self_attention(self_query, new_kv, new_cache, dec_len[sentence])
    cross_out = cross_attention(cross_query, memory, src_len)
    hidden = tokens.astype(jnp.float32) + self_out + cross_out
    row_mean = lax.optimization_barrier(jnp.mean(hidden, -1, keepdims=True))
    centered = hidden - row_mean
    variance = lax.optimization_barrier(jnp.mean(centered * centered, -1, keepdims=True))
    moe_in = (centered * lax.rsqrt(variance + 1e-05) * norm_gain.astype(jnp.float32)).astype(jnp.bfloat16)
    per_slot = expert_outputs(moe_in, routes, expert_in, expert_out)
    mixed = hidden + lax.optimization_barrier(jnp.sum(gate_weights.astype(jnp.float32)[..., None] * per_slot, 1))
    return (mixed.astype(jnp.bfloat16), new_cache)
```

```python
import functools
import math

import jax
import jax.numpy as jnp
from jax import lax
from jax.experimental import pallas as pl
from jax.experimental.pallas import tpu as pltpu
from jax.sharding import PartitionSpec as P

HEAD = 128
BEAM = 4
GROUP = 4
CHIPS = 4
EXPERTS = 16
PAGE_CAP = 16
MESH = pl.DeviceIdType.MESH
ANY = pl.BlockSpec(memory_space=pl.ANY)
DMA = pltpu.SemaphoreType.DMA


def place():
    dp = lax.axis_index("dp")
    ex = lax.axis_index("expert")
    return dp, ex, lax.div(ex, GROUP), lax.rem(ex, GROUP)


def send(src, dst, send_sem, recv_sem, dp, ex):
    return pltpu.make_async_remote_copy(
        src_ref=src,
        dst_ref=dst,
        send_sem=send_sem,
        recv_sem=recv_sem,
        device_id=(dp, ex),
        device_id_type=MESH,
    )


def greet(barrier, dp, ex):
    pl.semaphore_signal(barrier, inc=1, device_id=(dp, ex), device_id_type=MESH)


def ask_kernel(
    query, cross, parents, queries, crosses, wishes,
    local, q_send, q_recv, p_send, p_recv, c_send, c_recv,
):
    dp, ex, z, y = place()
    barrier = pltpu.get_barrier_semaphore()
    for off in range(1, BEAM):
        greet(barrier, dp, lax.rem(z + off, BEAM) * GROUP + y)
    for beam in range(BEAM):
        pl.when(beam * GROUP + z != ex)(functools.partial(greet, barrier, dp, beam * GROUP + z))
    pl.semaphore_wait(barrier, jnp.where(z == y, 6, 7))

    crossing = [
        send(cross.at[p], crosses.at[z], c_send.at[p], c_recv.at[z], dp, y * GROUP + p)
        for p in range(GROUP)
    ]
    for p in range(GROUP):
        pl.when(y * GROUP + p != ex)(crossing[p].start)
    moves = []
    for off in (1, 3, 2):
        peer = lax.rem(z + off, BEAM) * GROUP + y
        moves.append(send(parents, wishes.at[z], p_send.at[off - 1], p_recv.at[off - 1], dp, peer))
        moves.append(send(query, queries.at[z], q_send.at[off - 1], q_recv.at[off - 1], dp, peer))
    for move in moves:
        move.start()
    stays = [
        pltpu.make_async_copy(query, queries.at[z], local.at[0]),
        pltpu.make_async_copy(parents, wishes.at[z], local.at[1]),
    ]
    for stay in stays:
        stay.start()
    own = pltpu.make_async_copy(cross.at[y], crosses.at[z], local.at[2])
    pl.when(z == y)(own.start)
    pl.when(z == y)(own.wait)
    for stay in stays:
        stay.wait()
    for move in moves:
        move.wait()
    for p in range(GROUP):
        pl.when(y * GROUP + p != ex)(crossing[p].wait_send)
    for beam in range(BEAM):
        coming = send(cross.at[0], crosses.at[beam], c_send.at[0], c_recv.at[beam], dp, beam * GROUP + z)
        pl.when(beam * GROUP + z != ex)(coming.wait_recv)


def ask(query, cross, parents):
    shapes = [jax.ShapeDtypeStruct((BEAM,) + a.shape, a.dtype) for a in (query, cross[0], parents)]
    return pl.pallas_call(
        ask_kernel,
        out_shape=shapes,
        in_specs=[ANY] * 3,
        out_specs=[ANY] * 3,
        scratch_shapes=[DMA((3,))] + [DMA((3,))] * 4 + [DMA((4,))] * 2,
        compiler_params=pltpu.CompilerParams(collective_id=0, has_side_effects=True),
        name="ask",
    )(query, cross, parents)


def answer_kernel(
    outs, stats, cross, got, got_stats, crosses,
    local, o_send, o_recv, t_send, t_recv, c_send, c_recv,
):
    dp, ex, z, y = place()
    barrier = pltpu.get_barrier_semaphore()
    for off in range(1, BEAM):
        greet(barrier, dp, lax.rem(z + off, BEAM) * GROUP + y)
    for p in range(GROUP):
        pl.when(y * GROUP + p != ex)(functools.partial(greet, barrier, dp, y * GROUP + p))
    pl.semaphore_wait(barrier, jnp.where(z == y, 6, 7))

    crossing = [
        send(cross.at[beam], crosses.at[y], c_send.at[beam], c_recv.at[y], dp, beam * GROUP + z)
        for beam in range(BEAM)
    ]
    for beam in range(BEAM):
        pl.when(beam * GROUP + z != ex)(crossing[beam].start)
    moves = []
    for off in (1, 3, 2):
        other = lax.rem(z + off, BEAM)
        peer = other * GROUP + y
        moves.append(send(stats.at[other], got_stats.at[z], t_send.at[off - 1], t_recv.at[off - 1], dp, peer))
        moves.append(send(outs.at[other], got.at[z], o_send.at[off - 1], o_recv.at[off - 1], dp, peer))
    for move in moves:
        move.start()
    stays = [
        pltpu.make_async_copy(outs.at[z], got.at[z], local.at[0]),
        pltpu.make_async_copy(stats.at[z], got_stats.at[z], local.at[1]),
    ]
    for stay in stays:
        stay.start()
    own = pltpu.make_async_copy(cross.at[z], crosses.at[y], local.at[2])
    pl.when(z == y)(own.start)
    pl.when(z == y)(own.wait)
    for stay in stays:
        stay.wait()
    for move in moves:
        move.wait()
    for beam in range(BEAM):
        pl.when(beam * GROUP + z != ex)(crossing[beam].wait_send)
    for p in range(GROUP):
        coming = send(cross.at[0], crosses.at[p], c_send.at[0], c_recv.at[p], dp, y * GROUP + p)
        pl.when(y * GROUP + p != ex)(coming.wait_recv)


def answer(outs, stats, cross):
    shapes = [jax.ShapeDtypeStruct(a.shape, a.dtype) for a in (outs, stats, cross)]
    return pl.pallas_call(
        answer_kernel,
        out_shape=shapes,
        in_specs=[ANY] * 3,
        out_specs=[ANY] * 3,
        scratch_shapes=[DMA((3,))] + [DMA((3,))] * 4 + [DMA((4,))] * 2,
        compiler_params=pltpu.CompilerParams(collective_id=1, has_side_effects=True),
        name="answer",
    )(outs, stats, cross)


def pack_kernel(wishes, cache, packed, sems):
    _, _, z, _ = place()
    rows = cache.shape[0]

    def each(act):
        for off in range(1, BEAM):
            asker = lax.rem(z + off, BEAM)

            def one(row, count):
                wanted = wishes[asker, row] == z
                page = pltpu.make_async_copy(
                    cache.at[row], packed.at[off - 1, count], sems.at[off - 1, row]
                )
                pl.when(wanted)(lambda: act(page))
                return count + wanted.astype(jnp.int32)

            lax.fori_loop(0, rows, one, jnp.int32(0))

    each(lambda page: page.start())
    each(lambda page: page.wait())


def pack(wishes, cache):
    return pl.pallas_call(
        pack_kernel,
        out_shape=jax.ShapeDtypeStruct((BEAM - 1, PAGE_CAP) + cache.shape[1:], cache.dtype),
        in_specs=[pl.BlockSpec(memory_space=pltpu.SMEM), ANY],
        out_specs=ANY,
        scratch_shapes=[DMA((BEAM - 1, cache.shape[0]))],
        name="pack",
    )(wishes, cache)


def unpack_kernel(parents, cache, arrived, fresh, sem):
    _, _, z, _ = place()
    rows = cache.shape[0]

    def begin(row, counts):
        parent = parents[row]
        off = lax.rem(z - parent + BEAM, BEAM)

        def keep():
            pltpu.make_async_copy(cache.at[row], fresh.at[row], sem).start()

        pl.when(off == 0)(keep)
        after = []
        for step in range(1, BEAM):
            hit = off == step

            def take(step=step):
                pltpu.make_async_copy(arrived.at[step - 1, counts[step - 1]], fresh.at[row], sem).start()

            pl.when(hit)(take)
            after.append(counts[step - 1] + hit.astype(jnp.int32))
        return tuple(after)

    lax.fori_loop(0, rows, begin, (jnp.int32(0),) * (BEAM - 1))
    pltpu.make_async_copy(cache, fresh, sem).wait()


def unpack(parents, cache, arrived):
    return pl.pallas_call(
        unpack_kernel,
        out_shape=jax.ShapeDtypeStruct(cache.shape, cache.dtype),
        in_specs=[pl.BlockSpec(memory_space=pltpu.SMEM), ANY, ANY],
        out_specs=ANY,
        scratch_shapes=[DMA],
        name="unpack",
    )(parents, cache, arrived)


ORDER = (0, 1, 3, 2)
OWN, LEFT, RIGHT, OPPOSITE = range(4)


def expert_kernel(
    slots, first, second, pages, returned, arrived,
    held, first_v, second_v, picked, inner, total, to_twin, from_twin, to_chip, from_chip, result,
    w_sem, local, d_send, d_recv, r_send, r_recv,
    g_send, g_recv, o_send, o_recv, t_send, t_recv,
    y_send, y_recv, x_send, x_recv, p_send, p_recv,
):
    dp, ex, z, y = place()
    x, core = lax.div(dp, 2), lax.rem(dp, 2)
    twin = x * 2 + 1 - core
    chip = [x, lax.rem(x + CHIPS - 1, CHIPS), lax.rem(x + 1, CHIPS), lax.rem(x + 2, CHIPS)]
    width = slots.shape[-1]
    hidden = first.shape[-1]
    block = EXPERTS * slots.shape[1]

    barrier = pltpu.get_barrier_semaphore()
    for a in range(BEAM):
        for b in range(GROUP):
            if a or b:
                greet(barrier, dp, lax.rem(z + a, BEAM) * GROUP + lax.rem(y + b, GROUP))
    greet(barrier, twin, ex)
    for side in (LEFT, RIGHT, OPPOSITE):
        greet(barrier, chip[side] * 2 + core, ex)
    loads = [
        pltpu.make_async_copy(first, first_v, w_sem.at[0]),
        pltpu.make_async_copy(second, second_v, w_sem.at[1]),
    ]
    for load in loads:
        load.start()
    pl.semaphore_wait(barrier, EXPERTS - 1 + 4)

    def peer(a, b):
        return lax.rem(z + a, BEAM) * GROUP + lax.rem(y + b, GROUP)

    def source(a, b):
        return lax.rem(z + BEAM - a, BEAM) * GROUP + lax.rem(y + GROUP - b, GROUP)

    home = held.at[x, core]
    stay = pltpu.make_async_copy(slots.at[ex], home.at[ex], local.at[0])
    stay.start()
    sent = []
    for a in ORDER:
        for b in range(GROUP):
            if a or b:
                spot = a * GROUP + b
                move = send(slots.at[peer(a, b)], home.at[ex], d_send.at[spot], d_recv.at[spot], dp, peer(a, b))
                move.start()
                sent.append(move)

    def chunk(which, owner, j):
        zz = lax.rem(z + BEAM - ORDER[j], BEAM)
        return held.at[chip[which], owner, pl.ds(zz * GROUP, GROUP)]

    def to_sibling(which, j):
        part = chunk(which, core, j)
        move = send(part, part, t_send.at[which, j], t_recv.at[which, j], twin, ex)
        move.start()
        sent.append(move)

    def from_sibling(which):
        for j in range(4):
            part = chunk(which, 1 - core, j)
            send(part, part, t_send.at[which, j], t_recv.at[which, j], twin, ex).wait_recv()

    stay.wait()
    for j, a in enumerate(ORDER):
        for b in range(GROUP):
            if a or b:
                spot = a * GROUP + b
                there = home.at[source(a, b)]
                send(there, there, d_send.at[spot], d_recv.at[spot], dp, source(a, b)).wait_recv()
        part = chunk(OWN, core, j)
        for way, side in ((0, RIGHT), (1, LEFT)):
            move = send(part, part, g_send.at[way, j], g_recv.at[way, j], chip[side] * 2 + core, ex)
            move.start()
            sent.append(move)
        to_sibling(OWN, j)

    paged = []
    for off in (1, 3, 2):
        move = send(
            pages.at[off - 1], arrived.at[off - 1], p_send.at[off - 1], p_recv.at[off - 1],
            dp, lax.rem(z + off, BEAM) * GROUP + y,
        )
        move.start()
        paged.append(move)

    def project(which):
        cells = picked.shape[0] // 2
        for half, owner in ((0, core), (1, 1 - core)):
            picked[half * cells : (half + 1) * cells, :] = held[chip[which], owner].reshape(cells, width)
        tile = min(256, hidden)

        @pl.loop(0, hidden // tile)
        def _(n):
            spot = pl.ds(pl.multiple_of(n * tile, tile), tile)
            part = jnp.dot(picked[...], first_v[:, spot], preferred_element_type=jnp.float32)
            inner[:, spot] = jnp.maximum(part, 0.0).astype(inner.dtype)

        wide = min(256, width)

        @pl.loop(0, width // wide)
        def _(n):
            spot = pl.ds(pl.multiple_of(n * wide, wide), wide)
            part = jnp.dot(inner[...], second_v[:, spot], preferred_element_type=jnp.float32)
            total[which, :, spot] = part[:cells]
            to_twin[which, :, spot] = part[cells:].astype(to_twin.dtype)

        move = send(to_twin.at[which], from_twin.at[which], y_send.at[which], y_recv.at[which], twin, ex)
        move.start()
        sent.append(move)

    def forward(which):
        there = from_twin.at[which]
        send(there, there, y_send.at[which], y_recv.at[which], twin, ex).wait_recv()
        wide = min(256, width)

        @pl.loop(0, width // wide)
        def _(n):
            spot = pl.ds(pl.multiple_of(n * wide, wide), wide)
            both = total[which, :, spot] + from_twin[which, :, spot].astype(jnp.float32)
            to_chip[which - 1, :, spot] = both.astype(to_chip.dtype)

        move = send(
            to_chip.at[which - 1], from_chip.at[which - 1], x_send.at[which - 1], x_recv.at[which - 1],
            chip[which] * 2 + core, ex,
        )
        move.start()
        sent.append(move)

    def landed(way, j):
        side = LEFT if way == 0 else RIGHT
        part = chunk(side, core, j)
        send(part, part, g_send.at[way, j], g_recv.at[way, j], dp, ex).wait_recv()
        to_sibling(side, j)
        if (j < 2) == (way == 0):
            onward = RIGHT if way == 0 else LEFT
            move = send(part, part, o_send.at[j], o_recv.at[j], chip[onward] * 2 + core, ex)
            move.start()
            sent.append(move)

    for load in loads:
        load.wait()
    from_sibling(OWN)
    project(OWN)
    for j in range(4):
        landed(0, j)
        landed(1, j)
    from_sibling(LEFT)
    project(LEFT)
    from_sibling(RIGHT)
    project(RIGHT)
    forward(LEFT)
    forward(RIGHT)
    for j in range(4):
        part = chunk(OPPOSITE, core, j)
        send(part, part, o_send.at[j], o_recv.at[j], dp, ex).wait_recv()
        to_sibling(OPPOSITE, j)
    from_sibling(OPPOSITE)
    project(OPPOSITE)
    forward(OPPOSITE)

    there = from_twin.at[OWN]
    send(there, there, y_send.at[OWN], y_recv.at[OWN], twin, ex).wait_recv()
    for which in (LEFT, RIGHT, OPPOSITE):
        there = from_chip.at[which - 1]
        send(there, there, x_send.at[which - 1], x_recv.at[which - 1], dp, ex).wait_recv()
    wide = min(256, width)

    @pl.loop(0, width // wide)
    def _(n):
        spot = pl.ds(pl.multiple_of(n * wide, wide), wide)
        whole = total[OWN, :, spot] + from_twin[OWN, :, spot].astype(jnp.float32)
        for which in (LEFT, RIGHT, OPPOSITE):
            whole = whole + from_chip[which - 1, :, spot].astype(jnp.float32)
        result[:, :, spot] = whole.astype(result.dtype).reshape(EXPERTS, block // EXPERTS, wide)

    stay = pltpu.make_async_copy(result.at[ex], returned.at[ex], local.at[1])
    stay.start()
    for a in (2, 1, 3, 0):
        for b in range(GROUP):
            if a or b:
                spot = a * GROUP + b
                move = send(result.at[peer(a, b)], returned.at[ex], r_send.at[spot], r_recv.at[spot], dp, peer(a, b))
                move.start()
                sent.append(move)
    stay.wait()
    for a in range(BEAM):
        for b in range(GROUP):
            if a or b:
                spot = a * GROUP + b
                there = returned.at[source(a, b)]
                send(there, there, r_send.at[spot], r_recv.at[spot], dp, source(a, b)).wait_recv()
    for move in sent:
        move.wait_send()
    for move in paged:
        move.wait()


def experts(slots, first, second, pages):
    count, cap, width = slots.shape
    hidden = first.shape[-1]
    block = count * cap
    kind = slots.dtype
    scratch = [
        pltpu.VMEM((CHIPS, 2, count, cap, width), kind),
        pltpu.VMEM(first.shape, kind),
        pltpu.VMEM(second.shape, kind),
        pltpu.VMEM((2 * block, width), kind),
        pltpu.VMEM((2 * block, hidden), kind),
        pltpu.VMEM((4, block, width), jnp.float32),
        pltpu.VMEM((4, block, width), kind),
        pltpu.VMEM((4, block, width), kind),
        pltpu.VMEM((3, block, width), kind),
        pltpu.VMEM((3, block, width), kind),
        pltpu.VMEM((count, cap, width), kind),
    ]
    sems = [
        DMA((2,)), DMA((2,)), DMA((16,)), DMA((16,)), DMA((16,)), DMA((16,)),
        DMA((2, 4)), DMA((2, 4)), DMA((4,)), DMA((4,)), DMA((4, 4)), DMA((4, 4)),
        DMA((4,)), DMA((4,)), DMA((3,)), DMA((3,)), DMA((3,)), DMA((3,)),
    ]
    return pl.pallas_call(
        expert_kernel,
        out_shape=[
            jax.ShapeDtypeStruct(slots.shape, kind),
            jax.ShapeDtypeStruct(pages.shape, pages.dtype),
        ],
        in_specs=[ANY] * 4,
        out_specs=[ANY] * 2,
        scratch_shapes=scratch + sems,
        compiler_params=pltpu.CompilerParams(
            collective_id=2, has_side_effects=True, vmem_limit_bytes=48 * 2**20
        ),
        name="experts",
    )(slots, first, second, pages)


def per_device(
    tokens,
    self_query,
    new_kv,
    kv_cache,
    parents,
    dec_len,
    cross_query,
    memory,
    src_len,
    norm_gain,
    routes,
    gate_weights,
    expert_in,
    expert_out,
):
    row_count, model_width = tokens.shape
    head_count = model_width // HEAD
    scale = 1.0 / math.sqrt(HEAD)
    expert_pos = lax.axis_index("expert")
    sub_pos = expert_pos % GROUP
    span = kv_cache.shape[1]
    quarter = row_count // BEAM

    queries, cross_q, wishes = ask(
        self_query, cross_query.reshape(GROUP, quarter, model_width), parents.reshape(1, row_count)
    )
    pages = pack(wishes.reshape(BEAM, row_count), kv_cache)

    keys = kv_cache[:, :, :model_width].reshape(row_count, span, head_count, HEAD)
    values = kv_cache[:, :, model_width:].reshape(row_count, span, head_count, HEAD)
    asked = queries.reshape(BEAM, row_count, head_count, HEAD)
    lengths = lax.dynamic_slice_in_dim(dec_len, sub_pos * row_count, row_count)
    valid = (jnp.arange(span, dtype=jnp.int32)[None, :] < lengths[:, None])[None, :, None, :]
    scores = jnp.einsum("brhk,rphk->brhp", asked, keys, preferred_element_type=jnp.float32) * scale
    peak = jnp.max(jnp.where(valid, scores, -1e30), -1)
    terms = jnp.where(valid, jnp.exp(scores - peak[..., None]), 0.0)
    mass = jnp.sum(terms, -1)
    weights = (terms / mass[..., None]).astype(jnp.bfloat16)
    outs = jnp.einsum("brhp,rphk->brhk", weights, values, preferred_element_type=jnp.float32)
    outs = outs.astype(jnp.bfloat16).reshape(BEAM, row_count, model_width)
    stats = jnp.pad(peak + jnp.log(mass), ((0, 0), (0, 0), (0, HEAD - head_count)))

    local_len = memory.shape[1]
    cross_q = cross_q.reshape(BEAM, quarter, head_count, HEAD)
    mem_keys = memory[:, :, :model_width].reshape(quarter, local_len, head_count, HEAD)
    mem_values = memory[:, :, model_width:].reshape(quarter, local_len, head_count, HEAD)
    cross_scores = (
        jnp.einsum("bshk,sphk->bshp", cross_q, mem_keys, preferred_element_type=jnp.float32) * scale
    )
    reach = (jnp.arange(local_len, dtype=jnp.int32)[None, :] < src_len[:, None])[None, :, None, :]
    cross_peak = jnp.max(jnp.where(reach, cross_scores, -1e30), -1)
    cross_terms = jnp.where(reach, jnp.exp(cross_scores - cross_peak[..., None]), 0.0)
    cross_weights = cross_terms / jnp.sum(cross_terms, -1)[..., None]
    owner_out = jnp.einsum(
        "bshp,sphk->bshk",
        cross_weights.astype(jnp.bfloat16),
        mem_values,
        preferred_element_type=jnp.float32,
    )
    owner_out = owner_out.astype(jnp.bfloat16).reshape(BEAM, quarter, model_width)

    got, got_stats, cross_out = answer(outs, stats, owner_out)

    own_key = new_kv[:, :model_width].reshape(row_count, head_count, HEAD)
    own_value = new_kv[:, model_width:].reshape(row_count, head_count, HEAD)
    own = (
        jnp.einsum(
            "rhk,rhk->rh",
            self_query.reshape(row_count, head_count, HEAD),
            own_key,
            preferred_element_type=jnp.float32,
        )
        * scale
    )
    chosen = parents[None, :] == jnp.arange(BEAM, dtype=jnp.int32)[:, None]
    cached = jnp.sum(jnp.where(chosen[..., None], got.astype(jnp.float32), 0.0), 0)
    level = jnp.sum(jnp.where(chosen[..., None], got_stats[..., :head_count], 0.0), 0)
    top = jnp.maximum(level, own)
    part = jnp.exp(level - top)
    own_part = jnp.exp(own - top)
    cache_share = part / (part + own_part)
    own_share = own_part / (part + own_part)
    self_out = (
        cache_share[..., None] * cached.reshape(row_count, head_count, HEAD)
        + own_share[..., None] * own_value.astype(jnp.float32)
    ).reshape(row_count, model_width)
    cross_out = cross_out.reshape(row_count, model_width).astype(jnp.float32)

    hidden = tokens.astype(jnp.float32) + self_out + cross_out
    row_mean = jnp.mean(hidden, -1, keepdims=True)
    centered = hidden - row_mean
    variance = jnp.mean(centered * centered, -1, keepdims=True)
    moe_in = (centered * lax.rsqrt(variance + 1e-05) * norm_gain).astype(jnp.bfloat16)

    slot_cap = 4 * row_count // EXPERTS
    named = routes[:, :, None] == jnp.arange(EXPERTS, dtype=jnp.int32)[None, None, :]
    per_row = jnp.sum(named.astype(jnp.int32), 1)
    before = jnp.cumsum(per_row, 0) - per_row
    slot = jnp.sum(jnp.where(named, before[:, None, :], 0), -1) + routes * slot_cap
    places = jnp.arange(EXPERTS * slot_cap, dtype=jnp.int32)
    taken = (slot[:, :, None] == places[None, None, :]).astype(jnp.bfloat16)
    table = (taken[:, 0] + taken[:, 1]).T
    slots = jnp.dot(table, moe_in, preferred_element_type=jnp.float32).astype(jnp.bfloat16)

    returned, arrived = experts(
        slots.reshape(EXPERTS, slot_cap, model_width), expert_in[0], expert_out[0], pages
    )
    per_slot = jnp.einsum(
        "rks,sd->rkd",
        taken,
        returned.reshape(EXPERTS * slot_cap, model_width),
        preferred_element_type=jnp.float32,
    )
    mixed = hidden + jnp.sum(gate_weights[..., None] * per_slot, 1)
    return (mixed.astype(jnp.bfloat16), unpack(parents, kv_cache, arrived))


def solution(mesh):
    placed = (
        P(("dp", "expert"), None),
        P(("dp", "expert"), None),
        P(("dp", "expert"), None),
        P(("dp", "expert"), None, None),
        P(("dp", "expert")),
        P("dp"),
        P(("dp", "expert"), None),
        P(("dp", "expert"), None, None),
        P(("dp", "expert")),
        P(),
        P(("dp", "expert"), None),
        P(("dp", "expert"), None),
        P("expert", None, "dp"),
        P("expert", "dp", None),
    )
    return jax.shard_map(
        per_device,
        mesh=mesh,
        in_specs=placed,
        out_specs=(P(("dp", "expert"), None), P(("dp", "expert"), None, None)),
        check_vma=False,
    )
```

```python
import functools
import math

import jax
import jax.numpy as jnp
from jax import lax
from jax.experimental import pallas as pl
from jax.experimental.pallas import tpu as pltpu
from jax.sharding import PartitionSpec as P

HEAD = 128
BEAM = 4
GROUP = 4
CHIPS = 4
EXPERTS = 16
PAGE_CAP = 16
MESH = pl.DeviceIdType.MESH
ANY = pl.BlockSpec(memory_space=pl.ANY)
DMA = pltpu.SemaphoreType.DMA


def place():
    dp = lax.axis_index("dp")
    ex = lax.axis_index("expert")
    return dp, ex, lax.div(ex, GROUP), lax.rem(ex, GROUP)


def send(src, dst, send_sem, recv_sem, dp, ex):
    return pltpu.make_async_remote_copy(
        src_ref=src,
        dst_ref=dst,
        send_sem=send_sem,
        recv_sem=recv_sem,
        device_id=(dp, ex),
        device_id_type=MESH,
    )


def greet(barrier, dp, ex):
    pl.semaphore_signal(barrier, inc=1, device_id=(dp, ex), device_id_type=MESH)


def ask_kernel(
    query, cross, parents, queries, crosses, wishes,
    local, q_send, q_recv, p_send, p_recv, c_send, c_recv,
):
    dp, ex, z, y = place()
    barrier = pltpu.get_barrier_semaphore()
    for off in range(1, BEAM):
        greet(barrier, dp, lax.rem(z + off, BEAM) * GROUP + y)
    for beam in range(BEAM):
        pl.when(beam * GROUP + z != ex)(functools.partial(greet, barrier, dp, beam * GROUP + z))
    pl.semaphore_wait(barrier, jnp.where(z == y, 6, 7))

    crossing = [
        send(cross.at[p], crosses.at[z], c_send.at[p], c_recv.at[z], dp, y * GROUP + p)
        for p in range(GROUP)
    ]
    for p in range(GROUP):
        pl.when(y * GROUP + p != ex)(crossing[p].start)
    moves = []
    for off in (1, 3, 2):
        peer = lax.rem(z + off, BEAM) * GROUP + y
        moves.append(send(parents, wishes.at[z], p_send.at[off - 1], p_recv.at[off - 1], dp, peer))
        moves.append(send(query, queries.at[z], q_send.at[off - 1], q_recv.at[off - 1], dp, peer))
    for move in moves:
        move.start()
    stays = [
        pltpu.make_async_copy(query, queries.at[z], local.at[0]),
        pltpu.make_async_copy(parents, wishes.at[z], local.at[1]),
    ]
    for stay in stays:
        stay.start()
    own = pltpu.make_async_copy(cross.at[y], crosses.at[z], local.at[2])
    pl.when(z == y)(own.start)
    pl.when(z == y)(own.wait)
    for stay in stays:
        stay.wait()
    for move in moves:
        move.wait()
    for p in range(GROUP):
        pl.when(y * GROUP + p != ex)(crossing[p].wait_send)
    for beam in range(BEAM):
        coming = send(cross.at[0], crosses.at[beam], c_send.at[0], c_recv.at[beam], dp, beam * GROUP + z)
        pl.when(beam * GROUP + z != ex)(coming.wait_recv)


def ask(query, cross, parents):
    shapes = [jax.ShapeDtypeStruct((BEAM,) + a.shape, a.dtype) for a in (query, cross[0], parents)]
    return pl.pallas_call(
        ask_kernel,
        out_shape=shapes,
        in_specs=[ANY] * 3,
        out_specs=[ANY] * 3,
        scratch_shapes=[DMA((3,))] + [DMA((3,))] * 4 + [DMA((4,))] * 2,
        compiler_params=pltpu.CompilerParams(collective_id=0, has_side_effects=True),
        name="ask",
    )(query, cross, parents)


def answer_kernel(
    outs, stats, cross, got, got_stats, crosses,
    local, o_send, o_recv, t_send, t_recv, c_send, c_recv,
):
    dp, ex, z, y = place()
    barrier = pltpu.get_barrier_semaphore()
    for off in range(1, BEAM):
        greet(barrier, dp, lax.rem(z + off, BEAM) * GROUP + y)
    for p in range(GROUP):
        pl.when(y * GROUP + p != ex)(functools.partial(greet, barrier, dp, y * GROUP + p))
    pl.semaphore_wait(barrier, jnp.where(z == y, 6, 7))

    crossing = [
        send(cross.at[beam], crosses.at[y], c_send.at[beam], c_recv.at[y], dp, beam * GROUP + z)
        for beam in range(BEAM)
    ]
    for beam in range(BEAM):
        pl.when(beam * GROUP + z != ex)(crossing[beam].start)
    moves = []
    for off in (1, 3, 2):
        other = lax.rem(z + off, BEAM)
        peer = other * GROUP + y
        moves.append(send(stats.at[other], got_stats.at[z], t_send.at[off - 1], t_recv.at[off - 1], dp, peer))
        moves.append(send(outs.at[other], got.at[z], o_send.at[off - 1], o_recv.at[off - 1], dp, peer))
    for move in moves:
        move.start()
    stays = [
        pltpu.make_async_copy(outs.at[z], got.at[z], local.at[0]),
        pltpu.make_async_copy(stats.at[z], got_stats.at[z], local.at[1]),
    ]
    for stay in stays:
        stay.start()
    own = pltpu.make_async_copy(cross.at[z], crosses.at[y], local.at[2])
    pl.when(z == y)(own.start)
    pl.when(z == y)(own.wait)
    for stay in stays:
        stay.wait()
    for move in moves:
        move.wait()
    for beam in range(BEAM):
        pl.when(beam * GROUP + z != ex)(crossing[beam].wait_send)
    for p in range(GROUP):
        coming = send(cross.at[0], crosses.at[p], c_send.at[0], c_recv.at[p], dp, y * GROUP + p)
        pl.when(y * GROUP + p != ex)(coming.wait_recv)


def answer(outs, stats, cross):
    shapes = [jax.ShapeDtypeStruct(a.shape, a.dtype) for a in (outs, stats, cross)]
    return pl.pallas_call(
        answer_kernel,
        out_shape=shapes,
        in_specs=[ANY] * 3,
        out_specs=[ANY] * 3,
        scratch_shapes=[DMA((3,))] + [DMA((3,))] * 4 + [DMA((4,))] * 2,
        compiler_params=pltpu.CompilerParams(collective_id=1, has_side_effects=True),
        name="answer",
    )(outs, stats, cross)


def pack_kernel(wishes, cache, packed, sems):
    _, _, z, _ = place()
    rows = cache.shape[0]

    def each(act):
        for off in range(1, BEAM):
            asker = lax.rem(z + off, BEAM)

            def one(row, count):
                wanted = wishes[asker, row] == z
                page = pltpu.make_async_copy(
                    cache.at[row], packed.at[off - 1, count], sems.at[off - 1, row]
                )
                pl.when(wanted)(lambda: act(page))
                return count + wanted.astype(jnp.int32)

            lax.fori_loop(0, rows, one, jnp.int32(0))

    each(lambda page: page.start())
    each(lambda page: page.wait())


def pack(wishes, cache):
    return pl.pallas_call(
        pack_kernel,
        out_shape=jax.ShapeDtypeStruct((BEAM - 1, PAGE_CAP) + cache.shape[1:], cache.dtype),
        in_specs=[pl.BlockSpec(memory_space=pltpu.SMEM), ANY],
        out_specs=pl.BlockSpec(memory_space=pltpu.VMEM),
        scratch_shapes=[DMA((BEAM - 1, cache.shape[0]))],
        compiler_params=pltpu.CompilerParams(vmem_limit_bytes=32 * 2**20),
        name="pack",
    )(wishes, cache)


def unpack_kernel(parents, cache, arrived, fresh, sem):
    _, _, z, _ = place()
    rows = cache.shape[0]

    def begin(row, counts):
        parent = parents[row]
        off = lax.rem(z - parent + BEAM, BEAM)

        def keep():
            pltpu.make_async_copy(cache.at[row], fresh.at[row], sem).start()

        pl.when(off == 0)(keep)
        after = []
        for step in range(1, BEAM):
            hit = off == step

            def take(step=step):
                pltpu.make_async_copy(arrived.at[step - 1, counts[step - 1]], fresh.at[row], sem).start()

            pl.when(hit)(take)
            after.append(counts[step - 1] + hit.astype(jnp.int32))
        return tuple(after)

    lax.fori_loop(0, rows, begin, (jnp.int32(0),) * (BEAM - 1))
    pltpu.make_async_copy(cache, fresh, sem).wait()


def unpack(parents, cache, arrived):
    return pl.pallas_call(
        unpack_kernel,
        out_shape=jax.ShapeDtypeStruct(cache.shape, cache.dtype),
        in_specs=[pl.BlockSpec(memory_space=pltpu.SMEM), ANY, ANY],
        out_specs=pl.BlockSpec(memory_space=pltpu.VMEM),
        scratch_shapes=[DMA],
        compiler_params=pltpu.CompilerParams(vmem_limit_bytes=32 * 2**20),
        name="unpack",
    )(parents, cache, arrived)


ORDER = (0, 1, 3, 2)
OWN, LEFT, RIGHT, OPPOSITE = range(4)


def expert_kernel(
    slots, first, second, pages, returned, arrived,
    held, first_v, second_v, picked, inner, total, to_twin, from_twin, to_chip, from_chip, far, result,
    w_sem, local, d_send, d_recv, r_send, r_recv,
    g_send, g_recv, o_send, o_recv, t_send, t_recv,
    y_send, y_recv, x_send, x_recv, f_send, f_recv, p_send, p_recv,
):
    dp, ex, z, y = place()
    x, core = lax.div(dp, 2), lax.rem(dp, 2)
    twin = x * 2 + 1 - core
    chip = [x, lax.rem(x + CHIPS - 1, CHIPS), lax.rem(x + 1, CHIPS), lax.rem(x + 2, CHIPS)]
    width = slots.shape[-1]
    hidden = first.shape[-1]
    block = EXPERTS * slots.shape[1]

    barrier = pltpu.get_barrier_semaphore()
    for a in range(BEAM):
        for b in range(GROUP):
            if a or b:
                greet(barrier, dp, lax.rem(z + a, BEAM) * GROUP + lax.rem(y + b, GROUP))
    greet(barrier, twin, ex)
    for side in (LEFT, RIGHT, OPPOSITE):
        greet(barrier, chip[side] * 2 + core, ex)
    loads = [
        pltpu.make_async_copy(first, first_v, w_sem.at[0]),
        pltpu.make_async_copy(second, second_v, w_sem.at[1]),
    ]
    for load in loads:
        load.start()
    pl.semaphore_wait(barrier, EXPERTS - 1 + 4)

    def peer(a, b):
        return lax.rem(z + a, BEAM) * GROUP + lax.rem(y + b, GROUP)

    def source(a, b):
        return lax.rem(z + BEAM - a, BEAM) * GROUP + lax.rem(y + GROUP - b, GROUP)

    home = held.at[x, core]
    stay = pltpu.make_async_copy(slots.at[ex], home.at[ex], local.at[0])
    stay.start()
    sent = []
    for a in ORDER:
        for b in range(GROUP):
            if a or b:
                spot = a * GROUP + b
                move = send(slots.at[peer(a, b)], home.at[ex], d_send.at[spot], d_recv.at[spot], dp, peer(a, b))
                move.start()
                sent.append(move)

    def chunk(which, owner, j):
        zz = lax.rem(z + BEAM - ORDER[j], BEAM)
        return held.at[chip[which], owner, pl.ds(zz * GROUP, GROUP)]

    def to_sibling(which, j):
        part = chunk(which, core, j)
        move = send(part, part, t_send.at[which, j], t_recv.at[which, j], twin, ex)
        move.start()
        sent.append(move)

    def from_sibling(which):
        for j in range(4):
            part = chunk(which, 1 - core, j)
            send(part, part, t_send.at[which, j], t_recv.at[which, j], twin, ex).wait_recv()

    stay.wait()
    for j, a in enumerate(ORDER):
        for b in range(GROUP):
            if a or b:
                spot = a * GROUP + b
                there = home.at[source(a, b)]
                send(there, there, d_send.at[spot], d_recv.at[spot], dp, source(a, b)).wait_recv()
        part = chunk(OWN, core, j)
        for way, side in ((0, RIGHT), (1, LEFT)):
            move = send(part, part, g_send.at[way, j], g_recv.at[way, j], chip[side] * 2 + core, ex)
            move.start()
            sent.append(move)
        to_sibling(OWN, j)

    paged = []
    for off in (1, 3, 2):
        move = send(
            pages.at[off - 1], arrived.at[off - 1], p_send.at[off - 1], p_recv.at[off - 1],
            dp, lax.rem(z + off, BEAM) * GROUP + y,
        )
        move.start()
        paged.append(move)

    cells = picked.shape[0] // 2
    tile = min(1024, hidden)
    wide = min(1024, width)
    slim = min(256, width)
    band = block // 4

    def up(which):
        for half, owner in ((0, core), (1, 1 - core)):
            picked[half * cells : (half + 1) * cells, :] = held[chip[which], owner].reshape(cells, width)

        @pl.loop(0, hidden // tile)
        def _(n):
            spot = pl.ds(pl.multiple_of(n * tile, tile), tile)
            part = jnp.dot(picked[...], first_v[:, spot], preferred_element_type=jnp.float32)
            inner[:, spot] = jnp.maximum(part, 0.0).astype(inner.dtype)

    def down(which):
        @pl.loop(0, width // wide)
        def _(n):
            spot = pl.ds(pl.multiple_of(n * wide, wide), wide)
            part = jnp.dot(inner[...], second_v[:, spot], preferred_element_type=jnp.float32)
            total[which, :, spot] = part[:cells]
            to_twin[which, :, spot] = part[cells:].astype(to_twin.dtype)

        move = send(to_twin.at[which], from_twin.at[which], y_send.at[which], y_recv.at[which], twin, ex)
        move.start()
        sent.append(move)

    def forward(which):
        there = from_twin.at[which]
        send(there, there, y_send.at[which], y_recv.at[which], twin, ex).wait_recv()

        @pl.loop(0, width // slim)
        def _(n):
            spot = pl.ds(pl.multiple_of(n * slim, slim), slim)
            both = total[which, :, spot] + from_twin[which, :, spot].astype(jnp.float32)
            to_chip[which - 1, :, spot] = both.astype(to_chip.dtype)

        if which == OPPOSITE:
            for q in (0, 2, 1, 3):
                rows = pl.ds(q * band, band)
                relay(to_chip.at[2, rows], far.at[rows], f_send.at[q], f_recv.at[q], RIGHT if q < 2 else LEFT)
        else:
            for q in (2, 3) if which == RIGHT else (0, 1):
                last_leg(which, q)

    def relay(src, dst, send_sem, recv_sem, side):
        move = send(src, dst, send_sem, recv_sem, chip[side] * 2 + core, ex)
        move.start()
        sent.append(move)

    def last_leg(which, q):
        rows = pl.ds(q * band, band)
        spot = which - 1
        relay(to_chip.at[spot, rows], from_chip.at[spot, rows], x_send.at[spot, q], x_recv.at[spot, q], which)

    def merge(q):
        rows = pl.ds(q * band, band)
        which = RIGHT if q < 2 else LEFT
        there = far.at[rows]
        send(there, there, f_send.at[q], f_recv.at[q], dp, ex).wait_recv()

        @pl.loop(0, width // slim)
        def _(n):
            spot = pl.ds(pl.multiple_of(n * slim, slim), slim)
            both = to_chip[which - 1, rows, spot].astype(jnp.float32) + far[rows, spot].astype(jnp.float32)
            to_chip[which - 1, rows, spot] = both.astype(to_chip.dtype)

        last_leg(which, q)

    def landed(way, j):
        side = LEFT if way == 0 else RIGHT
        part = chunk(side, core, j)
        send(part, part, g_send.at[way, j], g_recv.at[way, j], dp, ex).wait_recv()
        to_sibling(side, j)
        if (j < 2) == (way == 0):
            onward = RIGHT if way == 0 else LEFT
            move = send(part, part, o_send.at[j], o_recv.at[j], chip[onward] * 2 + core, ex)
            move.start()
            sent.append(move)

    for load in loads:
        load.wait()
    from_sibling(OWN)
    up(OWN)
    down(OWN)
    for j in range(4):
        landed(0, j)
        landed(1, j)
    from_sibling(LEFT)
    up(LEFT)
    down(LEFT)
    from_sibling(RIGHT)
    up(RIGHT)
    forward(LEFT)
    down(RIGHT)
    for j in range(4):
        part = chunk(OPPOSITE, core, j)
        send(part, part, o_send.at[j], o_recv.at[j], dp, ex).wait_recv()
        to_sibling(OPPOSITE, j)
    from_sibling(OPPOSITE)
    up(OPPOSITE)
    forward(RIGHT)
    down(OPPOSITE)
    forward(OPPOSITE)
    for q in (0, 2, 1, 3):
        merge(q)

    there = from_twin.at[OWN]
    send(there, there, y_send.at[OWN], y_recv.at[OWN], twin, ex).wait_recv()
    cap = block // EXPERTS
    stay = pltpu.make_async_copy(result.at[ex], returned.at[ex], local.at[1])
    for q in (0, 2, 1, 3):
        rows = pl.ds(q * band, band)
        for spot in (0, 1):
            there = from_chip.at[spot, rows]
            send(there, there, x_send.at[spot, q], x_recv.at[spot, q], dp, ex).wait_recv()

        @pl.loop(0, width // slim)
        def _(n):
            spot = pl.ds(pl.multiple_of(n * slim, slim), slim)
            whole = total[OWN, rows, spot] + from_twin[OWN, rows, spot].astype(jnp.float32)
            for side in (0, 1):
                whole = whole + from_chip[side, rows, spot].astype(jnp.float32)
            packets = whole.astype(result.dtype).reshape(GROUP, cap, slim)
            result[q * GROUP : (q + 1) * GROUP, :, spot] = packets

        for target in range(q * GROUP, (q + 1) * GROUP):
            move = send(result.at[target], returned.at[ex], r_send.at[target], r_recv.at[ex], dp, target)
            pl.when(target != ex)(move.start)
            pl.when(target == ex)(stay.start)
    for origin in range(EXPERTS):
        there = returned.at[origin]
        move = send(there, there, r_send.at[origin], r_recv.at[origin], dp, origin)
        pl.when(origin != ex)(move.wait)
    stay.wait()
    for move in sent:
        move.wait_send()
    for move in paged:
        move.wait()


def experts(slots, first, second, pages):
    count, cap, width = slots.shape
    hidden = first.shape[-1]
    block = count * cap
    kind = slots.dtype
    scratch = [
        pltpu.VMEM((CHIPS, 2, count, cap, width), kind),
        pltpu.VMEM(first.shape, kind),
        pltpu.VMEM(second.shape, kind),
        pltpu.VMEM((2 * block, width), kind),
        pltpu.VMEM((2 * block, hidden), kind),
        pltpu.VMEM((4, block, width), jnp.float32),
        pltpu.VMEM((4, block, width), kind),
        pltpu.VMEM((4, block, width), kind),
        pltpu.VMEM((3, block, width), kind),
        pltpu.VMEM((2, block, width), kind),
        pltpu.VMEM((block, width), kind),
        pltpu.VMEM((count, cap, width), kind),
    ]
    sems = [
        DMA((2,)), DMA((2,)), DMA((16,)), DMA((16,)), DMA((16,)), DMA((16,)),
        DMA((2, 4)), DMA((2, 4)), DMA((4,)), DMA((4,)), DMA((4, 4)), DMA((4, 4)),
        DMA((4,)), DMA((4,)), DMA((2, 4)), DMA((2, 4)), DMA((4,)), DMA((4,)), DMA((3,)), DMA((3,)),
    ]
    return pl.pallas_call(
        expert_kernel,
        out_shape=[
            jax.ShapeDtypeStruct(slots.shape, kind),
            jax.ShapeDtypeStruct(pages.shape, pages.dtype),
        ],
        in_specs=[ANY] * 4,
        out_specs=[ANY] * 2,
        scratch_shapes=scratch + sems,
        compiler_params=pltpu.CompilerParams(
            collective_id=2, has_side_effects=True, vmem_limit_bytes=48 * 2**20
        ),
        name="experts",
    )(slots, first, second, pages)


def per_device(
    tokens,
    self_query,
    new_kv,
    kv_cache,
    parents,
    dec_len,
    cross_query,
    memory,
    src_len,
    norm_gain,
    routes,
    gate_weights,
    expert_in,
    expert_out,
):
    row_count, model_width = tokens.shape
    head_count = model_width // HEAD
    scale = 1.0 / math.sqrt(HEAD)
    expert_pos = lax.axis_index("expert")
    sub_pos = expert_pos % GROUP
    span = kv_cache.shape[1]
    quarter = row_count // BEAM

    queries, cross_q, wishes = ask(
        self_query, cross_query.reshape(GROUP, quarter, model_width), parents.reshape(1, row_count)
    )
    pages = pack(wishes.reshape(BEAM, row_count), kv_cache)

    keys = kv_cache[:, :, :model_width].reshape(row_count, span, head_count, HEAD)
    values = kv_cache[:, :, model_width:].reshape(row_count, span, head_count, HEAD)
    asked = queries.reshape(BEAM, row_count, head_count, HEAD)
    lengths = lax.dynamic_slice_in_dim(dec_len, sub_pos * row_count, row_count)
    valid = (jnp.arange(span, dtype=jnp.int32)[None, :] < lengths[:, None])[None, :, None, :]
    scores = jnp.einsum("brhk,rphk->brhp", asked, keys, preferred_element_type=jnp.float32) * scale
    peak = jnp.max(jnp.where(valid, scores, -1e30), -1)
    terms = jnp.where(valid, jnp.exp(scores - peak[..., None]), 0.0)
    mass = jnp.sum(terms, -1)
    weights = (terms / mass[..., None]).astype(jnp.bfloat16)
    outs = jnp.einsum("brhp,rphk->brhk", weights, values, preferred_element_type=jnp.float32)
    outs = outs.astype(jnp.bfloat16).reshape(BEAM, row_count, model_width)
    stats = jnp.pad(peak + jnp.log(mass), ((0, 0), (0, 0), (0, HEAD - head_count)))

    local_len = memory.shape[1]
    cross_q = cross_q.reshape(BEAM, quarter, head_count, HEAD)
    mem_keys = memory[:, :, :model_width].reshape(quarter, local_len, head_count, HEAD)
    mem_values = memory[:, :, model_width:].reshape(quarter, local_len, head_count, HEAD)
    cross_scores = (
        jnp.einsum("bshk,sphk->bshp", cross_q, mem_keys, preferred_element_type=jnp.float32) * scale
    )
    reach = (jnp.arange(local_len, dtype=jnp.int32)[None, :] < src_len[:, None])[None, :, None, :]
    cross_peak = jnp.max(jnp.where(reach, cross_scores, -1e30), -1)
    cross_terms = jnp.where(reach, jnp.exp(cross_scores - cross_peak[..., None]), 0.0)
    cross_weights = cross_terms / jnp.sum(cross_terms, -1)[..., None]
    owner_out = jnp.einsum(
        "bshp,sphk->bshk",
        cross_weights.astype(jnp.bfloat16),
        mem_values,
        preferred_element_type=jnp.float32,
    )
    owner_out = owner_out.astype(jnp.bfloat16).reshape(BEAM, quarter, model_width)

    got, got_stats, cross_out = answer(outs, stats, owner_out)

    own_key = new_kv[:, :model_width].reshape(row_count, head_count, HEAD)
    own_value = new_kv[:, model_width:].reshape(row_count, head_count, HEAD)
    own = (
        jnp.einsum(
            "rhk,rhk->rh",
            self_query.reshape(row_count, head_count, HEAD),
            own_key,
            preferred_element_type=jnp.float32,
        )
        * scale
    )
    chosen = parents[None, :] == jnp.arange(BEAM, dtype=jnp.int32)[:, None]
    cached = jnp.sum(jnp.where(chosen[..., None], got.astype(jnp.float32), 0.0), 0)
    level = jnp.sum(jnp.where(chosen[..., None], got_stats[..., :head_count], 0.0), 0)
    top = jnp.maximum(level, own)
    part = jnp.exp(level - top)
    own_part = jnp.exp(own - top)
    cache_share = part / (part + own_part)
    own_share = own_part / (part + own_part)
    self_out = (
        cache_share[..., None] * cached.reshape(row_count, head_count, HEAD)
        + own_share[..., None] * own_value.astype(jnp.float32)
    ).reshape(row_count, model_width)
    cross_out = cross_out.reshape(row_count, model_width).astype(jnp.float32)

    hidden = tokens.astype(jnp.float32) + self_out + cross_out
    row_mean = jnp.mean(hidden, -1, keepdims=True)
    centered = hidden - row_mean
    variance = jnp.mean(centered * centered, -1, keepdims=True)
    moe_in = (centered * lax.rsqrt(variance + 1e-05) * norm_gain).astype(jnp.bfloat16)

    slot_cap = 4 * row_count // EXPERTS
    named = routes[:, :, None] == jnp.arange(EXPERTS, dtype=jnp.int32)[None, None, :]
    per_row = jnp.sum(named.astype(jnp.int32), 1)
    before = jnp.cumsum(per_row, 0) - per_row
    slot = jnp.sum(jnp.where(named, before[:, None, :], 0), -1) + routes * slot_cap
    places = jnp.arange(EXPERTS * slot_cap, dtype=jnp.int32)
    taken = (slot[:, :, None] == places[None, None, :]).astype(jnp.bfloat16)
    table = (taken[:, 0] + taken[:, 1]).T
    slots = jnp.dot(table, moe_in, preferred_element_type=jnp.float32).astype(jnp.bfloat16)

    returned, arrived = experts(
        slots.reshape(EXPERTS, slot_cap, model_width), expert_in[0], expert_out[0], pages
    )
    per_slot = jnp.einsum(
        "rks,sd->rkd",
        taken,
        returned.reshape(EXPERTS * slot_cap, model_width),
        preferred_element_type=jnp.float32,
    )
    mixed = hidden + jnp.sum(gate_weights[..., None] * per_slot, 1)
    return (mixed.astype(jnp.bfloat16), unpack(parents, kv_cache, arrived))


def solution(mesh):
    placed = (
        P(("dp", "expert"), None),
        P(("dp", "expert"), None),
        P(("dp", "expert"), None),
        P(("dp", "expert"), None, None),
        P(("dp", "expert")),
        P("dp"),
        P(("dp", "expert"), None),
        P(("dp", "expert"), None, None),
        P(("dp", "expert")),
        P(),
        P(("dp", "expert"), None),
        P(("dp", "expert"), None),
        P("expert", None, "dp"),
        P("expert", "dp", None),
    )
    return jax.shard_map(
        per_device,
        mesh=mesh,
        in_specs=placed,
        out_specs=(P(("dp", "expert"), None), P(("dp", "expert"), None, None)),
        check_vma=False,
    )
```

```python
import functools
import math

import jax
import jax.numpy as jnp
from jax import lax
from jax.experimental import pallas as pl
from jax.experimental.pallas import tpu as pltpu
from jax.sharding import PartitionSpec as P

HEAD = 128
BEAM = 4
GROUP = 4
CHIPS = 4
EXPERTS = 16
PAGE_CAP = 16
MESH = pl.DeviceIdType.MESH
ANY = pl.BlockSpec(memory_space=pl.ANY)
DMA = pltpu.SemaphoreType.DMA


def place():
    dp = lax.axis_index("dp")
    ex = lax.axis_index("expert")
    return dp, ex, lax.div(ex, GROUP), lax.rem(ex, GROUP)


def send(src, dst, send_sem, recv_sem, dp, ex):
    return pltpu.make_async_remote_copy(
        src_ref=src,
        dst_ref=dst,
        send_sem=send_sem,
        recv_sem=recv_sem,
        device_id=(dp, ex),
        device_id_type=MESH,
    )


def greet(barrier, dp, ex):
    pl.semaphore_signal(barrier, inc=1, device_id=(dp, ex), device_id_type=MESH)


def unpack_kernel(parents, cache, arrived, fresh, sem):
    _, _, z, _ = place()
    rows = cache.shape[0]

    def begin(row, counts):
        parent = parents[row]
        off = lax.rem(z - parent + BEAM, BEAM)

        def keep():
            pltpu.make_async_copy(cache.at[row], fresh.at[row], sem).start()

        pl.when(off == 0)(keep)
        after = []
        for step in range(1, BEAM):
            hit = off == step

            def take(step=step):
                pltpu.make_async_copy(arrived.at[step - 1, counts[step - 1]], fresh.at[row], sem).start()

            pl.when(hit)(take)
            after.append(counts[step - 1] + hit.astype(jnp.int32))
        return tuple(after)

    lax.fori_loop(0, rows, begin, (jnp.int32(0),) * (BEAM - 1))
    pltpu.make_async_copy(cache, fresh, sem).wait()


def unpack(parents, cache, arrived):
    return pl.pallas_call(
        unpack_kernel,
        out_shape=jax.ShapeDtypeStruct(cache.shape, cache.dtype),
        in_specs=[pl.BlockSpec(memory_space=pltpu.SMEM), ANY, ANY],
        out_specs=pl.BlockSpec(memory_space=pltpu.VMEM),
        scratch_shapes=[DMA],
        compiler_params=pltpu.CompilerParams(vmem_limit_bytes=58 * 2**20),
        name="unpack",
    )(parents, cache, arrived)


ORDER = (0, 1, 3, 2)
OWN, LEFT, RIGHT, OPPOSITE = range(4)


def layer_kernel(
    query, cross, lanes, info, tokens, new_kv, gain, cache, memory, first, second,
    mixed, arrived,
    cache_v, memory_v, tokens_v, new_kv_v, gain_v, info_v, queries, wishes, crosses,
    outs, stats, owner_out, got, got_stats, cross_out, hidden_v, pages, slots, returned,
    held, first_v, second_v, picked, inner, total, to_twin, from_twin, to_chip, from_chip, far, result,
    l_sem, local, k_send, k_recv, n_send, n_recv, e_send, e_recv, b_send, b_recv, s_send, s_recv, c_send, c_recv,
    d_send, d_recv, r_send, r_recv,
    g_send, g_recv, o_send, o_recv, t_send, t_recv,
    y_send, y_recv, x_send, x_recv, f_send, f_recv, p_send, p_recv,
):
    dp, ex, z, y = place()
    x, core = lax.div(dp, 2), lax.rem(dp, 2)
    twin = x * 2 + 1 - core
    chip = [x, lax.rem(x + CHIPS - 1, CHIPS), lax.rem(x + 1, CHIPS), lax.rem(x + 2, CHIPS)]
    row_count, width = tokens.shape
    hidden = first.shape[-1]
    kind = tokens.dtype
    heads = width // HEAD
    span = cache.shape[1]
    quarter, reach = memory.shape[:2]
    block = EXPERTS * slots.shape[1]
    scale = 1.0 / math.sqrt(HEAD)

    barrier = pltpu.get_barrier_semaphore()
    for a in range(BEAM):
        for b in range(GROUP):
            if a or b:
                greet(barrier, dp, lax.rem(z + a, BEAM) * GROUP + lax.rem(y + b, GROUP))
    greet(barrier, twin, ex)
    for side in (LEFT, RIGHT, OPPOSITE):
        greet(barrier, chip[side] * 2 + core, ex)
    pairs = (
        (first, first_v), (second, second_v), (cache, cache_v), (memory, memory_v), (tokens, tokens_v),
        (new_kv, new_kv_v), (gain, gain_v), (info, info_v), (query, queries.at[z]), (lanes, wishes.at[z]),
    )
    loads = [pltpu.make_async_copy(a, b, l_sem.at[i]) for i, (a, b) in enumerate(pairs)]
    for i in (9, 8, 2, 5, 3, 4, 6, 7, 0, 1):
        loads[i].start()
    own_cross = pltpu.make_async_copy(cross.at[y], crosses.at[z], local.at[2])
    pl.when(z == y)(own_cross.start)
    pl.semaphore_wait(barrier, EXPERTS - 1 + 4)

    sent = []
    asks = []
    for off in (1, 3, 2):
        target = lax.rem(z + off, BEAM) * GROUP + y
        asks.append(send(lanes, wishes.at[z], n_send.at[off - 1], n_recv.at[off - 1], dp, target))
        asks.append(send(query, queries.at[z], k_send.at[off - 1], k_recv.at[off - 1], dp, target))
    for move in asks:
        move.start()
    crossing = [
        send(cross.at[p], crosses.at[z], e_send.at[p], e_recv.at[z], dp, y * GROUP + p) for p in range(GROUP)
    ]
    for p in range(GROUP):
        pl.when(y * GROUP + p != ex)(crossing[p].start)

    for i in (5, 8, 9):
        loads[i].wait()
    lane = lax.broadcasted_iota(jnp.int32, (row_count, HEAD), 1)
    own = jnp.zeros((row_count, HEAD), jnp.float32)
    for h in range(heads):
        spot = slice(h * HEAD, (h + 1) * HEAD)
        both = queries[z, :, spot].astype(jnp.float32) * new_kv_v[:, spot].astype(jnp.float32)
        own = own + jnp.where(lane == h, jnp.sum(both, -1, keepdims=True) * scale, 0.0)

    asked = BEAM * row_count
    shape = (asked, row_count * span)
    lane_row = lax.broadcasted_iota(jnp.int32, shape, 1)
    same = lax.rem(lax.broadcasted_iota(jnp.int32, shape, 0), row_count) == lax.div(lane_row, span)
    loads[2].wait()
    for move in asks:
        move.wait()
    valid = same & (lax.rem(lane_row, span) < wishes[z, 0:1, : shape[1]])
    stat_lane = lax.broadcasted_iota(jnp.int32, (asked, HEAD), 1)
    stats[...] = jnp.zeros_like(stats)

    @pl.loop(0, heads // batch_of(heads))
    def _(n):
        for m in range(batch_of(heads)):
            h = n * batch_of(heads) + m
            spot = pl.ds(pl.multiple_of(h * HEAD, HEAD), HEAD)
            spot_v = pl.ds(pl.multiple_of(width + h * HEAD, HEAD), HEAD)
            q_h = queries[:, :, spot].reshape(asked, HEAD)
            k_h = cache_v[:, :, spot].reshape(row_count * span, HEAD)
            v_h = cache_v[:, :, spot_v].reshape(row_count * span, HEAD)
            scores = lax.dot_general(q_h, k_h, (((1,), (1,)), ((), ())), preferred_element_type=jnp.float32)
            scores = jnp.where(valid, scores * scale, -1e30)
            peak = jnp.max(scores, -1, keepdims=True)
            terms = jnp.exp(scores - peak)
            mass = jnp.sum(terms, -1, keepdims=True)
            part = jnp.dot((terms / mass).astype(kind), v_h, preferred_element_type=jnp.float32)
            outs[:, :, spot] = part.astype(kind).reshape(BEAM, row_count, HEAD)
            level = jnp.where(stat_lane == h, peak + jnp.log(mass), 0.0)
            stats[...] += level.reshape(BEAM, row_count, HEAD)

    answers = []
    for off in (1, 3, 2):
        other = lax.rem(z + off, BEAM)
        target = other * GROUP + y
        answers.append(send(stats.at[other], got_stats.at[z], b_send.at[off - 1], b_recv.at[off - 1], dp, target))
        answers.append(send(outs.at[other], got.at[z], s_send.at[off - 1], s_recv.at[off - 1], dp, target))
    for move in answers:
        move.start()
    stays = [
        pltpu.make_async_copy(outs.at[z], got.at[z], local.at[0]),
        pltpu.make_async_copy(stats.at[z], got_stats.at[z], local.at[1]),
    ]
    for stay in stays:
        stay.start()

    for p in range(GROUP):
        pl.when(y * GROUP + p != ex)(crossing[p].wait_send)
    for beam in range(BEAM):
        coming = send(cross.at[0], crosses.at[beam], e_send.at[0], e_recv.at[beam], dp, beam * GROUP + z)
        pl.when(beam * GROUP + z != ex)(coming.wait_recv)
    pl.when(z == y)(own_cross.wait)
    loads[3].wait()
    asked_c = BEAM * quarter
    shape_c = (asked_c, quarter * reach)
    lane_c = lax.broadcasted_iota(jnp.int32, shape_c, 1)
    same_c = lax.rem(lax.broadcasted_iota(jnp.int32, shape_c, 0), quarter) == lax.div(lane_c, reach)
    valid_c = same_c & (lax.rem(lane_c, reach) < wishes[z, 1:2, : shape_c[1]])

    @pl.loop(0, heads // batch_of(heads))
    def _(n):
        for m in range(batch_of(heads)):
            h = n * batch_of(heads) + m
            spot = pl.ds(pl.multiple_of(h * HEAD, HEAD), HEAD)
            spot_v = pl.ds(pl.multiple_of(width + h * HEAD, HEAD), HEAD)
            q_h = crosses[:, :, spot].reshape(asked_c, HEAD)
            k_h = memory_v[:, :, spot].reshape(quarter * reach, HEAD)
            v_h = memory_v[:, :, spot_v].reshape(quarter * reach, HEAD)
            scores = lax.dot_general(q_h, k_h, (((1,), (1,)), ((), ())), preferred_element_type=jnp.float32)
            scores = jnp.where(valid_c, scores * scale, -1e30)
            peak = jnp.max(scores, -1, keepdims=True)
            terms = jnp.exp(scores - peak)
            mass = jnp.sum(terms, -1, keepdims=True)
            part = jnp.dot((terms / mass).astype(kind), v_h, preferred_element_type=jnp.float32)
            owner_out[:, :, spot] = part.astype(kind).reshape(BEAM, quarter, HEAD)

    own_back = pltpu.make_async_copy(owner_out.at[z], cross_out.at[y], local.at[2])
    crossing = [
        send(owner_out.at[beam], cross_out.at[y], c_send.at[beam], c_recv.at[y], dp, beam * GROUP + z)
        for beam in range(BEAM)
    ]
    for beam in range(BEAM):
        pl.when(beam * GROUP + z != ex)(crossing[beam].start)
    pl.when(z == y)(own_back.start)

    page_shape = (PAGE_CAP * span, row_count * span)
    page_row = lax.broadcasted_iota(jnp.int32, page_shape, 0)
    page_lane = lax.broadcasted_iota(jnp.int32, page_shape, 1)
    page_slot = lax.div(page_row, span)
    same_place = lax.rem(page_row, span) == lax.rem(page_lane, span)
    strip = min(1024, 2 * width)
    for off in (1, 3, 2):
        asker = lax.rem(z + off, BEAM)
        wanted = wishes[asker, 4:5, : page_shape[1]] == z
        pick = same_place & wanted & (page_slot == wishes[asker, 5:6, : page_shape[1]])
        pick = pick.astype(jnp.float32).astype(kind)

        @pl.loop(0, 2 * width // strip)
        def _(n):
            spot = pl.ds(pl.multiple_of(n * strip, strip), strip)
            lines = cache_v[:, :, spot].reshape(row_count * span, strip)
            part = jnp.dot(pick, lines, preferred_element_type=jnp.float32).astype(kind)
            pages[off - 1, :, :, spot] = part.reshape(PAGE_CAP, span, strip)

    for load in loads[4:5] + loads[6:8]:
        load.wait()
    for stay in stays:
        stay.wait()
    for move in answers:
        move.wait()
    for beam in range(BEAM):
        pl.when(beam * GROUP + z != ex)(crossing[beam].wait_send)
    for p in range(GROUP):
        coming = send(owner_out.at[0], cross_out.at[p], c_send.at[0], c_recv.at[p], dp, y * GROUP + p)
        pl.when(y * GROUP + p != ex)(coming.wait_recv)
    pl.when(z == y)(own_back.wait)

    parent = info_v[:, 0:1]
    level = jnp.zeros((row_count, HEAD), jnp.float32)
    for beam in range(BEAM):
        level = level + jnp.where(parent == float(beam), got_stats[beam], 0.0)
    top = jnp.maximum(level, own)
    cache_part = jnp.exp(level - top)
    own_part = jnp.exp(own - top)
    cache_share = cache_part / (cache_part + own_part)
    own_share = own_part / (cache_part + own_part)
    for h in range(heads):
        spot = slice(h * HEAD, (h + 1) * HEAD)
        cached = jnp.zeros((row_count, HEAD), jnp.float32)
        for beam in range(BEAM):
            cached = cached + jnp.where(parent == float(beam), got[beam, :, spot].astype(jnp.float32), 0.0)
        own_value = new_kv_v[:, width + h * HEAD : width + (h + 1) * HEAD].astype(jnp.float32)
        mine = cache_share[:, h : h + 1] * cached + own_share[:, h : h + 1] * own_value
        crossed = cross_out[:, :, spot].reshape(row_count, HEAD).astype(jnp.float32)
        hidden_v[:, spot] = tokens_v[:, spot].astype(jnp.float32) + mine + crossed
    whole = hidden_v[...]
    centered = whole - jnp.mean(whole, -1, keepdims=True)
    variance = jnp.mean(centered * centered, -1, keepdims=True)
    moe_in = (centered * lax.rsqrt(variance + 1e-05) * gain_v[...]).astype(kind)
    slot_row = lax.broadcasted_iota(jnp.int32, (block, row_count), 0)
    table = (slot_row == wishes[z, 2:3, :row_count]) | (slot_row == wishes[z, 3:4, :row_count])
    table = table.astype(jnp.float32).astype(kind)
    packets = jnp.dot(table, moe_in, preferred_element_type=jnp.float32).astype(kind)
    slots[...] = packets.reshape(slots.shape)

    def peer(a, b):
        return lax.rem(z + a, BEAM) * GROUP + lax.rem(y + b, GROUP)

    def source(a, b):
        return lax.rem(z + BEAM - a, BEAM) * GROUP + lax.rem(y + GROUP - b, GROUP)

    home = held.at[x, core]
    stay = pltpu.make_async_copy(slots.at[ex], home.at[ex], local.at[0])
    stay.start()
    for a in ORDER:
        for b in range(GROUP):
            if a or b:
                spot = a * GROUP + b
                move = send(slots.at[peer(a, b)], home.at[ex], d_send.at[spot], d_recv.at[spot], dp, peer(a, b))
                move.start()
                sent.append(move)

    def chunk(which, owner, j):
        zz = lax.rem(z + BEAM - ORDER[j], BEAM)
        return held.at[chip[which], owner, pl.ds(zz * GROUP, GROUP)]

    def to_sibling(which, j):
        part = chunk(which, core, j)
        move = send(part, part, t_send.at[which, j], t_recv.at[which, j], twin, ex)
        move.start()
        sent.append(move)

    def from_sibling(which):
        for j in range(4):
            part = chunk(which, 1 - core, j)
            send(part, part, t_send.at[which, j], t_recv.at[which, j], twin, ex).wait_recv()

    stay.wait()
    for j, a in enumerate(ORDER):
        for b in range(GROUP):
            if a or b:
                spot = a * GROUP + b
                there = home.at[source(a, b)]
                send(there, there, d_send.at[spot], d_recv.at[spot], dp, source(a, b)).wait_recv()
        part = chunk(OWN, core, j)
        for way, side in ((0, RIGHT), (1, LEFT)):
            move = send(part, part, g_send.at[way, j], g_recv.at[way, j], chip[side] * 2 + core, ex)
            move.start()
            sent.append(move)
        to_sibling(OWN, j)

    cells = picked.shape[0] // 2
    tile = min(1024, hidden)
    wide = min(1024, width)
    slim = min(256, width)
    band = block // 4

    def up(which):
        for half, owner in ((0, core), (1, 1 - core)):
            picked[half * cells : (half + 1) * cells, :] = held[chip[which], owner].reshape(cells, width)

        @pl.loop(0, hidden // tile)
        def _(n):
            spot = pl.ds(pl.multiple_of(n * tile, tile), tile)
            part = jnp.dot(picked[...], first_v[:, spot], preferred_element_type=jnp.float32)
            inner[:, spot] = jnp.maximum(part, 0.0).astype(inner.dtype)

    def down(which):
        @pl.loop(0, width // wide)
        def _(n):
            spot = pl.ds(pl.multiple_of(n * wide, wide), wide)
            part = jnp.dot(inner[...], second_v[:, spot], preferred_element_type=jnp.float32)
            total[which, :, spot] = part[:cells]
            to_twin[which, :, spot] = part[cells:].astype(to_twin.dtype)

        move = send(to_twin.at[which], from_twin.at[which], y_send.at[which], y_recv.at[which], twin, ex)
        move.start()
        sent.append(move)

    def forward(which):
        there = from_twin.at[which]
        send(there, there, y_send.at[which], y_recv.at[which], twin, ex).wait_recv()

        @pl.loop(0, width // slim)
        def _(n):
            spot = pl.ds(pl.multiple_of(n * slim, slim), slim)
            both = total[which, :, spot] + from_twin[which, :, spot].astype(jnp.float32)
            to_chip[which - 1, :, spot] = both.astype(to_chip.dtype)

        if which == OPPOSITE:
            for q in (0, 2, 1, 3):
                rows = pl.ds(q * band, band)
                relay(to_chip.at[2, rows], far.at[rows], f_send.at[q], f_recv.at[q], RIGHT if q < 2 else LEFT)
        else:
            for q in (2, 3) if which == RIGHT else (0, 1):
                last_leg(which, q)

    def relay(src, dst, send_sem, recv_sem, side):
        move = send(src, dst, send_sem, recv_sem, chip[side] * 2 + core, ex)
        move.start()
        sent.append(move)

    def last_leg(which, q):
        rows = pl.ds(q * band, band)
        spot = which - 1
        relay(to_chip.at[spot, rows], from_chip.at[spot, rows], x_send.at[spot, q], x_recv.at[spot, q], which)

    def merge(q):
        rows = pl.ds(q * band, band)
        which = RIGHT if q < 2 else LEFT
        there = far.at[rows]
        send(there, there, f_send.at[q], f_recv.at[q], dp, ex).wait_recv()

        @pl.loop(0, width // slim)
        def _(n):
            spot = pl.ds(pl.multiple_of(n * slim, slim), slim)
            both = to_chip[which - 1, rows, spot].astype(jnp.float32) + far[rows, spot].astype(jnp.float32)
            to_chip[which - 1, rows, spot] = both.astype(to_chip.dtype)

        last_leg(which, q)

    def landed(way, j):
        side = LEFT if way == 0 else RIGHT
        part = chunk(side, core, j)
        send(part, part, g_send.at[way, j], g_recv.at[way, j], dp, ex).wait_recv()
        to_sibling(side, j)
        if (j < 2) == (way == 0):
            onward = RIGHT if way == 0 else LEFT
            move = send(part, part, o_send.at[j], o_recv.at[j], chip[onward] * 2 + core, ex)
            move.start()
            sent.append(move)

    paged = []
    for off in (1, 3, 2):
        move = send(
            pages.at[off - 1], arrived.at[off - 1], p_send.at[off - 1], p_recv.at[off - 1],
            dp, lax.rem(z + off, BEAM) * GROUP + y,
        )
        move.start()
        paged.append(move)
    for load in loads[:2]:
        load.wait()
    from_sibling(OWN)
    up(OWN)
    down(OWN)
    for j in range(4):
        landed(0, j)
        landed(1, j)
    from_sibling(LEFT)
    up(LEFT)
    down(LEFT)
    from_sibling(RIGHT)
    up(RIGHT)
    forward(LEFT)
    down(RIGHT)
    for j in range(4):
        part = chunk(OPPOSITE, core, j)
        send(part, part, o_send.at[j], o_recv.at[j], dp, ex).wait_recv()
        to_sibling(OPPOSITE, j)
    from_sibling(OPPOSITE)
    up(OPPOSITE)
    forward(RIGHT)
    down(OPPOSITE)
    forward(OPPOSITE)
    for q in (0, 2, 1, 3):
        merge(q)

    there = from_twin.at[OWN]
    send(there, there, y_send.at[OWN], y_recv.at[OWN], twin, ex).wait_recv()
    cap = block // EXPERTS
    stay = pltpu.make_async_copy(result.at[ex], returned.at[ex], local.at[1])
    for q in (0, 2, 1, 3):
        rows = pl.ds(q * band, band)
        for spot in (0, 1):
            there = from_chip.at[spot, rows]
            send(there, there, x_send.at[spot, q], x_recv.at[spot, q], dp, ex).wait_recv()

        @pl.loop(0, width // slim)
        def _(n):
            spot = pl.ds(pl.multiple_of(n * slim, slim), slim)
            whole = total[OWN, rows, spot] + from_twin[OWN, rows, spot].astype(jnp.float32)
            for side in (0, 1):
                whole = whole + from_chip[side, rows, spot].astype(jnp.float32)
            packets = whole.astype(result.dtype).reshape(GROUP, cap, slim)
            result[q * GROUP : (q + 1) * GROUP, :, spot] = packets

        for target in range(q * GROUP, (q + 1) * GROUP):
            move = send(result.at[target], returned.at[ex], r_send.at[target], r_recv.at[ex], dp, target)
            pl.when(target != ex)(move.start)
            pl.when(target == ex)(stay.start)
    for origin in range(EXPERTS):
        there = returned.at[origin]
        move = send(there, there, r_send.at[origin], r_recv.at[origin], dp, origin)
        pl.when(origin != ex)(move.wait)
    stay.wait()
    back = returned[...].reshape(block, width)
    places = lax.broadcasted_iota(jnp.int32, (row_count, block), 1).astype(jnp.float32)
    final = hidden_v[...]
    for k in range(2):
        taken = (places == info_v[:, 1 + k : 2 + k]).astype(kind)
        final = final + info_v[:, 3 + k : 4 + k] * jnp.dot(taken, back, preferred_element_type=jnp.float32)
    mixed[...] = final.astype(mixed.dtype)
    for move in sent:
        move.wait_send()
    for move in paged:
        move.wait()


def batch_of(heads):
    return math.gcd(heads, 4)


def layer(query, cross, lanes, info, tokens, new_kv, gain, cache, memory, first, second):
    row_count, width = tokens.shape
    hidden = first.shape[-1]
    kind = tokens.dtype
    cap = 4 * row_count // EXPERTS
    block = EXPERTS * cap
    quarter = row_count // BEAM

    def room(*shape, dtype=kind):
        return pltpu.VMEM(shape, dtype)

    paged = (BEAM - 1, PAGE_CAP) + cache.shape[1:]
    scratch = [
        room(*cache.shape), room(*memory.shape), room(row_count, width), room(row_count, 2 * width),
        room(1, width, dtype=jnp.float32), room(row_count, HEAD, dtype=jnp.float32),
        room(BEAM, row_count, width), room(BEAM, *lanes.shape, dtype=jnp.int32), room(BEAM, quarter, width),
        room(BEAM, row_count, width), room(BEAM, row_count, HEAD, dtype=jnp.float32), room(BEAM, quarter, width),
        room(BEAM, row_count, width), room(BEAM, row_count, HEAD, dtype=jnp.float32), room(BEAM, quarter, width),
        room(row_count, width, dtype=jnp.float32), room(*paged), room(EXPERTS, cap, width), room(EXPERTS, cap, width),
        room(CHIPS, 2, EXPERTS, cap, width), room(*first.shape), room(*second.shape),
        room(2 * block, width), room(2 * block, hidden), room(4, block, width, dtype=jnp.float32),
        room(4, block, width), room(4, block, width), room(3, block, width), room(2, block, width),
        room(block, width), room(EXPERTS, cap, width),
    ]
    sems = [
        DMA((10,)), DMA((3,)), DMA((3,)), DMA((3,)), DMA((3,)), DMA((3,)), DMA((4,)), DMA((4,)),
        DMA((3,)), DMA((3,)), DMA((3,)), DMA((3,)), DMA((4,)), DMA((4,)),
        DMA((16,)), DMA((16,)), DMA((16,)), DMA((16,)),
        DMA((2, 4)), DMA((2, 4)), DMA((4,)), DMA((4,)), DMA((4, 4)), DMA((4, 4)),
        DMA((4,)), DMA((4,)), DMA((2, 4)), DMA((2, 4)), DMA((4,)), DMA((4,)), DMA((3,)), DMA((3,)),
    ]
    return pl.pallas_call(
        layer_kernel,
        out_shape=[jax.ShapeDtypeStruct((row_count, width), kind), jax.ShapeDtypeStruct(paged, kind)],
        in_specs=[ANY] * 11,
        out_specs=[pl.BlockSpec(memory_space=pltpu.VMEM), ANY],
        scratch_shapes=scratch + sems,
        compiler_params=pltpu.CompilerParams(
            collective_id=0, has_side_effects=True, vmem_limit_bytes=58 * 2**20
        ),
        name="layer",
    )(query, cross, lanes, info, tokens, new_kv, gain, cache, memory, first, second)


def per_device(
    tokens,
    self_query,
    new_kv,
    kv_cache,
    parents,
    dec_len,
    cross_query,
    memory,
    src_len,
    norm_gain,
    routes,
    gate_weights,
    expert_in,
    expert_out,
):
    row_count, model_width = tokens.shape
    span = kv_cache.shape[1]
    quarter, reach = memory.shape[:2]
    slot_cap = 4 * row_count // EXPERTS
    sub_pos = lax.axis_index("expert") % GROUP
    lengths = lax.dynamic_slice_in_dim(dec_len, sub_pos * row_count, row_count)
    order = jnp.arange(row_count, dtype=jnp.int32)
    earlier = order[:, None] > order[None, :]
    rank = jnp.sum((earlier & (parents[:, None] == parents[None, :])).astype(jnp.int32), 1)
    alike = routes[:, :, None, None] == routes[None, None, :, :]
    slot = jnp.sum((alike & earlier[:, None, :, None]).astype(jnp.int32), (2, 3)) + routes * slot_cap
    long = max(quarter * reach, row_count * span)

    def line(values):
        return jnp.pad(values, (0, long - values.shape[0]))

    lanes = jnp.stack(
        [
            line(jnp.repeat(lengths, span)),
            line(jnp.repeat(src_len, reach)),
            line(slot[:, 0]),
            line(slot[:, 1]),
            line(jnp.repeat(parents, span)),
            line(jnp.repeat(rank, span)),
            jnp.zeros((long,), jnp.int32),
            jnp.zeros((long,), jnp.int32),
        ]
    )
    info = jnp.concatenate([parents[:, None].astype(jnp.float32), slot.astype(jnp.float32), gate_weights], 1)
    info = jnp.pad(info, ((0, 0), (0, HEAD - info.shape[1])))
    mixed, arrived = layer(
        self_query,
        cross_query.reshape(GROUP, quarter, model_width),
        lanes,
        info,
        tokens,
        new_kv,
        norm_gain[None],
        kv_cache,
        memory,
        expert_in[0],
        expert_out[0],
    )
    return (mixed, unpack(parents, kv_cache, arrived))


def solution(mesh):
    placed = (
        P(("dp", "expert"), None),
        P(("dp", "expert"), None),
        P(("dp", "expert"), None),
        P(("dp", "expert"), None, None),
        P(("dp", "expert")),
        P("dp"),
        P(("dp", "expert"), None),
        P(("dp", "expert"), None, None),
        P(("dp", "expert")),
        P(),
        P(("dp", "expert"), None),
        P(("dp", "expert"), None),
        P("expert", None, "dp"),
        P("expert", "dp", None),
    )
    return jax.shard_map(
        per_device,
        mesh=mesh,
        in_specs=placed,
        out_specs=(P(("dp", "expert"), None), P(("dp", "expert"), None, None)),
        check_vma=False,
    )
```

```python
import functools
import math

import jax
import jax.numpy as jnp
from jax import lax
from jax.experimental import pallas as pl
from jax.experimental.pallas import tpu as pltpu
from jax.sharding import PartitionSpec as P

HEAD = 128
BEAM = 4
GROUP = 4
CHIPS = 4
EXPERTS = 16
PAGE_CAP = 16
MESH = pl.DeviceIdType.MESH
ANY = pl.BlockSpec(memory_space=pl.ANY)
DMA = pltpu.SemaphoreType.DMA


def place():
    dp = lax.axis_index("dp")
    ex = lax.axis_index("expert")
    return dp, ex, lax.div(ex, GROUP), lax.rem(ex, GROUP)


def send(src, dst, send_sem, recv_sem, dp, ex):
    return pltpu.make_async_remote_copy(
        src_ref=src,
        dst_ref=dst,
        send_sem=send_sem,
        recv_sem=recv_sem,
        device_id=(dp, ex),
        device_id_type=MESH,
    )


def greet(barrier, dp, ex):
    pl.semaphore_signal(barrier, inc=1, device_id=(dp, ex), device_id_type=MESH)


def unpack_kernel(parents, cache, arrived, fresh, sem):
    _, _, z, _ = place()
    rows = cache.shape[0]

    def begin(row, counts):
        parent = parents[row]
        off = lax.rem(z - parent + BEAM, BEAM)

        def keep():
            pltpu.make_async_copy(cache.at[row], fresh.at[row], sem).start()

        pl.when(off == 0)(keep)
        after = []
        for step in range(1, BEAM):
            hit = off == step

            def take(step=step):
                pltpu.make_async_copy(arrived.at[step - 1, counts[step - 1]], fresh.at[row], sem).start()

            pl.when(hit)(take)
            after.append(counts[step - 1] + hit.astype(jnp.int32))
        return tuple(after)

    lax.fori_loop(0, rows, begin, (jnp.int32(0),) * (BEAM - 1))
    pltpu.make_async_copy(cache, fresh, sem).wait()


def unpack(parents, cache, arrived):
    return pl.pallas_call(
        unpack_kernel,
        out_shape=jax.ShapeDtypeStruct(cache.shape, cache.dtype),
        in_specs=[pl.BlockSpec(memory_space=pltpu.SMEM), ANY, ANY],
        out_specs=pl.BlockSpec(memory_space=pltpu.VMEM),
        scratch_shapes=[DMA],
        compiler_params=pltpu.CompilerParams(vmem_limit_bytes=58 * 2**20),
        name="unpack",
    )(parents, cache, arrived)


ORDER = (0, 1, 3, 2)
OWN, LEFT, RIGHT, OPPOSITE = range(4)
EARLY = 4


def eye(n):
    shape = (n, n)
    return lax.broadcasted_iota(jnp.int32, shape, 0) == lax.broadcasted_iota(jnp.int32, shape, 1)


def upright(row):
    return jnp.sum(jnp.where(eye(row.shape[1]), row, 0.0), 1, keepdims=True)


def flat(column):
    return jnp.sum(jnp.where(eye(column.shape[0]), column, 0.0), 0, keepdims=True)


def spread(column, times):
    shape = (column.shape[0], column.shape[0] * times)
    owner = lax.div(lax.broadcasted_iota(jnp.int32, shape, 1), times)
    return jnp.sum(jnp.where(owner == lax.broadcasted_iota(jnp.int32, shape, 0), column, 0.0), 0, keepdims=True)


def rank(column, rows):
    shape = (column.shape[0], rows[0].shape[1])
    earlier = lax.broadcasted_iota(jnp.int32, shape, 1) < lax.broadcasted_iota(jnp.int32, shape, 0)
    alike = functools.reduce(jnp.logical_or, [column == row for row in rows])
    return jnp.sum(jnp.where(earlier & alike, 1.0, 0.0), 1, keepdims=True)


def number(shape, axis):
    return lax.broadcasted_iota(jnp.int32, shape, axis)


def real(values):
    return values.astype(jnp.float32)


def layer_kernel(
    query, cross, parents, dec_len, src_len, routes, gates, tokens, new_kv, gain, cache, memory, first, second,
    mixed, arrived,
    cache_v, memory_v, tokens_v, new_kv_v, gain_v, query_v, wish, packed, queries, wishes, crosses, bias, bias_c,
    outs, stats, owner_out, got, got_stats, cross_out, hidden_v, pages, slots, returned,
    held, first_v, second_v, picked, inner, total, to_twin, from_twin, to_chip, from_chip, far, result,
    l_sem, local, k_send, k_recv, n_send, n_recv, e_send, e_recv, b_send, b_recv, s_send, s_recv, c_send, c_recv,
    d_send, d_recv, r_send, r_recv,
    g_send, g_recv, o_send, o_recv, t_send, t_recv,
    y_send, y_recv, x_send, x_recv, f_send, f_recv, p_send, p_recv,
):
    dp, ex, z, y = place()
    x, core = lax.div(dp, 2), lax.rem(dp, 2)
    twin = x * 2 + 1 - core
    chip = [x, lax.rem(x + CHIPS - 1, CHIPS), lax.rem(x + 1, CHIPS), lax.rem(x + 2, CHIPS)]
    row_count, width = tokens.shape
    hidden = first.shape[-1]
    kind = tokens.dtype
    heads = width // HEAD
    span = cache.shape[1]
    quarter, reach = memory.shape[:2]
    cap = slots.shape[1]
    block = EXPERTS * cap
    scale = 1.0 / math.sqrt(HEAD)

    barrier = pltpu.get_barrier_semaphore()
    for a in range(BEAM):
        for b in range(GROUP):
            if a or b:
                greet(barrier, dp, lax.rem(z + a, BEAM) * GROUP + lax.rem(y + b, GROUP))
    greet(barrier, twin, ex)
    for side in (LEFT, RIGHT, OPPOSITE):
        greet(barrier, chip[side] * 2 + core, ex)
    pairs = (
        (query, query_v), (new_kv, new_kv_v), (cache, cache_v), (memory, memory_v),
        (tokens, tokens_v), (gain, gain_v), (first, first_v), (second, second_v),
    )
    loads = [pltpu.make_async_copy(a, b, l_sem.at[i]) for i, (a, b) in enumerate(pairs)]
    for load in loads:
        load.start()
    own_cross = pltpu.make_async_copy(cross.at[y], crosses.at[z], local.at[2])
    pl.when(z == y)(own_cross.start)

    parent_row = real(parents[...])
    parent = upright(parent_row)
    parent_rank = rank(parent, [parent_row])
    rank_row = flat(parent_rank)
    ticket = number((BEAM * PAGE_CAP, row_count), 0)
    chosen = (real(lax.div(ticket, PAGE_CAP)) == parent_row) & (real(lax.rem(ticket, PAGE_CAP)) == rank_row)
    chosen = real(chosen).astype(kind)
    wish[0:1, :row_count] = parents[...]
    loads[0].wait()
    lines = jnp.dot(chosen, query_v[...], preferred_element_type=jnp.float32).astype(kind)
    packed[...] = lines.reshape(packed.shape)
    pl.semaphore_wait(barrier, EXPERTS - 1 + 4)

    sent = []
    asks = []
    for off in (1, 3, 2):
        other = lax.rem(z + off, BEAM)
        target = other * GROUP + y
        asks.append(send(wish, wishes.at[z], n_send.at[off - 1], n_recv.at[off - 1], dp, target))
        asks.append(send(packed.at[other], queries.at[z], k_send.at[off - 1], k_recv.at[off - 1], dp, target))
    for move in asks:
        move.start()
    crossing = [
        send(cross.at[p], crosses.at[z], e_send.at[p], e_recv.at[z], dp, y * GROUP + p) for p in range(GROUP)
    ]
    for p in range(GROUP):
        pl.when(y * GROUP + p != ex)(crossing[p].start)
    queries[z] = packed[z]
    wishes[z] = wish[...]

    loads[1].wait()
    lane = number((row_count, HEAD), 1)
    own = jnp.zeros((row_count, HEAD), jnp.float32)
    for h in range(heads):
        spot = slice(h * HEAD, (h + 1) * HEAD)
        both = real(query_v[:, spot]) * real(new_kv_v[:, spot])
        own = own + jnp.where(lane == h, jnp.sum(both, -1, keepdims=True) * scale, 0.0)
    named_rows = [real(routes[k : k + 1, :]) for k in range(2)]
    named = [upright(row) for row in named_rows]
    slot = [column * float(cap) + rank(column, named_rows) for column in named]
    slot_rows = [flat(column) for column in slot]

    at = number((row_count, dec_len.shape[1]), 1) - y * row_count == number((row_count, dec_len.shape[1]), 0)
    lengths = jnp.sum(jnp.where(at, real(dec_len[...]), 0.0), 1, keepdims=True)
    keys = row_count * span
    in_reach = real(lax.rem(number((1, keys), 1), span)) < spread(lengths, span)
    keys_c = quarter * reach
    in_reach_c = real(lax.rem(number((1, keys_c), 1), reach)) < spread(upright(real(src_len[...])), reach)
    asked_c = BEAM * quarter
    same_c = lax.rem(number((asked_c, keys_c), 0), quarter) == lax.div(number((asked_c, keys_c), 1), reach)
    for half in range(2):
        bias_c[half * asked_c : (half + 1) * asked_c, :] = jnp.where(same_c & in_reach_c, 0.0, -1e30)

    loads[2].wait()
    for move in asks:
        move.wait()
    asked = BEAM * PAGE_CAP
    ticket = real(number((PAGE_CAP, keys), 0))
    codes = []
    for beam in range(BEAM):
        wanted_row = real(wishes[beam, 0:1, :row_count])
        wanted = upright(wanted_row)
        code = spread(jnp.where(wanted == real(z), rank(wanted, [wanted_row]), -1.0), span)
        codes.append(code)
        part = jnp.where((ticket == code) & in_reach, 0.0, -1e30)
        for half in range(2):
            first_row = half * asked + beam * PAGE_CAP
            bias[first_row : first_row + PAGE_CAP, :] = part
    stats[...] = jnp.zeros_like(stats)
    pair = 2 * HEAD
    batch = math.gcd(heads // 2, 2)

    def attend(asker, keeper, extra, base):
        blank = jnp.zeros((asker.shape[0], HEAD), kind)
        both = jnp.concatenate(
            [
                jnp.concatenate([asker[:, :HEAD], blank], 1),
                jnp.concatenate([blank, asker[:, HEAD:]], 1),
            ],
            0,
        )
        keys_of = keeper(base)
        scores = lax.dot_general(both, keys_of, (((1,), (1,)), ((), ())), preferred_element_type=jnp.float32)
        scores = scores * scale + extra[...]
        peak = jnp.max(scores, -1, keepdims=True)
        terms = jnp.exp(scores - peak)
        mass = jnp.sum(terms, -1, keepdims=True)
        part = jnp.dot((terms / mass).astype(kind), keeper(width + base), preferred_element_type=jnp.float32)
        return part.astype(kind), peak + jnp.log(mass)

    stat_lane = number((asked, HEAD), 1)

    @pl.loop(0, heads // 2 // batch)
    def _(n):
        for m in range(batch):
            base = (n * batch + m) * pair
            spot = pl.ds(pl.multiple_of(base, pair), pair)

            def keeper(start):
                return cache_v[:, :, pl.ds(pl.multiple_of(start, pair), pair)].reshape(keys, pair)

            part, level = attend(queries[:, :, spot].reshape(asked, pair), keeper, bias, base)
            levels = jnp.zeros((asked, HEAD), jnp.float32)
            for half in range(2):
                rows = slice(half * asked, (half + 1) * asked)
                piece = part[rows, half * HEAD : (half + 1) * HEAD].reshape(BEAM, PAGE_CAP, HEAD)
                outs[:, :, pl.ds(pl.multiple_of(base + half * HEAD, HEAD), HEAD)] = piece
                levels = jnp.where(stat_lane == 2 * (n * batch + m) + half, level[rows], levels)
            stats[...] += levels.reshape(BEAM, PAGE_CAP, HEAD)

    answers = []
    for off in (1, 3, 2):
        other = lax.rem(z + off, BEAM)
        target = other * GROUP + y
        answers.append(send(stats.at[other], got_stats.at[z], b_send.at[off - 1], b_recv.at[off - 1], dp, target))
        answers.append(send(outs.at[other], got.at[z], s_send.at[off - 1], s_recv.at[off - 1], dp, target))
    for move in answers:
        move.start()
    got[z] = outs[z]
    got_stats[z] = stats[z]

    for p in range(GROUP):
        pl.when(y * GROUP + p != ex)(crossing[p].wait_send)
    for beam in range(BEAM):
        coming = send(cross.at[0], crosses.at[beam], e_send.at[0], e_recv.at[beam], dp, beam * GROUP + z)
        pl.when(beam * GROUP + z != ex)(coming.wait_recv)
    pl.when(z == y)(own_cross.wait)
    loads[3].wait()

    @pl.loop(0, heads // 2 // batch)
    def _(n):
        for m in range(batch):
            base = (n * batch + m) * pair
            spot = pl.ds(pl.multiple_of(base, pair), pair)

            def keeper(start):
                return memory_v[:, :, pl.ds(pl.multiple_of(start, pair), pair)].reshape(keys_c, pair)

            part, _ = attend(crosses[:, :, spot].reshape(asked_c, pair), keeper, bias_c, base)
            for half in range(2):
                piece = part[half * asked_c : (half + 1) * asked_c, half * HEAD : (half + 1) * HEAD]
                place_at = pl.ds(pl.multiple_of(base + half * HEAD, HEAD), HEAD)
                owner_out[:, :, place_at] = piece.reshape(BEAM, quarter, HEAD)

    own_back = pltpu.make_async_copy(owner_out.at[z], cross_out.at[y], local.at[2])
    crossing = [
        send(owner_out.at[beam], cross_out.at[y], c_send.at[beam], c_recv.at[y], dp, beam * GROUP + z)
        for beam in range(BEAM)
    ]
    for beam in range(BEAM):
        pl.when(beam * GROUP + z != ex)(crossing[beam].start)
    pl.when(z == y)(own_back.start)

    paged = []

    def turn(off, start, stop, which):
        rows = pl.ds(start, stop - start)
        move = send(
            pages.at[off - 1, rows], arrived.at[off - 1, rows], p_send.at[off - 1, which], p_recv.at[off - 1, which],
            dp, lax.rem(z + off, BEAM) * GROUP + y,
        )
        move.start()
        paged.append(move)

    page_shape = (PAGE_CAP * span, keys)
    page_row, page_lane = number(page_shape, 0), number(page_shape, 1)
    page_slot = real(lax.div(page_row, span))
    same_place = lax.rem(page_row, span) == lax.rem(page_lane, span)
    strip = min(1024, 2 * width)
    for off in (1, 3, 2):
        asker = lax.rem(z + off, BEAM)
        code = jnp.zeros_like(codes[0])
        for beam in range(BEAM):
            code = code + jnp.where(real(asker) == float(beam), codes[beam], 0.0)
        pick = real(same_place & (page_slot == code)).astype(kind)

        @pl.loop(0, 2 * width // strip)
        def _(n):
            spot = pl.ds(pl.multiple_of(n * strip, strip), strip)
            part = jnp.dot(pick, cache_v[:, :, spot].reshape(keys, strip), preferred_element_type=jnp.float32)
            pages[off - 1, :, :, spot] = part.astype(kind).reshape(PAGE_CAP, span, strip)

        if off != 2 and EARLY:
            turn(off, 0, EARLY, 0)

    for load in loads[4:6]:
        load.wait()
    for move in answers:
        move.wait()
    for beam in range(BEAM):
        pl.when(beam * GROUP + z != ex)(crossing[beam].wait_send)
    for p in range(GROUP):
        coming = send(owner_out.at[0], cross_out.at[p], c_send.at[0], c_recv.at[p], dp, y * GROUP + p)
        pl.when(y * GROUP + p != ex)(coming.wait_recv)
    pl.when(z == y)(own_back.wait)

    ticket = number((row_count, asked), 1)
    chosen = (parent == real(lax.div(ticket, PAGE_CAP))) & (parent_rank == real(lax.rem(ticket, PAGE_CAP)))
    chosen = real(chosen)
    level = jnp.dot(
        chosen,
        got_stats[...].reshape(asked, HEAD),
        precision=lax.Precision.HIGHEST,
        preferred_element_type=jnp.float32,
    )
    cached = jnp.dot(chosen.astype(kind), got[...].reshape(asked, width), preferred_element_type=jnp.float32)
    top = jnp.maximum(level, own)
    cache_part = jnp.exp(level - top)
    own_part = jnp.exp(own - top)
    cache_share = cache_part / (cache_part + own_part)
    own_share = own_part / (cache_part + own_part)
    for h in range(heads):
        spot = slice(h * HEAD, (h + 1) * HEAD)
        own_value = real(new_kv_v[:, width + h * HEAD : width + (h + 1) * HEAD])
        mine = cache_share[:, h : h + 1] * cached[:, spot] + own_share[:, h : h + 1] * own_value
        crossed = real(cross_out[:, :, spot].reshape(row_count, HEAD))
        hidden_v[:, spot] = real(tokens_v[:, spot]) + mine + crossed
    whole = hidden_v[...]
    centered = whole - jnp.mean(whole, -1, keepdims=True)
    variance = jnp.mean(centered * centered, -1, keepdims=True)
    moe_in = (centered * lax.rsqrt(variance + 1e-05) * gain_v[...]).astype(kind)
    slot_row = real(number((block, row_count), 0))
    table = real((slot_row == slot_rows[0]) | (slot_row == slot_rows[1])).astype(kind)
    packets = jnp.dot(table, moe_in, preferred_element_type=jnp.float32).astype(kind)
    slots[...] = packets.reshape(slots.shape)

    def peer(a, b):
        return lax.rem(z + a, BEAM) * GROUP + lax.rem(y + b, GROUP)

    def source(a, b):
        return lax.rem(z + BEAM - a, BEAM) * GROUP + lax.rem(y + GROUP - b, GROUP)

    home = held.at[x, core]
    stay = pltpu.make_async_copy(slots.at[ex], home.at[ex], local.at[0])
    stay.start()
    for a in ORDER:
        for b in range(GROUP):
            if a or b:
                spot = a * GROUP + b
                move = send(slots.at[peer(a, b)], home.at[ex], d_send.at[spot], d_recv.at[spot], dp, peer(a, b))
                move.start()
                sent.append(move)

    def chunk(which, owner, j):
        zz = lax.rem(z + BEAM - ORDER[j], BEAM)
        return held.at[chip[which], owner, pl.ds(zz * GROUP, GROUP)]

    def to_sibling(which, j):
        part = chunk(which, core, j)
        move = send(part, part, t_send.at[which, j], t_recv.at[which, j], twin, ex)
        move.start()
        sent.append(move)

    def from_sibling(which):
        for j in range(4):
            part = chunk(which, 1 - core, j)
            send(part, part, t_send.at[which, j], t_recv.at[which, j], twin, ex).wait_recv()

    stay.wait()
    for j, a in enumerate(ORDER):
        for b in range(GROUP):
            if a or b:
                spot = a * GROUP + b
                there = home.at[source(a, b)]
                send(there, there, d_send.at[spot], d_recv.at[spot], dp, source(a, b)).wait_recv()
        part = chunk(OWN, core, j)
        for way, side in ((0, RIGHT), (1, LEFT)):
            move = send(part, part, g_send.at[way, j], g_recv.at[way, j], chip[side] * 2 + core, ex)
            move.start()
            sent.append(move)
        to_sibling(OWN, j)

    cells = picked.shape[0] // 2
    tile = min(1024, hidden)
    wide = min(1024, width)
    slim = min(256, width)
    band = block // 4

    def up(which):
        for half, owner in ((0, core), (1, 1 - core)):
            picked[half * cells : (half + 1) * cells, :] = held[chip[which], owner].reshape(cells, width)

        @pl.loop(0, hidden // tile)
        def _(n):
            spot = pl.ds(pl.multiple_of(n * tile, tile), tile)
            part = jnp.dot(picked[...], first_v[:, spot], preferred_element_type=jnp.float32)
            inner[:, spot] = jnp.maximum(part, 0.0).astype(inner.dtype)

    def down(which):
        @pl.loop(0, width // wide)
        def _(n):
            spot = pl.ds(pl.multiple_of(n * wide, wide), wide)
            part = jnp.dot(inner[...], second_v[:, spot], preferred_element_type=jnp.float32)
            total[which, :, spot] = part[:cells]
            to_twin[which, :, spot] = part[cells:].astype(to_twin.dtype)

        move = send(to_twin.at[which], from_twin.at[which], y_send.at[which], y_recv.at[which], twin, ex)
        move.start()
        sent.append(move)

    def forward(which):
        there = from_twin.at[which]
        send(there, there, y_send.at[which], y_recv.at[which], twin, ex).wait_recv()

        @pl.loop(0, width // slim)
        def _(n):
            spot = pl.ds(pl.multiple_of(n * slim, slim), slim)
            both = total[which, :, spot] + from_twin[which, :, spot].astype(jnp.float32)
            to_chip[which - 1, :, spot] = both.astype(to_chip.dtype)

        if which == OPPOSITE:
            for q in (0, 2, 1, 3):
                rows = pl.ds(q * band, band)
                relay(to_chip.at[2, rows], far.at[rows], f_send.at[q], f_recv.at[q], RIGHT if q < 2 else LEFT)
        else:
            for q in (2, 3) if which == RIGHT else (0, 1):
                last_leg(which, q)

    def relay(src, dst, send_sem, recv_sem, side):
        move = send(src, dst, send_sem, recv_sem, chip[side] * 2 + core, ex)
        move.start()
        sent.append(move)

    def last_leg(which, q):
        rows = pl.ds(q * band, band)
        spot = which - 1
        relay(to_chip.at[spot, rows], from_chip.at[spot, rows], x_send.at[spot, q], x_recv.at[spot, q], which)

    def merge(q):
        rows = pl.ds(q * band, band)
        which = RIGHT if q < 2 else LEFT
        there = far.at[rows]
        send(there, there, f_send.at[q], f_recv.at[q], dp, ex).wait_recv()

        @pl.loop(0, width // slim)
        def _(n):
            spot = pl.ds(pl.multiple_of(n * slim, slim), slim)
            both = to_chip[which - 1, rows, spot].astype(jnp.float32) + far[rows, spot].astype(jnp.float32)
            to_chip[which - 1, rows, spot] = both.astype(to_chip.dtype)

        last_leg(which, q)

    def landed(way, j):
        side = LEFT if way == 0 else RIGHT
        part = chunk(side, core, j)
        send(part, part, g_send.at[way, j], g_recv.at[way, j], dp, ex).wait_recv()
        to_sibling(side, j)
        if (j < 2) == (way == 0):
            onward = RIGHT if way == 0 else LEFT
            move = send(part, part, o_send.at[j], o_recv.at[j], chip[onward] * 2 + core, ex)
            move.start()
            sent.append(move)

    for off in (1, 3, 2):
        begin = EARLY if off != 2 else 0
        turn(off, begin, PAGE_CAP, 1)
    for load in loads[6:8]:
        load.wait()
    from_sibling(OWN)
    up(OWN)
    down(OWN)
    for j in range(4):
        landed(0, j)
        landed(1, j)
    from_sibling(LEFT)
    up(LEFT)
    down(LEFT)
    from_sibling(RIGHT)
    up(RIGHT)
    forward(LEFT)
    down(RIGHT)
    for j in range(4):
        part = chunk(OPPOSITE, core, j)
        send(part, part, o_send.at[j], o_recv.at[j], dp, ex).wait_recv()
        to_sibling(OPPOSITE, j)
    from_sibling(OPPOSITE)
    up(OPPOSITE)
    forward(RIGHT)
    down(OPPOSITE)
    forward(OPPOSITE)
    for q in (0, 2, 1, 3):
        merge(q)

    there = from_twin.at[OWN]
    send(there, there, y_send.at[OWN], y_recv.at[OWN], twin, ex).wait_recv()
    stay = pltpu.make_async_copy(result.at[ex], returned.at[ex], local.at[1])
    for q in (0, 2, 1, 3):
        rows = pl.ds(q * band, band)
        for spot in (0, 1):
            there = from_chip.at[spot, rows]
            send(there, there, x_send.at[spot, q], x_recv.at[spot, q], dp, ex).wait_recv()

        @pl.loop(0, width // slim)
        def _(n):
            spot = pl.ds(pl.multiple_of(n * slim, slim), slim)
            whole = total[OWN, rows, spot] + from_twin[OWN, rows, spot].astype(jnp.float32)
            for side in (0, 1):
                whole = whole + from_chip[side, rows, spot].astype(jnp.float32)
            packets = whole.astype(result.dtype).reshape(GROUP, cap, slim)
            result[q * GROUP : (q + 1) * GROUP, :, spot] = packets

        for target in range(q * GROUP, (q + 1) * GROUP):
            move = send(result.at[target], returned.at[ex], r_send.at[target], r_recv.at[ex], dp, target)
            pl.when(target != ex)(move.start)
            pl.when(target == ex)(stay.start)
    for origin in range(EXPERTS):
        there = returned.at[origin]
        move = send(there, there, r_send.at[origin], r_recv.at[origin], dp, origin)
        pl.when(origin != ex)(move.wait)
    stay.wait()
    back = returned[...].reshape(block, width)
    places = real(number((row_count, block), 1))
    final = hidden_v[...]
    for k in range(2):
        taken = real(places == slot[k]).astype(kind)
        final = final + upright(gates[k : k + 1, :]) * jnp.dot(taken, back, preferred_element_type=jnp.float32)
    mixed[...] = final.astype(mixed.dtype)
    for move in sent:
        move.wait_send()
    for move in paged:
        move.wait()


def layer(*operands):
    tokens, _, _, cache, memory, first, second = operands[7:]
    row_count, width = tokens.shape
    hidden = first.shape[-1]
    kind = tokens.dtype
    cap = 4 * row_count // EXPERTS
    block = EXPERTS * cap
    quarter = row_count // BEAM

    def room(*shape, dtype=kind):
        return pltpu.VMEM(shape, dtype)

    paged = (BEAM - 1, PAGE_CAP) + cache.shape[1:]
    scratch = [
        room(*cache.shape), room(*memory.shape), room(row_count, width), room(row_count, 2 * width),
        room(1, width, dtype=jnp.float32), room(row_count, width), room(8, HEAD, dtype=jnp.int32),
        room(BEAM, PAGE_CAP, width), room(BEAM, PAGE_CAP, width), room(BEAM, 8, HEAD, dtype=jnp.int32),
        room(BEAM, quarter, width), room(2 * BEAM * PAGE_CAP, row_count * cache.shape[1], dtype=jnp.float32),
        room(2 * BEAM * quarter, quarter * memory.shape[1], dtype=jnp.float32),
        room(BEAM, PAGE_CAP, width), room(BEAM, PAGE_CAP, HEAD, dtype=jnp.float32), room(BEAM, quarter, width),
        room(BEAM, PAGE_CAP, width), room(BEAM, PAGE_CAP, HEAD, dtype=jnp.float32), room(BEAM, quarter, width),
        room(row_count, width, dtype=jnp.float32), room(*paged), room(EXPERTS, cap, width), room(EXPERTS, cap, width),
        room(CHIPS, 2, EXPERTS, cap, width), room(*first.shape), room(*second.shape),
        room(2 * block, width), room(2 * block, hidden), room(4, block, width, dtype=jnp.float32),
        room(4, block, width), room(4, block, width), room(3, block, width), room(2, block, width),
        room(block, width), room(EXPERTS, cap, width),
    ]
    sems = [
        DMA((8,)), DMA((3,)), DMA((3,)), DMA((3,)), DMA((3,)), DMA((3,)), DMA((4,)), DMA((4,)),
        DMA((3,)), DMA((3,)), DMA((3,)), DMA((3,)), DMA((4,)), DMA((4,)),
        DMA((16,)), DMA((16,)), DMA((16,)), DMA((16,)),
        DMA((2, 4)), DMA((2, 4)), DMA((4,)), DMA((4,)), DMA((4, 4)), DMA((4, 4)),
        DMA((4,)), DMA((4,)), DMA((2, 4)), DMA((2, 4)), DMA((4,)), DMA((4,)), DMA((3, 2)), DMA((3, 2)),
    ]
    return pl.pallas_call(
        layer_kernel,
        out_shape=[jax.ShapeDtypeStruct((row_count, width), kind), jax.ShapeDtypeStruct(paged, kind)],
        in_specs=[ANY] * 2 + [pl.BlockSpec(memory_space=pltpu.VMEM)] * 5 + [ANY] * 7,
        out_specs=[pl.BlockSpec(memory_space=pltpu.VMEM), ANY],
        scratch_shapes=scratch + sems,
        compiler_params=pltpu.CompilerParams(
            collective_id=0, has_side_effects=True, vmem_limit_bytes=58 * 2**20
        ),
        name="layer",
    )(*operands)


def per_device(
    tokens,
    self_query,
    new_kv,
    kv_cache,
    parents,
    dec_len,
    cross_query,
    memory,
    src_len,
    norm_gain,
    routes,
    gate_weights,
    expert_in,
    expert_out,
):
    row_count, model_width = tokens.shape
    mixed, arrived = layer(
        self_query,
        cross_query.reshape(GROUP, row_count // BEAM, model_width),
        parents[None],
        dec_len[None],
        src_len[None],
        routes.T,
        gate_weights.T,
        tokens,
        new_kv,
        norm_gain[None],
        kv_cache,
        memory,
        expert_in[0],
        expert_out[0],
    )
    return (mixed, unpack(parents, kv_cache, arrived))


def solution(mesh):
    placed = (
        P(("dp", "expert"), None),
        P(("dp", "expert"), None),
        P(("dp", "expert"), None),
        P(("dp", "expert"), None, None),
        P(("dp", "expert")),
        P("dp"),
        P(("dp", "expert"), None),
        P(("dp", "expert"), None, None),
        P(("dp", "expert")),
        P(),
        P(("dp", "expert"), None),
        P(("dp", "expert"), None),
        P("expert", None, "dp"),
        P("expert", "dp", None),
    )
    return jax.shard_map(
        per_device,
        mesh=mesh,
        in_specs=placed,
        out_specs=(P(("dp", "expert"), None), P(("dp", "expert"), None, None)),
        check_vma=False,
    )
```

```python
import functools
import math

import jax
import jax.numpy as jnp
from jax import lax
from jax.experimental import pallas as pl
from jax.experimental.pallas import tpu as pltpu
from jax.sharding import PartitionSpec as P

HEAD = 128
BEAM = 4
GROUP = 4
CHIPS = 4
EXPERTS = 16
PAGE_CAP = 16
MESH = pl.DeviceIdType.MESH
ANY = pl.BlockSpec(memory_space=pl.ANY)
DMA = pltpu.SemaphoreType.DMA


def place():
    dp = lax.axis_index("dp")
    ex = lax.axis_index("expert")
    return dp, ex, lax.div(ex, GROUP), lax.rem(ex, GROUP)


def send(src, dst, send_sem, recv_sem, dp, ex):
    return pltpu.make_async_remote_copy(
        src_ref=src,
        dst_ref=dst,
        send_sem=send_sem,
        recv_sem=recv_sem,
        device_id=(dp, ex),
        device_id_type=MESH,
    )


def greet(barrier, dp, ex):
    pl.semaphore_signal(barrier, inc=1, device_id=(dp, ex), device_id_type=MESH)


def unpack_kernel(parents, cache, arrived, fresh, sem):
    _, _, z, _ = place()
    rows = cache.shape[0]

    def begin(row, counts):
        parent = parents[row]
        off = lax.rem(z - parent + BEAM, BEAM)

        def keep():
            pltpu.make_async_copy(cache.at[row], fresh.at[row], sem).start()

        pl.when(off == 0)(keep)
        after = []
        for step in range(1, BEAM):
            hit = off == step

            def take(step=step):
                pltpu.make_async_copy(arrived.at[step - 1, counts[step - 1]], fresh.at[row], sem).start()

            pl.when(hit)(take)
            after.append(counts[step - 1] + hit.astype(jnp.int32))
        return tuple(after)

    lax.fori_loop(0, rows, begin, (jnp.int32(0),) * (BEAM - 1))
    pltpu.make_async_copy(cache, fresh, sem).wait()


def unpack(parents, cache, arrived):
    return pl.pallas_call(
        unpack_kernel,
        out_shape=jax.ShapeDtypeStruct(cache.shape, cache.dtype),
        in_specs=[pl.BlockSpec(memory_space=pltpu.SMEM), ANY, ANY],
        out_specs=pl.BlockSpec(memory_space=pltpu.VMEM),
        scratch_shapes=[DMA],
        compiler_params=pltpu.CompilerParams(vmem_limit_bytes=58 * 2**20),
        name="unpack",
    )(parents, cache, arrived)


ORDER = (0, 1, 3, 2)
OWN, LEFT, RIGHT, OPPOSITE = range(4)
EARLY = 4
MID = 2


def eye(n):
    shape = (n, n)
    return lax.broadcasted_iota(jnp.int32, shape, 0) == lax.broadcasted_iota(jnp.int32, shape, 1)


def upright(row):
    return jnp.sum(jnp.where(eye(row.shape[1]), row, 0.0), 1, keepdims=True)


def flat(column):
    return jnp.sum(jnp.where(eye(column.shape[0]), column, 0.0), 0, keepdims=True)


def spread(column, times):
    shape = (column.shape[0], column.shape[0] * times)
    owner = lax.div(lax.broadcasted_iota(jnp.int32, shape, 1), times)
    return jnp.sum(jnp.where(owner == lax.broadcasted_iota(jnp.int32, shape, 0), column, 0.0), 0, keepdims=True)


def rank(column, rows):
    shape = (column.shape[0], rows[0].shape[1])
    earlier = lax.broadcasted_iota(jnp.int32, shape, 1) < lax.broadcasted_iota(jnp.int32, shape, 0)
    alike = functools.reduce(jnp.logical_or, [column == row for row in rows])
    return jnp.sum(jnp.where(earlier & alike, 1.0, 0.0), 1, keepdims=True)


def number(shape, axis):
    return lax.broadcasted_iota(jnp.int32, shape, axis)


def real(values):
    return values.astype(jnp.float32)


def layer_kernel(
    query, cross, parents, dec_len, src_len, routes, gates, tokens, new_kv, gain, cache, memory, first, second,
    mixed, arrived,
    cache_v, memory_v, tokens_v, new_kv_v, gain_v, query_v, wish, packed, queries, wishes, crosses, bias, bias_c,
    outs, stats, owner_out, got, got_stats, cross_out, hidden_v, pages, slots, returned,
    held, first_v, second_v, picked, inner, total, to_twin, from_twin, to_chip, from_chip, far, result,
    l_sem, local, k_send, k_recv, n_send, n_recv, e_send, e_recv, b_send, b_recv, s_send, s_recv, c_send, c_recv,
    d_send, d_recv, r_send, r_recv,
    g_send, g_recv, o_send, o_recv, t_send, t_recv,
    y_send, y_recv, x_send, x_recv, f_send, f_recv, p_send, p_recv,
):
    dp, ex, z, y = place()
    x, core = lax.div(dp, 2), lax.rem(dp, 2)
    twin = x * 2 + 1 - core
    chip = [x, lax.rem(x + CHIPS - 1, CHIPS), lax.rem(x + 1, CHIPS), lax.rem(x + 2, CHIPS)]
    row_count, width = tokens.shape
    hidden = first.shape[-1]
    kind = tokens.dtype
    heads = width // HEAD
    span = cache.shape[1]
    quarter, reach = memory.shape[:2]
    cap = slots.shape[1]
    block = EXPERTS * cap
    scale = 1.0 / math.sqrt(HEAD)

    barrier = pltpu.get_barrier_semaphore()
    for a in range(BEAM):
        for b in range(GROUP):
            if a or b:
                greet(barrier, dp, lax.rem(z + a, BEAM) * GROUP + lax.rem(y + b, GROUP))
    greet(barrier, twin, ex)
    for side in (LEFT, RIGHT, OPPOSITE):
        greet(barrier, chip[side] * 2 + core, ex)
    pairs = (
        (query, query_v), (new_kv, new_kv_v), (cache, cache_v), (memory, memory_v),
        (tokens, tokens_v), (gain, gain_v), (first, first_v), (second, second_v),
    )
    loads = [pltpu.make_async_copy(a, b, l_sem.at[i]) for i, (a, b) in enumerate(pairs)]
    for i in (0, 3, 1, 2, 4, 5, 6, 7):
        loads[i].start()
    own_cross = pltpu.make_async_copy(cross.at[y], crosses.at[z], local.at[2])
    pl.when(z == y)(own_cross.start)

    parent_row = real(parents[...])
    parent = upright(parent_row)
    parent_rank = rank(parent, [parent_row])
    rank_row = flat(parent_rank)
    ticket = number((BEAM * PAGE_CAP, row_count), 0)
    chosen = (real(lax.div(ticket, PAGE_CAP)) == parent_row) & (real(lax.rem(ticket, PAGE_CAP)) == rank_row)
    chosen = real(chosen).astype(kind)
    wish[0:1, :row_count] = parents[...]
    loads[0].wait()
    lines = jnp.dot(chosen, query_v[...], preferred_element_type=jnp.float32).astype(kind)
    packed[...] = lines.reshape(packed.shape)
    pl.semaphore_wait(barrier, EXPERTS - 1 + 4)

    sent = []
    crossing = [
        send(cross.at[p], crosses.at[z], e_send.at[p], e_recv.at[z], dp, y * GROUP + p) for p in range(GROUP)
    ]
    for p in range(GROUP):
        pl.when(y * GROUP + p != ex)(crossing[p].start)
    asks = []
    for off in (1, 3, 2):
        other = lax.rem(z + off, BEAM)
        target = other * GROUP + y
        asks.append(send(wish, wishes.at[z], n_send.at[off - 1], n_recv.at[off - 1], dp, target))
        asks.append(send(packed.at[other], queries.at[z], k_send.at[off - 1], k_recv.at[off - 1], dp, target))
    for move in asks:
        move.start()
    queries[z] = packed[z]
    wishes[z] = wish[...]

    loads[1].wait()
    lane = number((row_count, HEAD), 1)
    own = jnp.zeros((row_count, HEAD), jnp.float32)
    for h in range(heads):
        spot = slice(h * HEAD, (h + 1) * HEAD)
        both = real(query_v[:, spot]) * real(new_kv_v[:, spot])
        own = own + jnp.where(lane == h, jnp.sum(both, -1, keepdims=True) * scale, 0.0)
    named_rows = [real(routes[k : k + 1, :]) for k in range(2)]
    named = [upright(row) for row in named_rows]
    slot = [column * float(cap) + rank(column, named_rows) for column in named]
    slot_rows = [flat(column) for column in slot]

    at = number((row_count, dec_len.shape[1]), 1) - y * row_count == number((row_count, dec_len.shape[1]), 0)
    lengths = jnp.sum(jnp.where(at, real(dec_len[...]), 0.0), 1, keepdims=True)
    keys = row_count * span
    in_reach = real(lax.rem(number((1, keys), 1), span)) < spread(lengths, span)
    keys_c = quarter * reach
    in_reach_c = real(lax.rem(number((1, keys_c), 1), reach)) < spread(upright(real(src_len[...])), reach)
    asked_c = BEAM * quarter
    same_c = lax.rem(number((asked_c, keys_c), 0), quarter) == lax.div(number((asked_c, keys_c), 1), reach)
    for half in range(2):
        bias_c[half * asked_c : (half + 1) * asked_c, :] = jnp.where(same_c & in_reach_c, 0.0, -1e30)

    pair = 2 * HEAD
    batch = math.gcd(heads // 2, 8)

    def attend(asker, keeper, extra, base):
        blank = jnp.zeros((asker.shape[0], HEAD), kind)
        both = jnp.concatenate(
            [
                jnp.concatenate([asker[:, :HEAD], blank], 1),
                jnp.concatenate([blank, asker[:, HEAD:]], 1),
            ],
            0,
        )
        keys_of = keeper(base)
        scores = lax.dot_general(both, keys_of, (((1,), (1,)), ((), ())), preferred_element_type=jnp.float32)
        scores = scores * scale + extra[...]
        peak = jnp.max(scores, -1, keepdims=True)
        terms = jnp.exp(scores - peak)
        mass = jnp.sum(terms, -1, keepdims=True)
        part = jnp.dot((terms / mass).astype(kind), keeper(width + base), preferred_element_type=jnp.float32)
        return part.astype(kind), peak + jnp.log(mass)

    for p in range(GROUP):
        pl.when(y * GROUP + p != ex)(crossing[p].wait_send)
    for beam in range(BEAM):
        coming = send(cross.at[0], crosses.at[beam], e_send.at[0], e_recv.at[beam], dp, beam * GROUP + z)
        pl.when(beam * GROUP + z != ex)(coming.wait_recv)
    pl.when(z == y)(own_cross.wait)
    loads[3].wait()

    @pl.loop(0, heads // 2 // batch)
    def _(n):
        for m in range(batch):
            base = (n * batch + m) * pair
            spot = pl.ds(pl.multiple_of(base, pair), pair)

            def keeper(start):
                return memory_v[:, :, pl.ds(pl.multiple_of(start, pair), pair)].reshape(keys_c, pair)

            part, _ = attend(crosses[:, :, spot].reshape(asked_c, pair), keeper, bias_c, base)
            for half in range(2):
                piece = part[half * asked_c : (half + 1) * asked_c, half * HEAD : (half + 1) * HEAD]
                place_at = pl.ds(pl.multiple_of(base + half * HEAD, HEAD), HEAD)
                owner_out[:, :, place_at] = piece.reshape(BEAM, quarter, HEAD)

    own_back = pltpu.make_async_copy(owner_out.at[z], cross_out.at[y], local.at[2])
    crossing = [
        send(owner_out.at[beam], cross_out.at[y], c_send.at[beam], c_recv.at[y], dp, beam * GROUP + z)
        for beam in range(BEAM)
    ]
    for beam in range(BEAM):
        pl.when(beam * GROUP + z != ex)(crossing[beam].start)
    pl.when(z == y)(own_back.start)

    loads[2].wait()
    for move in asks:
        move.wait()
    asked = BEAM * PAGE_CAP
    ticket = real(number((PAGE_CAP, keys), 0))
    codes = []
    for beam in range(BEAM):
        wanted_row = real(wishes[beam, 0:1, :row_count])
        wanted = upright(wanted_row)
        code = spread(jnp.where(wanted == real(z), rank(wanted, [wanted_row]), -1.0), span)
        codes.append(code)
        part = jnp.where((ticket == code) & in_reach, 0.0, -1e30)
        for half in range(2):
            first_row = half * asked + beam * PAGE_CAP
            bias[first_row : first_row + PAGE_CAP, :] = part
    stats[...] = jnp.zeros_like(stats)
    stat_lane = number((asked, HEAD), 1)

    @pl.loop(0, heads // 2 // batch)
    def _(n):
        for m in range(batch):
            base = (n * batch + m) * pair
            spot = pl.ds(pl.multiple_of(base, pair), pair)

            def keeper(start):
                return cache_v[:, :, pl.ds(pl.multiple_of(start, pair), pair)].reshape(keys, pair)

            part, level = attend(queries[:, :, spot].reshape(asked, pair), keeper, bias, base)
            levels = jnp.zeros((asked, HEAD), jnp.float32)
            for half in range(2):
                rows = slice(half * asked, (half + 1) * asked)
                piece = part[rows, half * HEAD : (half + 1) * HEAD].reshape(BEAM, PAGE_CAP, HEAD)
                outs[:, :, pl.ds(pl.multiple_of(base + half * HEAD, HEAD), HEAD)] = piece
                levels = jnp.where(stat_lane == 2 * (n * batch + m) + half, level[rows], levels)
            stats[...] += levels.reshape(BEAM, PAGE_CAP, HEAD)

    answers = []
    for off in (1, 3, 2):
        other = lax.rem(z + off, BEAM)
        target = other * GROUP + y
        answers.append(send(stats.at[other], got_stats.at[z], b_send.at[off - 1], b_recv.at[off - 1], dp, target))
        answers.append(send(outs.at[other], got.at[z], s_send.at[off - 1], s_recv.at[off - 1], dp, target))
    for move in answers:
        move.start()
    got[z] = outs[z]
    got_stats[z] = stats[z]

    paged = []

    def turn(off, start, stop, which):
        rows = pl.ds(start, stop - start)
        move = send(
            pages.at[off - 1, rows], arrived.at[off - 1, rows], p_send.at[off - 1, which], p_recv.at[off - 1, which],
            dp, lax.rem(z + off, BEAM) * GROUP + y,
        )
        move.start()
        paged.append(move)

    page_shape = (PAGE_CAP * span, keys)
    page_row, page_lane = number(page_shape, 0), number(page_shape, 1)
    page_slot = real(lax.div(page_row, span))
    same_place = lax.rem(page_row, span) == lax.rem(page_lane, span)
    strip = min(1024, 2 * width)
    for off in (1, 3, 2):
        asker = lax.rem(z + off, BEAM)
        code = jnp.zeros_like(codes[0])
        for beam in range(BEAM):
            code = code + jnp.where(real(asker) == float(beam), codes[beam], 0.0)
        pick = real(same_place & (page_slot == code)).astype(kind)

        @pl.loop(0, 2 * width // strip)
        def _(n):
            spot = pl.ds(pl.multiple_of(n * strip, strip), strip)
            part = jnp.dot(pick, cache_v[:, :, spot].reshape(keys, strip), preferred_element_type=jnp.float32)
            pages[off - 1, :, :, spot] = part.astype(kind).reshape(PAGE_CAP, span, strip)

        if off != 2 and EARLY:
            turn(off, 0, EARLY, 0)

    for load in loads[4:6]:
        load.wait()
    for move in answers:
        move.wait()
    for beam in range(BEAM):
        pl.when(beam * GROUP + z != ex)(crossing[beam].wait_send)
    for p in range(GROUP):
        coming = send(owner_out.at[0], cross_out.at[p], c_send.at[0], c_recv.at[p], dp, y * GROUP + p)
        pl.when(y * GROUP + p != ex)(coming.wait_recv)
    pl.when(z == y)(own_back.wait)

    ticket = number((row_count, asked), 1)
    chosen = (parent == real(lax.div(ticket, PAGE_CAP))) & (parent_rank == real(lax.rem(ticket, PAGE_CAP)))
    chosen = real(chosen)
    level = jnp.dot(
        chosen,
        got_stats[...].reshape(asked, HEAD),
        precision=lax.Precision.HIGHEST,
        preferred_element_type=jnp.float32,
    )
    cached = jnp.dot(chosen.astype(kind), got[...].reshape(asked, width), preferred_element_type=jnp.float32)
    top = jnp.maximum(level, own)
    cache_part = jnp.exp(level - top)
    own_part = jnp.exp(own - top)
    cache_share = cache_part / (cache_part + own_part)
    own_share = own_part / (cache_part + own_part)
    for h in range(heads):
        spot = slice(h * HEAD, (h + 1) * HEAD)
        own_value = real(new_kv_v[:, width + h * HEAD : width + (h + 1) * HEAD])
        mine = cache_share[:, h : h + 1] * cached[:, spot] + own_share[:, h : h + 1] * own_value
        crossed = real(cross_out[:, :, spot].reshape(row_count, HEAD))
        hidden_v[:, spot] = real(tokens_v[:, spot]) + mine + crossed
    whole = hidden_v[...]
    centered = whole - jnp.mean(whole, -1, keepdims=True)
    variance = jnp.mean(centered * centered, -1, keepdims=True)
    moe_in = (centered * lax.rsqrt(variance + 1e-05) * gain_v[...]).astype(kind)
    slot_row = real(number((block, row_count), 0))
    table = real((slot_row == slot_rows[0]) | (slot_row == slot_rows[1])).astype(kind)
    packets = jnp.dot(table, moe_in, preferred_element_type=jnp.float32).astype(kind)
    slots[...] = packets.reshape(slots.shape)

    def peer(a, b):
        return lax.rem(z + a, BEAM) * GROUP + lax.rem(y + b, GROUP)

    def source(a, b):
        return lax.rem(z + BEAM - a, BEAM) * GROUP + lax.rem(y + GROUP - b, GROUP)

    home = held.at[x, core]
    stay = pltpu.make_async_copy(slots.at[ex], home.at[ex], local.at[0])
    stay.start()
    for a in ORDER:
        for b in range(GROUP):
            if a or b:
                spot = a * GROUP + b
                move = send(slots.at[peer(a, b)], home.at[ex], d_send.at[spot], d_recv.at[spot], dp, peer(a, b))
                move.start()
                sent.append(move)

    if MID:
        for off in (1, 3):
            turn(off, EARLY, EARLY + MID, 2)

    def chunk(which, owner, j):
        zz = lax.rem(z + BEAM - ORDER[j], BEAM)
        return held.at[chip[which], owner, pl.ds(zz * GROUP, GROUP)]

    def to_sibling(which, j):
        part = chunk(which, core, j)
        move = send(part, part, t_send.at[which, j], t_recv.at[which, j], twin, ex)
        move.start()
        sent.append(move)

    def from_sibling(which):
        for j in range(4):
            part = chunk(which, 1 - core, j)
            send(part, part, t_send.at[which, j], t_recv.at[which, j], twin, ex).wait_recv()

    stay.wait()
    for j, a in enumerate(ORDER):
        for b in range(GROUP):
            if a or b:
                spot = a * GROUP + b
                there = home.at[source(a, b)]
                send(there, there, d_send.at[spot], d_recv.at[spot], dp, source(a, b)).wait_recv()
        part = chunk(OWN, core, j)
        for way, side in ((0, RIGHT), (1, LEFT)):
            move = send(part, part, g_send.at[way, j], g_recv.at[way, j], chip[side] * 2 + core, ex)
            move.start()
            sent.append(move)
        to_sibling(OWN, j)

    cells = picked.shape[0] // 2
    tile = min(1024, hidden)
    wide = min(2048, width)
    slim = min(256, width)
    band = block // 4

    def up(which):
        for half, owner in ((0, core), (1, 1 - core)):
            picked[half * cells : (half + 1) * cells, :] = held[chip[which], owner].reshape(cells, width)

        @pl.loop(0, hidden // tile)
        def _(n):
            spot = pl.ds(pl.multiple_of(n * tile, tile), tile)
            part = jnp.dot(picked[...], first_v[:, spot], preferred_element_type=jnp.float32)
            inner[:, spot] = jnp.maximum(part, 0.0).astype(inner.dtype)

    def down(which):
        @pl.loop(0, width // wide)
        def _(n):
            spot = pl.ds(pl.multiple_of(n * wide, wide), wide)
            part = jnp.dot(inner[...], second_v[:, spot], preferred_element_type=jnp.float32)
            total[which, :, spot] = part[:cells]
            to_twin[which, :, spot] = part[cells:].astype(to_twin.dtype)

        move = send(to_twin.at[which], from_twin.at[which], y_send.at[which], y_recv.at[which], twin, ex)
        move.start()
        sent.append(move)

    def forward(which):
        there = from_twin.at[which]
        send(there, there, y_send.at[which], y_recv.at[which], twin, ex).wait_recv()

        @pl.loop(0, width // slim)
        def _(n):
            spot = pl.ds(pl.multiple_of(n * slim, slim), slim)
            both = total[which, :, spot] + from_twin[which, :, spot].astype(jnp.float32)
            to_chip[which - 1, :, spot] = both.astype(to_chip.dtype)

        if which == OPPOSITE:
            for q in (0, 2, 1, 3):
                rows = pl.ds(q * band, band)
                relay(to_chip.at[2, rows], far.at[rows], f_send.at[q], f_recv.at[q], RIGHT if q < 2 else LEFT)
        else:
            for q in (2, 3) if which == RIGHT else (0, 1):
                last_leg(which, q)

    def relay(src, dst, send_sem, recv_sem, side):
        move = send(src, dst, send_sem, recv_sem, chip[side] * 2 + core, ex)
        move.start()
        sent.append(move)

    def last_leg(which, q):
        rows = pl.ds(q * band, band)
        spot = which - 1
        relay(to_chip.at[spot, rows], from_chip.at[spot, rows], x_send.at[spot, q], x_recv.at[spot, q], which)

    def merge(q):
        rows = pl.ds(q * band, band)
        which = RIGHT if q < 2 else LEFT
        there = far.at[rows]
        send(there, there, f_send.at[q], f_recv.at[q], dp, ex).wait_recv()

        @pl.loop(0, width // slim)
        def _(n):
            spot = pl.ds(pl.multiple_of(n * slim, slim), slim)
            both = to_chip[which - 1, rows, spot].astype(jnp.float32) + far[rows, spot].astype(jnp.float32)
            to_chip[which - 1, rows, spot] = both.astype(to_chip.dtype)

        last_leg(which, q)

    def landed(way, j):
        side = LEFT if way == 0 else RIGHT
        part = chunk(side, core, j)
        send(part, part, g_send.at[way, j], g_recv.at[way, j], dp, ex).wait_recv()
        to_sibling(side, j)
        if (j < 2) == (way == 0):
            onward = RIGHT if way == 0 else LEFT
            move = send(part, part, o_send.at[j], o_recv.at[j], chip[onward] * 2 + core, ex)
            move.start()
            sent.append(move)

    for off in (1, 3, 2):
        begin = EARLY + MID if off != 2 else 0
        turn(off, begin, PAGE_CAP, 1)
    for load in loads[6:8]:
        load.wait()
    from_sibling(OWN)
    up(OWN)
    down(OWN)
    for j in range(4):
        landed(0, j)
        landed(1, j)
    from_sibling(LEFT)
    up(LEFT)
    down(LEFT)
    from_sibling(RIGHT)
    up(RIGHT)
    forward(LEFT)
    down(RIGHT)
    for j in range(4):
        part = chunk(OPPOSITE, core, j)
        send(part, part, o_send.at[j], o_recv.at[j], dp, ex).wait_recv()
        to_sibling(OPPOSITE, j)
    forward(RIGHT)
    from_sibling(OPPOSITE)
    up(OPPOSITE)
    down(OPPOSITE)
    forward(OPPOSITE)
    for q in (0, 2, 1, 3):
        merge(q)

    there = from_twin.at[OWN]
    send(there, there, y_send.at[OWN], y_recv.at[OWN], twin, ex).wait_recv()
    stay = pltpu.make_async_copy(result.at[ex], returned.at[ex], local.at[1])
    for q in (0, 2, 1, 3):
        rows = pl.ds(q * band, band)
        for spot in (0, 1):
            there = from_chip.at[spot, rows]
            send(there, there, x_send.at[spot, q], x_recv.at[spot, q], dp, ex).wait_recv()

        @pl.loop(0, width // slim)
        def _(n):
            spot = pl.ds(pl.multiple_of(n * slim, slim), slim)
            whole = total[OWN, rows, spot] + from_twin[OWN, rows, spot].astype(jnp.float32)
            for side in (0, 1):
                whole = whole + from_chip[side, rows, spot].astype(jnp.float32)
            packets = whole.astype(result.dtype).reshape(GROUP, cap, slim)
            result[q * GROUP : (q + 1) * GROUP, :, spot] = packets

        for target in range(q * GROUP, (q + 1) * GROUP):
            move = send(result.at[target], returned.at[ex], r_send.at[target], r_recv.at[ex], dp, target)
            pl.when(target != ex)(move.start)
            pl.when(target == ex)(stay.start)
    for origin in range(EXPERTS):
        there = returned.at[origin]
        move = send(there, there, r_send.at[origin], r_recv.at[origin], dp, origin)
        pl.when(origin != ex)(move.wait)
    stay.wait()
    back = returned[...].reshape(block, width)
    places = real(number((row_count, block), 1))
    final = hidden_v[...]
    for k in range(2):
        taken = real(places == slot[k]).astype(kind)
        final = final + upright(gates[k : k + 1, :]) * jnp.dot(taken, back, preferred_element_type=jnp.float32)
    mixed[...] = final.astype(mixed.dtype)
    for move in sent:
        move.wait_send()
    for move in paged:
        move.wait()


def layer(*operands):
    tokens, _, _, cache, memory, first, second = operands[7:]
    row_count, width = tokens.shape
    hidden = first.shape[-1]
    kind = tokens.dtype
    cap = 4 * row_count // EXPERTS
    block = EXPERTS * cap
    quarter = row_count // BEAM

    def room(*shape, dtype=kind):
        return pltpu.VMEM(shape, dtype)

    paged = (BEAM - 1, PAGE_CAP) + cache.shape[1:]
    scratch = [
        room(*cache.shape), room(*memory.shape), room(row_count, width), room(row_count, 2 * width),
        room(1, width, dtype=jnp.float32), room(row_count, width), room(8, HEAD, dtype=jnp.int32),
        room(BEAM, PAGE_CAP, width), room(BEAM, PAGE_CAP, width), room(BEAM, 8, HEAD, dtype=jnp.int32),
        room(BEAM, quarter, width), room(2 * BEAM * PAGE_CAP, row_count * cache.shape[1], dtype=jnp.float32),
        room(2 * BEAM * quarter, quarter * memory.shape[1], dtype=jnp.float32),
        room(BEAM, PAGE_CAP, width), room(BEAM, PAGE_CAP, HEAD, dtype=jnp.float32), room(BEAM, quarter, width),
        room(BEAM, PAGE_CAP, width), room(BEAM, PAGE_CAP, HEAD, dtype=jnp.float32), room(BEAM, quarter, width),
        room(row_count, width, dtype=jnp.float32), room(*paged), room(EXPERTS, cap, width), room(EXPERTS, cap, width),
        room(CHIPS, 2, EXPERTS, cap, width), room(*first.shape), room(*second.shape),
        room(2 * block, width), room(2 * block, hidden), room(4, block, width, dtype=jnp.float32),
        room(4, block, width), room(4, block, width), room(3, block, width), room(2, block, width),
        room(block, width), room(EXPERTS, cap, width),
    ]
    sems = [
        DMA((8,)), DMA((3,)), DMA((3,)), DMA((3,)), DMA((3,)), DMA((3,)), DMA((4,)), DMA((4,)),
        DMA((3,)), DMA((3,)), DMA((3,)), DMA((3,)), DMA((4,)), DMA((4,)),
        DMA((16,)), DMA((16,)), DMA((16,)), DMA((16,)),
        DMA((2, 4)), DMA((2, 4)), DMA((4,)), DMA((4,)), DMA((4, 4)), DMA((4, 4)),
        DMA((4,)), DMA((4,)), DMA((2, 4)), DMA((2, 4)), DMA((4,)), DMA((4,)), DMA((3, 3)), DMA((3, 3)),
    ]
    return pl.pallas_call(
        layer_kernel,
        out_shape=[jax.ShapeDtypeStruct((row_count, width), kind), jax.ShapeDtypeStruct(paged, kind)],
        in_specs=[ANY] * 2 + [pl.BlockSpec(memory_space=pltpu.VMEM)] * 5 + [ANY] * 7,
        out_specs=[pl.BlockSpec(memory_space=pltpu.VMEM), ANY],
        scratch_shapes=scratch + sems,
        compiler_params=pltpu.CompilerParams(
            collective_id=0, has_side_effects=True, vmem_limit_bytes=58 * 2**20
        ),
        name="layer",
    )(*operands)


def per_device(
    tokens,
    self_query,
    new_kv,
    kv_cache,
    parents,
    dec_len,
    cross_query,
    memory,
    src_len,
    norm_gain,
    routes,
    gate_weights,
    expert_in,
    expert_out,
):
    row_count, model_width = tokens.shape
    mixed, arrived = layer(
        self_query,
        cross_query.reshape(GROUP, row_count // BEAM, model_width),
        parents[None],
        dec_len[None],
        src_len[None],
        routes.T,
        gate_weights.T,
        tokens,
        new_kv,
        norm_gain[None],
        kv_cache,
        memory,
        expert_in[0],
        expert_out[0],
    )
    return (mixed, unpack(parents, kv_cache, arrived))


def solution(mesh):
    placed = (
        P(("dp", "expert"), None),
        P(("dp", "expert"), None),
        P(("dp", "expert"), None),
        P(("dp", "expert"), None, None),
        P(("dp", "expert")),
        P("dp"),
        P(("dp", "expert"), None),
        P(("dp", "expert"), None, None),
        P(("dp", "expert")),
        P(),
        P(("dp", "expert"), None),
        P(("dp", "expert"), None),
        P("expert", None, "dp"),
        P("expert", "dp", None),
    )
    return jax.shard_map(
        per_device,
        mesh=mesh,
        in_specs=placed,
        out_specs=(P(("dp", "expert"), None), P(("dp", "expert"), None, None)),
        check_vma=False,
    )
```

```python
import functools
import math

import jax
import jax.numpy as jnp
from jax import lax
from jax.experimental import pallas as pl
from jax.experimental.pallas import tpu as pltpu
from jax.sharding import PartitionSpec as P

HEAD = 128
BEAM = 4
GROUP = 4
CHIPS = 4
EXPERTS = 16
PAGE_CAP = 16
MESH = pl.DeviceIdType.MESH
ANY = pl.BlockSpec(memory_space=pl.ANY)
DMA = pltpu.SemaphoreType.DMA


def place():
    dp = lax.axis_index("dp")
    ex = lax.axis_index("expert")
    return dp, ex, lax.div(ex, GROUP), lax.rem(ex, GROUP)


def send(src, dst, send_sem, recv_sem, dp, ex):
    return pltpu.make_async_remote_copy(
        src_ref=src,
        dst_ref=dst,
        send_sem=send_sem,
        recv_sem=recv_sem,
        device_id=(dp, ex),
        device_id_type=MESH,
    )


def greet(barrier, dp, ex):
    pl.semaphore_signal(barrier, inc=1, device_id=(dp, ex), device_id_type=MESH)


def unpack_kernel(parents, cache, arrived, rows_in, fresh, rows_out, buffer, rows_v, got, put, row_sem):
    _, _, z, _ = place()
    rows = cache.shape[0]
    part = rows // got.shape[0]
    take_in = pltpu.make_async_copy(rows_in, rows_v, row_sem.at[0])
    take_in.start()

    def begin(row, counts):
        parent = parents[row]
        off = lax.rem(z - parent + BEAM, BEAM)
        sem = got.at[lax.div(row, part)]

        def keep():
            pltpu.make_async_copy(cache.at[row], buffer.at[row], sem).start()

        pl.when(off == 0)(keep)
        after = []
        for step in range(1, BEAM):
            hit = off == step

            def take(step=step):
                pltpu.make_async_copy(arrived.at[step - 1, counts[step - 1]], buffer.at[row], sem).start()

            pl.when(hit)(take)
            after.append(counts[step - 1] + hit.astype(jnp.int32))
        return tuple(after)

    lax.fori_loop(0, rows, begin, (jnp.int32(0),) * (BEAM - 1))
    take_in.wait()
    give = pltpu.make_async_copy(rows_v, rows_out, row_sem.at[1])
    give.start()
    puts = []
    for n in range(got.shape[0]):
        piece = pl.ds(n * part, part)
        pltpu.make_async_copy(cache.at[piece], buffer.at[piece], got.at[n]).wait()
        puts.append(pltpu.make_async_copy(buffer.at[piece], fresh.at[piece], put.at[n]))
        puts[-1].start()
    for move in puts:
        move.wait()
    give.wait()


def unpack(parents, cache, arrived, rows):
    return pl.pallas_call(
        unpack_kernel,
        out_shape=[jax.ShapeDtypeStruct(cache.shape, cache.dtype), jax.ShapeDtypeStruct(rows.shape, rows.dtype)],
        in_specs=[pl.BlockSpec(memory_space=pltpu.SMEM), ANY, ANY, ANY],
        out_specs=[ANY, ANY],
        scratch_shapes=[
            pltpu.VMEM(cache.shape, cache.dtype), pltpu.VMEM(rows.shape, rows.dtype),
            DMA((4,)), DMA((4,)), DMA((2,)),
        ],
        compiler_params=pltpu.CompilerParams(vmem_limit_bytes=58 * 2**20),
        name="unpack",
    )(parents, cache, arrived, rows)


ORDER = (0, 1, 3, 2)
OWN, LEFT, RIGHT, OPPOSITE = range(4)
EARLY = 4
MID = 4


def eye(n):
    shape = (n, n)
    return lax.broadcasted_iota(jnp.int32, shape, 0) == lax.broadcasted_iota(jnp.int32, shape, 1)


def upright(row):
    return jnp.sum(jnp.where(eye(row.shape[1]), row, 0.0), 1, keepdims=True)


def flat(column):
    return jnp.sum(jnp.where(eye(column.shape[0]), column, 0.0), 0, keepdims=True)


def spread(column, times):
    shape = (column.shape[0], column.shape[0] * times)
    owner = lax.div(lax.broadcasted_iota(jnp.int32, shape, 1), times)
    return jnp.sum(jnp.where(owner == lax.broadcasted_iota(jnp.int32, shape, 0), column, 0.0), 0, keepdims=True)


def rank(column, rows):
    shape = (column.shape[0], rows[0].shape[1])
    earlier = lax.broadcasted_iota(jnp.int32, shape, 1) < lax.broadcasted_iota(jnp.int32, shape, 0)
    alike = functools.reduce(jnp.logical_or, [column == row for row in rows])
    return jnp.sum(jnp.where(earlier & alike, 1.0, 0.0), 1, keepdims=True)


def number(shape, axis):
    return lax.broadcasted_iota(jnp.int32, shape, axis)


def real(values):
    return values.astype(jnp.float32)


def layer_kernel(
    query, cross, parents, dec_len, src_len, routes, gates, tokens, new_kv, gain, cache, memory, first, second,
    mixed, arrived,
    cache_v, memory_v, tokens_v, new_kv_v, gain_v, query_v, wish, packed, queries, wishes, crosses, bias, bias_c,
    outs, stats, owner_out, got, got_stats, cross_out, hidden_v, pages, slots, returned,
    held, first_v, second_v, picked, inner, total, to_twin, from_twin, to_chip, from_chip, far, result,
    l_sem, local, k_send, k_recv, n_send, n_recv, e_send, e_recv, b_send, b_recv, s_send, s_recv, c_send, c_recv,
    d_send, d_recv, r_send, r_recv,
    g_send, g_recv, o_send, o_recv, t_send, t_recv,
    y_send, y_recv, x_send, x_recv, f_send, f_recv, p_send, p_recv,
):
    dp, ex, z, y = place()
    x, core = lax.div(dp, 2), lax.rem(dp, 2)
    twin = x * 2 + 1 - core
    chip = [x, lax.rem(x + CHIPS - 1, CHIPS), lax.rem(x + 1, CHIPS), lax.rem(x + 2, CHIPS)]
    row_count, width = tokens.shape
    hidden = first.shape[-1]
    kind = tokens.dtype
    heads = width // HEAD
    span = cache.shape[1]
    quarter, reach = memory.shape[:2]
    cap = slots.shape[1]
    block = EXPERTS * cap
    scale = 1.0 / math.sqrt(HEAD)

    barrier = pltpu.get_barrier_semaphore()
    for a in range(BEAM):
        for b in range(GROUP):
            if a or b:
                greet(barrier, dp, lax.rem(z + a, BEAM) * GROUP + lax.rem(y + b, GROUP))
    greet(barrier, twin, ex)
    for side in (LEFT, RIGHT, OPPOSITE):
        greet(barrier, chip[side] * 2 + core, ex)
    pairs = (
        (query, query_v), (new_kv, new_kv_v), (cache, cache_v), (memory, memory_v),
        (tokens, tokens_v), (gain, gain_v), (first, first_v), (second, second_v),
    )
    loads = [pltpu.make_async_copy(a, b, l_sem.at[i]) for i, (a, b) in enumerate(pairs)]
    for i in (0, 3, 1, 2, 4, 5, 6, 7):
        loads[i].start()
    own_cross = pltpu.make_async_copy(cross.at[y], crosses.at[z], local.at[2])
    pl.when(z == y)(own_cross.start)

    parent_row = real(parents[...])
    parent = upright(parent_row)
    parent_rank = rank(parent, [parent_row])
    rank_row = flat(parent_rank)
    ticket = number((BEAM * PAGE_CAP, row_count), 0)
    chosen = (real(lax.div(ticket, PAGE_CAP)) == parent_row) & (real(lax.rem(ticket, PAGE_CAP)) == rank_row)
    chosen = real(chosen).astype(kind)
    wish[0:1, :row_count] = parents[...]
    loads[0].wait()
    lines = jnp.dot(chosen, query_v[...], preferred_element_type=jnp.float32).astype(kind)
    packed[...] = lines.reshape(packed.shape)
    pl.semaphore_wait(barrier, EXPERTS - 1 + 4)

    sent = []
    crossing = [
        send(cross.at[p], crosses.at[z], e_send.at[p], e_recv.at[z], dp, y * GROUP + p) for p in range(GROUP)
    ]
    for p in range(GROUP):
        pl.when(y * GROUP + p != ex)(crossing[p].start)
    asks = []
    for off in (1, 3, 2):
        other = lax.rem(z + off, BEAM)
        target = other * GROUP + y
        asks.append(send(wish, wishes.at[z], n_send.at[off - 1], n_recv.at[off - 1], dp, target))
        asks.append(send(packed.at[other], queries.at[z], k_send.at[off - 1], k_recv.at[off - 1], dp, target))
    for move in asks:
        move.start()
    queries[z] = packed[z]
    wishes[z] = wish[...]

    loads[1].wait()
    lane = number((row_count, HEAD), 1)
    own = jnp.zeros((row_count, HEAD), jnp.float32)
    for h in range(heads):
        spot = slice(h * HEAD, (h + 1) * HEAD)
        both = real(query_v[:, spot]) * real(new_kv_v[:, spot])
        own = own + jnp.where(lane == h, jnp.sum(both, -1, keepdims=True) * scale, 0.0)
    named_rows = [real(routes[k : k + 1, :]) for k in range(2)]
    named = [upright(row) for row in named_rows]
    slot = [column * float(cap) + rank(column, named_rows) for column in named]
    slot_rows = [flat(column) for column in slot]

    at = number((row_count, dec_len.shape[1]), 1) - y * row_count == number((row_count, dec_len.shape[1]), 0)
    lengths = jnp.sum(jnp.where(at, real(dec_len[...]), 0.0), 1, keepdims=True)
    keys = row_count * span
    in_reach = real(lax.rem(number((1, keys), 1), span)) < spread(lengths, span)
    keys_c = quarter * reach
    in_reach_c = real(lax.rem(number((1, keys_c), 1), reach)) < spread(upright(real(src_len[...])), reach)
    asked_c = BEAM * quarter
    same_c = lax.rem(number((asked_c, keys_c), 0), quarter) == lax.div(number((asked_c, keys_c), 1), reach)
    for half in range(2):
        bias_c[half * asked_c : (half + 1) * asked_c, :] = jnp.where(same_c & in_reach_c, 0.0, -1e30)

    pair = 2 * HEAD
    batch = math.gcd(heads // 2, 8)

    def attend(asker, keeper, extra, base):
        blank = jnp.zeros((asker.shape[0], HEAD), kind)
        both = jnp.concatenate(
            [
                jnp.concatenate([asker[:, :HEAD], blank], 1),
                jnp.concatenate([blank, asker[:, HEAD:]], 1),
            ],
            0,
        )
        keys_of = keeper(base)
        scores = lax.dot_general(both, keys_of, (((1,), (1,)), ((), ())), preferred_element_type=jnp.float32)
        scores = scores * scale + extra[...]
        peak = jnp.max(scores, -1, keepdims=True)
        terms = jnp.exp(scores - peak)
        mass = jnp.sum(terms, -1, keepdims=True)
        part = jnp.dot((terms / mass).astype(kind), keeper(width + base), preferred_element_type=jnp.float32)
        return part.astype(kind), peak + jnp.log(mass)

    for p in range(GROUP):
        pl.when(y * GROUP + p != ex)(crossing[p].wait_send)
    for beam in range(BEAM):
        coming = send(cross.at[0], crosses.at[beam], e_send.at[0], e_recv.at[beam], dp, beam * GROUP + z)
        pl.when(beam * GROUP + z != ex)(coming.wait_recv)
    pl.when(z == y)(own_cross.wait)
    loads[3].wait()

    @pl.loop(0, heads // 2 // batch)
    def _(n):
        for m in range(batch):
            base = (n * batch + m) * pair
            spot = pl.ds(pl.multiple_of(base, pair), pair)

            def keeper(start):
                return memory_v[:, :, pl.ds(pl.multiple_of(start, pair), pair)].reshape(keys_c, pair)

            part, _ = attend(crosses[:, :, spot].reshape(asked_c, pair), keeper, bias_c, base)
            for half in range(2):
                piece = part[half * asked_c : (half + 1) * asked_c, half * HEAD : (half + 1) * HEAD]
                place_at = pl.ds(pl.multiple_of(base + half * HEAD, HEAD), HEAD)
                owner_out[:, :, place_at] = piece.reshape(BEAM, quarter, HEAD)

    own_back = pltpu.make_async_copy(owner_out.at[z], cross_out.at[y], local.at[2])
    crossing = [
        send(owner_out.at[beam], cross_out.at[y], c_send.at[beam], c_recv.at[y], dp, beam * GROUP + z)
        for beam in range(BEAM)
    ]
    for beam in range(BEAM):
        pl.when(beam * GROUP + z != ex)(crossing[beam].start)
    pl.when(z == y)(own_back.start)

    loads[2].wait()
    for move in asks:
        move.wait()
    asked = BEAM * PAGE_CAP
    ticket = real(number((PAGE_CAP, keys), 0))
    codes = []
    for beam in range(BEAM):
        wanted_row = real(wishes[beam, 0:1, :row_count])
        wanted = upright(wanted_row)
        code = spread(jnp.where(wanted == real(z), rank(wanted, [wanted_row]), -1.0), span)
        codes.append(code)
        part = jnp.where((ticket == code) & in_reach, 0.0, -1e30)
        for half in range(2):
            first_row = half * asked + beam * PAGE_CAP
            bias[first_row : first_row + PAGE_CAP, :] = part
    stats[...] = jnp.zeros_like(stats)
    stat_lane = number((asked, HEAD), 1)

    @pl.loop(0, heads // 2 // batch)
    def _(n):
        for m in range(batch):
            base = (n * batch + m) * pair
            spot = pl.ds(pl.multiple_of(base, pair), pair)

            def keeper(start):
                return cache_v[:, :, pl.ds(pl.multiple_of(start, pair), pair)].reshape(keys, pair)

            part, level = attend(queries[:, :, spot].reshape(asked, pair), keeper, bias, base)
            levels = jnp.zeros((asked, HEAD), jnp.float32)
            for half in range(2):
                rows = slice(half * asked, (half + 1) * asked)
                piece = part[rows, half * HEAD : (half + 1) * HEAD].reshape(BEAM, PAGE_CAP, HEAD)
                outs[:, :, pl.ds(pl.multiple_of(base + half * HEAD, HEAD), HEAD)] = piece
                levels = jnp.where(stat_lane == 2 * (n * batch + m) + half, level[rows], levels)
            stats[...] += levels.reshape(BEAM, PAGE_CAP, HEAD)

    answers = []
    for off in (1, 3, 2):
        other = lax.rem(z + off, BEAM)
        target = other * GROUP + y
        answers.append(send(stats.at[other], got_stats.at[z], b_send.at[off - 1], b_recv.at[off - 1], dp, target))
        answers.append(send(outs.at[other], got.at[z], s_send.at[off - 1], s_recv.at[off - 1], dp, target))
    for move in answers:
        move.start()
    got[z] = outs[z]
    got_stats[z] = stats[z]

    paged = []

    def turn(off, start, stop, which):
        rows = pl.ds(start, stop - start)
        move = send(
            pages.at[off - 1, rows], arrived.at[off - 1, rows], p_send.at[off - 1, which], p_recv.at[off - 1, which],
            dp, lax.rem(z + off, BEAM) * GROUP + y,
        )
        move.start()
        paged.append(move)

    page_shape = (PAGE_CAP * span, keys)
    page_row, page_lane = number(page_shape, 0), number(page_shape, 1)
    page_slot = real(lax.div(page_row, span))
    same_place = lax.rem(page_row, span) == lax.rem(page_lane, span)
    strip = min(1024, 2 * width)
    for off in (1, 3, 2):
        asker = lax.rem(z + off, BEAM)
        code = jnp.zeros_like(codes[0])
        for beam in range(BEAM):
            code = code + jnp.where(real(asker) == float(beam), codes[beam], 0.0)
        pick = real(same_place & (page_slot == code)).astype(kind)

        @pl.loop(0, 2 * width // strip)
        def _(n):
            spot = pl.ds(pl.multiple_of(n * strip, strip), strip)
            part = jnp.dot(pick, cache_v[:, :, spot].reshape(keys, strip), preferred_element_type=jnp.float32)
            pages[off - 1, :, :, spot] = part.astype(kind).reshape(PAGE_CAP, span, strip)

        if off != 2 and EARLY:
            turn(off, 0, EARLY, 0)

    for load in loads[4:6]:
        load.wait()
    for move in answers:
        move.wait()
    for beam in range(BEAM):
        pl.when(beam * GROUP + z != ex)(crossing[beam].wait_send)
    for p in range(GROUP):
        coming = send(owner_out.at[0], cross_out.at[p], c_send.at[0], c_recv.at[p], dp, y * GROUP + p)
        pl.when(y * GROUP + p != ex)(coming.wait_recv)
    pl.when(z == y)(own_back.wait)

    ticket = number((row_count, asked), 1)
    chosen = (parent == real(lax.div(ticket, PAGE_CAP))) & (parent_rank == real(lax.rem(ticket, PAGE_CAP)))
    chosen = real(chosen)
    level = jnp.dot(
        chosen,
        got_stats[...].reshape(asked, HEAD),
        precision=lax.Precision.HIGHEST,
        preferred_element_type=jnp.float32,
    )
    cached = jnp.dot(chosen.astype(kind), got[...].reshape(asked, width), preferred_element_type=jnp.float32)
    top = jnp.maximum(level, own)
    cache_part = jnp.exp(level - top)
    own_part = jnp.exp(own - top)
    cache_share = cache_part / (cache_part + own_part)
    own_share = own_part / (cache_part + own_part)
    for h in range(heads):
        spot = slice(h * HEAD, (h + 1) * HEAD)
        own_value = real(new_kv_v[:, width + h * HEAD : width + (h + 1) * HEAD])
        mine = cache_share[:, h : h + 1] * cached[:, spot] + own_share[:, h : h + 1] * own_value
        crossed = real(cross_out[:, :, spot].reshape(row_count, HEAD))
        hidden_v[:, spot] = real(tokens_v[:, spot]) + mine + crossed
    whole = hidden_v[...]
    centered = whole - jnp.mean(whole, -1, keepdims=True)
    variance = jnp.mean(centered * centered, -1, keepdims=True)
    moe_in = (centered * lax.rsqrt(variance + 1e-05) * gain_v[...]).astype(kind)
    slot_row = real(number((block, row_count), 0))
    table = real((slot_row == slot_rows[0]) | (slot_row == slot_rows[1])).astype(kind)
    packets = jnp.dot(table, moe_in, preferred_element_type=jnp.float32).astype(kind)
    slots[...] = packets.reshape(slots.shape)

    def peer(a, b):
        return lax.rem(z + a, BEAM) * GROUP + lax.rem(y + b, GROUP)

    def source(a, b):
        return lax.rem(z + BEAM - a, BEAM) * GROUP + lax.rem(y + GROUP - b, GROUP)

    home = held.at[x, core]
    stay = pltpu.make_async_copy(slots.at[ex], home.at[ex], local.at[0])
    stay.start()
    for a in ORDER:
        for b in range(GROUP):
            if a or b:
                spot = a * GROUP + b
                move = send(slots.at[peer(a, b)], home.at[ex], d_send.at[spot], d_recv.at[spot], dp, peer(a, b))
                move.start()
                sent.append(move)

    if MID:
        for off in (1, 3):
            turn(off, EARLY, EARLY + MID, 2)

    def chunk(which, owner, j):
        zz = lax.rem(z + BEAM - ORDER[j], BEAM)
        return held.at[chip[which], owner, pl.ds(zz * GROUP, GROUP)]

    def to_sibling(which, j):
        part = chunk(which, core, j)
        move = send(part, part, t_send.at[which, j], t_recv.at[which, j], twin, ex)
        move.start()
        sent.append(move)

    def from_sibling(which):
        for j in range(4):
            part = chunk(which, 1 - core, j)
            send(part, part, t_send.at[which, j], t_recv.at[which, j], twin, ex).wait_recv()

    stay.wait()
    for j, a in enumerate(ORDER):
        for b in range(GROUP):
            if a or b:
                spot = a * GROUP + b
                there = home.at[source(a, b)]
                send(there, there, d_send.at[spot], d_recv.at[spot], dp, source(a, b)).wait_recv()
        part = chunk(OWN, core, j)
        for way, side in ((0, RIGHT), (1, LEFT)):
            move = send(part, part, g_send.at[way, j], g_recv.at[way, j], chip[side] * 2 + core, ex)
            move.start()
            sent.append(move)
        to_sibling(OWN, j)

    cells = picked.shape[0] // 2
    tile = min(1024, hidden)
    wide = min(2048, width)
    slim = min(1024, width)
    band = block // 4

    def up(which):
        for half, owner in ((0, core), (1, 1 - core)):
            picked[half * cells : (half + 1) * cells, :] = held[chip[which], owner].reshape(cells, width)

        @pl.loop(0, hidden // tile)
        def _(n):
            spot = pl.ds(pl.multiple_of(n * tile, tile), tile)
            part = jnp.dot(picked[...], first_v[:, spot], preferred_element_type=jnp.float32)
            inner[:, spot] = jnp.maximum(part, 0.0).astype(inner.dtype)

    def down(which):
        @pl.loop(0, width // wide)
        def _(n):
            spot = pl.ds(pl.multiple_of(n * wide, wide), wide)
            part = jnp.dot(inner[...], second_v[:, spot], preferred_element_type=jnp.float32)
            total[which, :, spot] = part[:cells]
            to_twin[which, :, spot] = part[cells:].astype(to_twin.dtype)

        move = send(to_twin.at[which], from_twin.at[which], y_send.at[which], y_recv.at[which], twin, ex)
        move.start()
        sent.append(move)

    def forward(which):
        there = from_twin.at[which]
        send(there, there, y_send.at[which], y_recv.at[which], twin, ex).wait_recv()

        @pl.loop(0, width // slim)
        def _(n):
            spot = pl.ds(pl.multiple_of(n * slim, slim), slim)
            both = total[which, :, spot] + from_twin[which, :, spot].astype(jnp.float32)
            to_chip[which - 1, :, spot] = both.astype(to_chip.dtype)

        if which == OPPOSITE:
            far_leg(0)
            far_leg(2)
        else:
            for q in (2, 3) if which == RIGHT else (0, 1):
                last_leg(which, q)

    def relay(src, dst, send_sem, recv_sem, side):
        move = send(src, dst, send_sem, recv_sem, chip[side] * 2 + core, ex)
        move.start()
        sent.append(move)

    def far_leg(q):
        rows = pl.ds(q * band, band)
        relay(to_chip.at[2, rows], far.at[rows], f_send.at[q], f_recv.at[q], RIGHT if q < 2 else LEFT)

    def last_leg(which, q):
        rows = pl.ds(q * band, band)
        spot = which - 1
        relay(to_chip.at[spot, rows], from_chip.at[spot, rows], x_send.at[spot, q], x_recv.at[spot, q], which)

    def merge(q):
        rows = pl.ds(q * band, band)
        which = RIGHT if q < 2 else LEFT
        there = far.at[rows]
        send(there, there, f_send.at[q], f_recv.at[q], dp, ex).wait_recv()
        if q in (0, 2):
            far_leg(q + 1)

        @pl.loop(0, width // slim)
        def _(n):
            spot = pl.ds(pl.multiple_of(n * slim, slim), slim)
            both = to_chip[which - 1, rows, spot].astype(jnp.float32) + far[rows, spot].astype(jnp.float32)
            to_chip[which - 1, rows, spot] = both.astype(to_chip.dtype)

        last_leg(which, q)

    def landed(way, j):
        side = LEFT if way == 0 else RIGHT
        part = chunk(side, core, j)
        send(part, part, g_send.at[way, j], g_recv.at[way, j], dp, ex).wait_recv()
        to_sibling(side, j)
        if (j < 2) == (way == 0):
            onward = RIGHT if way == 0 else LEFT
            move = send(part, part, o_send.at[j], o_recv.at[j], chip[onward] * 2 + core, ex)
            move.start()
            sent.append(move)

    for off in (1, 3, 2):
        begin = EARLY + MID if off != 2 else 0
        turn(off, begin, PAGE_CAP, 1)
    for load in loads[6:8]:
        load.wait()
    from_sibling(OWN)
    up(OWN)
    down(OWN)
    for j in range(4):
        landed(0, j)
        landed(1, j)
    from_sibling(LEFT)
    up(LEFT)
    down(LEFT)
    from_sibling(RIGHT)
    up(RIGHT)
    forward(LEFT)
    down(RIGHT)
    for j in range(4):
        part = chunk(OPPOSITE, core, j)
        send(part, part, o_send.at[j], o_recv.at[j], dp, ex).wait_recv()
        to_sibling(OPPOSITE, j)
    forward(RIGHT)
    from_sibling(OPPOSITE)
    up(OPPOSITE)
    down(OPPOSITE)
    forward(OPPOSITE)
    for q in (0, 2, 1, 3):
        merge(q)

    there = from_twin.at[OWN]
    send(there, there, y_send.at[OWN], y_recv.at[OWN], twin, ex).wait_recv()
    stay = pltpu.make_async_copy(result.at[ex], returned.at[ex], local.at[1])
    for q in (0, 2, 1, 3):
        rows = pl.ds(q * band, band)
        for spot in (0, 1):
            there = from_chip.at[spot, rows]
            send(there, there, x_send.at[spot, q], x_recv.at[spot, q], dp, ex).wait_recv()

        @pl.loop(0, width // slim)
        def _(n):
            spot = pl.ds(pl.multiple_of(n * slim, slim), slim)
            whole = total[OWN, rows, spot] + from_twin[OWN, rows, spot].astype(jnp.float32)
            for side in (0, 1):
                whole = whole + from_chip[side, rows, spot].astype(jnp.float32)
            packets = whole.astype(result.dtype).reshape(GROUP, cap, slim)
            result[q * GROUP : (q + 1) * GROUP, :, spot] = packets

        for target in range(q * GROUP, (q + 1) * GROUP):
            move = send(result.at[target], returned.at[ex], r_send.at[target], r_recv.at[ex], dp, target)
            pl.when(target != ex)(move.start)
            pl.when(target == ex)(stay.start)
    for origin in range(EXPERTS):
        there = returned.at[origin]
        move = send(there, there, r_send.at[origin], r_recv.at[origin], dp, origin)
        pl.when(origin != ex)(move.wait)
    stay.wait()
    back = returned[...].reshape(block, width)
    places = real(number((row_count, block), 1))
    final = hidden_v[...]
    for k in range(2):
        taken = real(places == slot[k]).astype(kind)
        final = final + upright(gates[k : k + 1, :]) * jnp.dot(taken, back, preferred_element_type=jnp.float32)
    mixed[...] = final.astype(mixed.dtype)
    for move in sent:
        move.wait_send()
    for move in paged:
        move.wait()


def layer(*operands):
    tokens, _, _, cache, memory, first, second = operands[7:]
    row_count, width = tokens.shape
    hidden = first.shape[-1]
    kind = tokens.dtype
    cap = 4 * row_count // EXPERTS
    block = EXPERTS * cap
    quarter = row_count // BEAM

    def room(*shape, dtype=kind):
        return pltpu.VMEM(shape, dtype)

    paged = (BEAM - 1, PAGE_CAP) + cache.shape[1:]
    scratch = [
        room(*cache.shape), room(*memory.shape), room(row_count, width), room(row_count, 2 * width),
        room(1, width, dtype=jnp.float32), room(row_count, width), room(8, HEAD, dtype=jnp.int32),
        room(BEAM, PAGE_CAP, width), room(BEAM, PAGE_CAP, width), room(BEAM, 8, HEAD, dtype=jnp.int32),
        room(BEAM, quarter, width), room(2 * BEAM * PAGE_CAP, row_count * cache.shape[1], dtype=jnp.float32),
        room(2 * BEAM * quarter, quarter * memory.shape[1], dtype=jnp.float32),
        room(BEAM, PAGE_CAP, width), room(BEAM, PAGE_CAP, HEAD, dtype=jnp.float32), room(BEAM, quarter, width),
        room(BEAM, PAGE_CAP, width), room(BEAM, PAGE_CAP, HEAD, dtype=jnp.float32), room(BEAM, quarter, width),
        room(row_count, width, dtype=jnp.float32), room(*paged), room(EXPERTS, cap, width), room(EXPERTS, cap, width),
        room(CHIPS, 2, EXPERTS, cap, width), room(*first.shape), room(*second.shape),
        room(2 * block, width), room(2 * block, hidden), room(4, block, width, dtype=jnp.float32),
        room(4, block, width), room(4, block, width), room(3, block, width), room(2, block, width),
        room(block, width), room(EXPERTS, cap, width),
    ]
    sems = [
        DMA((8,)), DMA((3,)), DMA((3,)), DMA((3,)), DMA((3,)), DMA((3,)), DMA((4,)), DMA((4,)),
        DMA((3,)), DMA((3,)), DMA((3,)), DMA((3,)), DMA((4,)), DMA((4,)),
        DMA((16,)), DMA((16,)), DMA((16,)), DMA((16,)),
        DMA((2, 4)), DMA((2, 4)), DMA((4,)), DMA((4,)), DMA((4, 4)), DMA((4, 4)),
        DMA((4,)), DMA((4,)), DMA((2, 4)), DMA((2, 4)), DMA((4,)), DMA((4,)), DMA((3, 3)), DMA((3, 3)),
    ]
    return pl.pallas_call(
        layer_kernel,
        out_shape=[jax.ShapeDtypeStruct((row_count, width), kind), jax.ShapeDtypeStruct(paged, kind)],
        in_specs=[ANY] * 2 + [pl.BlockSpec(memory_space=pltpu.VMEM)] * 5 + [ANY] * 7,
        out_specs=[pl.BlockSpec(memory_space=pltpu.VMEM), ANY],
        scratch_shapes=scratch + sems,
        compiler_params=pltpu.CompilerParams(
            collective_id=0, has_side_effects=True, vmem_limit_bytes=58 * 2**20
        ),
        name="layer",
    )(*operands)


def per_device(
    tokens,
    self_query,
    new_kv,
    kv_cache,
    parents,
    dec_len,
    cross_query,
    memory,
    src_len,
    norm_gain,
    routes,
    gate_weights,
    expert_in,
    expert_out,
):
    row_count, model_width = tokens.shape
    mixed, arrived = layer(
        self_query,
        cross_query.reshape(GROUP, row_count // BEAM, model_width),
        parents[None],
        dec_len[None],
        src_len[None],
        routes.T,
        gate_weights.T,
        tokens,
        new_kv,
        norm_gain[None],
        kv_cache,
        memory,
        expert_in[0],
        expert_out[0],
    )
    fresh, mixed = unpack(parents, kv_cache, arrived, mixed)
    return (mixed, fresh)


def solution(mesh):
    placed = (
        P(("dp", "expert"), None),
        P(("dp", "expert"), None),
        P(("dp", "expert"), None),
        P(("dp", "expert"), None, None),
        P(("dp", "expert")),
        P("dp"),
        P(("dp", "expert"), None),
        P(("dp", "expert"), None, None),
        P(("dp", "expert")),
        P(),
        P(("dp", "expert"), None),
        P(("dp", "expert"), None),
        P("expert", None, "dp"),
        P("expert", "dp", None),
    )
    return jax.shard_map(
        per_device,
        mesh=mesh,
        in_specs=placed,
        out_specs=(P(("dp", "expert"), None), P(("dp", "expert"), None, None)),
        check_vma=False,
    )
```

```python
import functools
import math

import jax
import jax.numpy as jnp
from jax import lax
from jax.experimental import pallas as pl
from jax.experimental.pallas import tpu as pltpu
from jax.sharding import PartitionSpec as P

HEAD = 128
BEAM = 4
GROUP = 4
CHIPS = 4
EXPERTS = 16
PAGE_CAP = 16
MESH = pl.DeviceIdType.MESH
ANY = pl.BlockSpec(memory_space=pl.ANY)
DMA = pltpu.SemaphoreType.DMA


def place():
    dp = lax.axis_index("dp")
    ex = lax.axis_index("expert")
    return dp, ex, lax.div(ex, GROUP), lax.rem(ex, GROUP)


def send(src, dst, send_sem, recv_sem, dp, ex):
    return pltpu.make_async_remote_copy(
        src_ref=src,
        dst_ref=dst,
        send_sem=send_sem,
        recv_sem=recv_sem,
        device_id=(dp, ex),
        device_id_type=MESH,
    )


def greet(barrier, dp, ex):
    pl.semaphore_signal(barrier, inc=1, device_id=(dp, ex), device_id_type=MESH)


def unpack_kernel(parents, cache, arrived, rows_in, fresh, rows_out, buffer, rows_v, got, put, row_sem):
    _, _, z, _ = place()
    rows = cache.shape[0]
    part = rows // got.shape[0]
    take_in = pltpu.make_async_copy(rows_in, rows_v, row_sem.at[0])
    take_in.start()

    def begin(row, counts):
        parent = parents[row]
        off = lax.rem(z - parent + BEAM, BEAM)
        sem = got.at[lax.div(row, part)]

        def keep():
            pltpu.make_async_copy(cache.at[row], buffer.at[row], sem).start()

        pl.when(off == 0)(keep)
        after = []
        for step in range(1, BEAM):
            hit = off == step

            def take(step=step):
                pltpu.make_async_copy(arrived.at[step - 1, counts[step - 1]], buffer.at[row], sem).start()

            pl.when(hit)(take)
            after.append(counts[step - 1] + hit.astype(jnp.int32))
        return tuple(after)

    lax.fori_loop(0, rows, begin, (jnp.int32(0),) * (BEAM - 1))
    take_in.wait()
    give = pltpu.make_async_copy(rows_v, rows_out, row_sem.at[1])
    give.start()
    puts = []
    for n in range(got.shape[0]):
        piece = pl.ds(n * part, part)
        pltpu.make_async_copy(cache.at[piece], buffer.at[piece], got.at[n]).wait()
        puts.append(pltpu.make_async_copy(buffer.at[piece], fresh.at[piece], put.at[n]))
        puts[-1].start()
    for move in puts:
        move.wait()
    give.wait()


def unpack(parents, cache, arrived, rows):
    return pl.pallas_call(
        unpack_kernel,
        out_shape=[jax.ShapeDtypeStruct(cache.shape, cache.dtype), jax.ShapeDtypeStruct(rows.shape, rows.dtype)],
        in_specs=[pl.BlockSpec(memory_space=pltpu.SMEM), ANY, ANY, ANY],
        out_specs=[ANY, ANY],
        scratch_shapes=[
            pltpu.VMEM(cache.shape, cache.dtype), pltpu.VMEM(rows.shape, rows.dtype),
            DMA((4,)), DMA((4,)), DMA((2,)),
        ],
        compiler_params=pltpu.CompilerParams(vmem_limit_bytes=58 * 2**20),
        name="unpack",
    )(parents, cache, arrived, rows)


ORDER = (0, 1, 3, 2)
OWN, LEFT, RIGHT, OPPOSITE = range(4)
EARLY = 4
MID = 4


def eye(n):
    shape = (n, n)
    return lax.broadcasted_iota(jnp.int32, shape, 0) == lax.broadcasted_iota(jnp.int32, shape, 1)


def upright(row):
    return jnp.sum(jnp.where(eye(row.shape[1]), row, 0.0), 1, keepdims=True)


def flat(column):
    return jnp.sum(jnp.where(eye(column.shape[0]), column, 0.0), 0, keepdims=True)


def spread(column, times):
    shape = (column.shape[0], column.shape[0] * times)
    owner = lax.div(lax.broadcasted_iota(jnp.int32, shape, 1), times)
    return jnp.sum(jnp.where(owner == lax.broadcasted_iota(jnp.int32, shape, 0), column, 0.0), 0, keepdims=True)


def rank(column, rows):
    shape = (column.shape[0], rows[0].shape[1])
    earlier = lax.broadcasted_iota(jnp.int32, shape, 1) < lax.broadcasted_iota(jnp.int32, shape, 0)
    alike = functools.reduce(jnp.logical_or, [column == row for row in rows])
    return jnp.sum(jnp.where(earlier & alike, 1.0, 0.0), 1, keepdims=True)


def number(shape, axis):
    return lax.broadcasted_iota(jnp.int32, shape, axis)


def real(values):
    return values.astype(jnp.float32)


def layer_kernel(
    query, cross, parents, dec_len, src_len, routes, gates, tokens, new_kv, gain, cache, memory, first, second,
    mixed, arrived,
    cache_v, memory_v, tokens_v, new_kv_v, gain_v, query_v, wish, packed, queries, wishes, crosses, bias, bias_c,
    outs, stats, owner_out, got, got_stats, cross_out, hidden_v, pages, slots, returned,
    held, first_v, second_v, picked, inner, total, to_twin, from_twin, to_chip, from_chip, far, result,
    l_sem, local, k_send, k_recv, n_send, n_recv, e_send, e_recv, b_send, b_recv, s_send, s_recv, c_send, c_recv,
    d_send, d_recv, r_send, r_recv,
    g_send, g_recv, o_send, o_recv, t_send, t_recv,
    y_send, y_recv, x_send, x_recv, f_send, f_recv, p_send, p_recv,
):
    dp, ex, z, y = place()
    x, core = lax.div(dp, 2), lax.rem(dp, 2)
    twin = x * 2 + 1 - core
    chip = [x, lax.rem(x + CHIPS - 1, CHIPS), lax.rem(x + 1, CHIPS), lax.rem(x + 2, CHIPS)]
    row_count, width = tokens.shape
    hidden = first.shape[-1]
    kind = tokens.dtype
    heads = width // HEAD
    span = cache.shape[1]
    quarter, reach = memory.shape[:2]
    cap = slots.shape[1]
    block = EXPERTS * cap
    scale = 1.0 / math.sqrt(HEAD)

    barrier = pltpu.get_barrier_semaphore()
    for a in range(BEAM):
        for b in range(GROUP):
            if a or b:
                greet(barrier, dp, lax.rem(z + a, BEAM) * GROUP + lax.rem(y + b, GROUP))
    greet(barrier, twin, ex)
    for side in (LEFT, RIGHT, OPPOSITE):
        greet(barrier, chip[side] * 2 + core, ex)
    pairs = (
        (query, query_v), (new_kv, new_kv_v), (cache, cache_v), (memory, memory_v),
        (tokens, tokens_v), (gain, gain_v), (first, first_v), (second, second_v),
    )
    loads = [pltpu.make_async_copy(a, b, l_sem.at[i]) for i, (a, b) in enumerate(pairs)]
    for i in (0, 3, 1, 2, 4, 5, 6, 7):
        loads[i].start()
    own_cross = pltpu.make_async_copy(cross.at[y], crosses.at[z], local.at[2])
    pl.when(z == y)(own_cross.start)

    parent_row = real(parents[...])
    parent = upright(parent_row)
    parent_rank = rank(parent, [parent_row])
    rank_row = flat(parent_rank)
    ticket = number((BEAM * PAGE_CAP, row_count), 0)
    chosen = (real(lax.div(ticket, PAGE_CAP)) == parent_row) & (real(lax.rem(ticket, PAGE_CAP)) == rank_row)
    chosen = real(chosen).astype(kind)
    wish[0:1, :row_count] = parents[...]
    loads[0].wait()
    lines = jnp.dot(chosen, query_v[...], preferred_element_type=jnp.float32).astype(kind)
    packed[...] = lines.reshape(packed.shape)
    pl.semaphore_wait(barrier, EXPERTS - 1 + 4)

    sent = []
    crossing = [
        send(cross.at[p], crosses.at[z], e_send.at[p], e_recv.at[z], dp, y * GROUP + p) for p in range(GROUP)
    ]
    for p in range(GROUP):
        pl.when(y * GROUP + p != ex)(crossing[p].start)
    asks = []
    for off in (1, 3, 2):
        other = lax.rem(z + off, BEAM)
        target = other * GROUP + y
        asks.append(send(wish, wishes.at[z], n_send.at[off - 1], n_recv.at[off - 1], dp, target))
        asks.append(send(packed.at[other], queries.at[z], k_send.at[off - 1], k_recv.at[off - 1], dp, target))
    for move in asks:
        move.start()
    queries[z] = packed[z]
    wishes[z] = wish[...]

    loads[1].wait()
    lane = number((row_count, HEAD), 1)
    own = jnp.zeros((row_count, HEAD), jnp.float32)
    for h in range(heads):
        spot = slice(h * HEAD, (h + 1) * HEAD)
        both = real(query_v[:, spot]) * real(new_kv_v[:, spot])
        own = own + jnp.where(lane == h, jnp.sum(both, -1, keepdims=True) * scale, 0.0)
    named_rows = [real(routes[k : k + 1, :]) for k in range(2)]
    named = [upright(row) for row in named_rows]
    slot = [column * float(cap) + rank(column, named_rows) for column in named]
    slot_rows = [flat(column) for column in slot]

    at = number((row_count, dec_len.shape[1]), 1) - y * row_count == number((row_count, dec_len.shape[1]), 0)
    lengths = jnp.sum(jnp.where(at, real(dec_len[...]), 0.0), 1, keepdims=True)
    keys = row_count * span
    in_reach = real(lax.rem(number((1, keys), 1), span)) < spread(lengths, span)
    keys_c = quarter * reach
    in_reach_c = real(lax.rem(number((1, keys_c), 1), reach)) < spread(upright(real(src_len[...])), reach)
    asked_c = BEAM * quarter
    same_c = lax.rem(number((asked_c, keys_c), 0), quarter) == lax.div(number((asked_c, keys_c), 1), reach)
    for half in range(2):
        bias_c[half * asked_c : (half + 1) * asked_c, :] = jnp.where(same_c & in_reach_c, 0.0, -1e30)

    pair = 2 * HEAD
    batch = math.gcd(heads // 2, 8)

    def attend(asker, keeper, extra, base):
        blank = jnp.zeros((asker.shape[0], HEAD), kind)
        both = jnp.concatenate(
            [
                jnp.concatenate([asker[:, :HEAD], blank], 1),
                jnp.concatenate([blank, asker[:, HEAD:]], 1),
            ],
            0,
        )
        keys_of = keeper(base)
        scores = lax.dot_general(both, keys_of, (((1,), (1,)), ((), ())), preferred_element_type=jnp.float32)
        scores = scores * scale + extra[...]
        peak = jnp.max(scores, -1, keepdims=True)
        terms = jnp.exp(scores - peak)
        mass = jnp.sum(terms, -1, keepdims=True)
        part = jnp.dot((terms / mass).astype(kind), keeper(width + base), preferred_element_type=jnp.float32)
        return part.astype(kind), peak + jnp.log(mass)

    for p in range(GROUP):
        pl.when(y * GROUP + p != ex)(crossing[p].wait_send)
    for beam in range(BEAM):
        coming = send(cross.at[0], crosses.at[beam], e_send.at[0], e_recv.at[beam], dp, beam * GROUP + z)
        pl.when(beam * GROUP + z != ex)(coming.wait_recv)
    pl.when(z == y)(own_cross.wait)
    loads[3].wait()

    @pl.loop(0, heads // 2 // batch)
    def _(n):
        for m in range(batch):
            base = (n * batch + m) * pair
            spot = pl.ds(pl.multiple_of(base, pair), pair)

            def keeper(start):
                return memory_v[:, :, pl.ds(pl.multiple_of(start, pair), pair)].reshape(keys_c, pair)

            part, _ = attend(crosses[:, :, spot].reshape(asked_c, pair), keeper, bias_c, base)
            for half in range(2):
                piece = part[half * asked_c : (half + 1) * asked_c, half * HEAD : (half + 1) * HEAD]
                place_at = pl.ds(pl.multiple_of(base + half * HEAD, HEAD), HEAD)
                owner_out[:, :, place_at] = piece.reshape(BEAM, quarter, HEAD)

    own_back = pltpu.make_async_copy(owner_out.at[z], cross_out.at[y], local.at[2])
    crossing = [
        send(owner_out.at[beam], cross_out.at[y], c_send.at[beam], c_recv.at[y], dp, beam * GROUP + z)
        for beam in range(BEAM)
    ]
    for beam in range(BEAM):
        pl.when(beam * GROUP + z != ex)(crossing[beam].start)
    pl.when(z == y)(own_back.start)

    loads[2].wait()
    for move in asks:
        move.wait()
    asked = BEAM * PAGE_CAP
    ticket = real(number((PAGE_CAP, keys), 0))
    codes = []
    for beam in range(BEAM):
        wanted_row = real(wishes[beam, 0:1, :row_count])
        wanted = upright(wanted_row)
        code = spread(jnp.where(wanted == real(z), rank(wanted, [wanted_row]), -1.0), span)
        codes.append(code)
        part = jnp.where((ticket == code) & in_reach, 0.0, -1e30)
        for half in range(2):
            first_row = half * asked + beam * PAGE_CAP
            bias[first_row : first_row + PAGE_CAP, :] = part
    stats[...] = jnp.zeros_like(stats)
    stat_lane = number((asked, HEAD), 1)

    @pl.loop(0, heads // 2 // batch)
    def _(n):
        for m in range(batch):
            base = (n * batch + m) * pair
            spot = pl.ds(pl.multiple_of(base, pair), pair)

            def keeper(start):
                return cache_v[:, :, pl.ds(pl.multiple_of(start, pair), pair)].reshape(keys, pair)

            part, level = attend(queries[:, :, spot].reshape(asked, pair), keeper, bias, base)
            levels = jnp.zeros((asked, HEAD), jnp.float32)
            for half in range(2):
                rows = slice(half * asked, (half + 1) * asked)
                piece = part[rows, half * HEAD : (half + 1) * HEAD].reshape(BEAM, PAGE_CAP, HEAD)
                outs[:, :, pl.ds(pl.multiple_of(base + half * HEAD, HEAD), HEAD)] = piece
                levels = jnp.where(stat_lane == 2 * (n * batch + m) + half, level[rows], levels)
            stats[...] += levels.reshape(BEAM, PAGE_CAP, HEAD)

    answers = []
    for off in (1, 3, 2):
        other = lax.rem(z + off, BEAM)
        target = other * GROUP + y
        answers.append(send(stats.at[other], got_stats.at[z], b_send.at[off - 1], b_recv.at[off - 1], dp, target))
        answers.append(send(outs.at[other], got.at[z], s_send.at[off - 1], s_recv.at[off - 1], dp, target))
    for move in answers:
        move.start()
    got[z] = outs[z]
    got_stats[z] = stats[z]

    paged = []

    def turn(off, start, stop, which):
        rows = pl.ds(start, stop - start)
        move = send(
            pages.at[off - 1, rows], arrived.at[off - 1, rows], p_send.at[off - 1, which], p_recv.at[off - 1, which],
            dp, lax.rem(z + off, BEAM) * GROUP + y,
        )
        move.start()
        paged.append(move)

    page_shape = (PAGE_CAP * span, keys)
    page_row, page_lane = number(page_shape, 0), number(page_shape, 1)
    page_slot = real(lax.div(page_row, span))
    same_place = lax.rem(page_row, span) == lax.rem(page_lane, span)
    strip = min(1024, 2 * width)
    for off in (1, 3, 2):
        asker = lax.rem(z + off, BEAM)
        code = jnp.zeros_like(codes[0])
        for beam in range(BEAM):
            code = code + jnp.where(real(asker) == float(beam), codes[beam], 0.0)
        pick = real(same_place & (page_slot == code)).astype(kind)

        @pl.loop(0, 2 * width // strip)
        def _(n):
            spot = pl.ds(pl.multiple_of(n * strip, strip), strip)
            part = jnp.dot(pick, cache_v[:, :, spot].reshape(keys, strip), preferred_element_type=jnp.float32)
            pages[off - 1, :, :, spot] = part.astype(kind).reshape(PAGE_CAP, span, strip)

        if off != 2 and EARLY:
            turn(off, 0, EARLY, 0)

    for load in loads[4:6]:
        load.wait()
    for move in answers:
        move.wait()
    for beam in range(BEAM):
        pl.when(beam * GROUP + z != ex)(crossing[beam].wait_send)
    for p in range(GROUP):
        coming = send(owner_out.at[0], cross_out.at[p], c_send.at[0], c_recv.at[p], dp, y * GROUP + p)
        pl.when(y * GROUP + p != ex)(coming.wait_recv)
    pl.when(z == y)(own_back.wait)

    ticket = number((row_count, asked), 1)
    chosen = (parent == real(lax.div(ticket, PAGE_CAP))) & (parent_rank == real(lax.rem(ticket, PAGE_CAP)))
    chosen = real(chosen)
    level = jnp.dot(
        chosen,
        got_stats[...].reshape(asked, HEAD),
        precision=lax.Precision.HIGHEST,
        preferred_element_type=jnp.float32,
    )
    cached = jnp.dot(chosen.astype(kind), got[...].reshape(asked, width), preferred_element_type=jnp.float32)
    top = jnp.maximum(level, own)
    cache_part = jnp.exp(level - top)
    own_part = jnp.exp(own - top)
    cache_share = cache_part / (cache_part + own_part)
    own_share = own_part / (cache_part + own_part)
    for h in range(heads):
        spot = slice(h * HEAD, (h + 1) * HEAD)
        own_value = real(new_kv_v[:, width + h * HEAD : width + (h + 1) * HEAD])
        mine = cache_share[:, h : h + 1] * cached[:, spot] + own_share[:, h : h + 1] * own_value
        crossed = real(cross_out[:, :, spot].reshape(row_count, HEAD))
        hidden_v[:, spot] = real(tokens_v[:, spot]) + mine + crossed
    whole = hidden_v[...]
    centered = whole - jnp.mean(whole, -1, keepdims=True)
    variance = jnp.mean(centered * centered, -1, keepdims=True)
    moe_in = (centered * lax.rsqrt(variance + 1e-05) * gain_v[...]).astype(kind)
    slot_row = real(number((block, row_count), 0))
    table = real((slot_row == slot_rows[0]) | (slot_row == slot_rows[1])).astype(kind)
    packets = jnp.dot(table, moe_in, preferred_element_type=jnp.float32).astype(kind)
    slots[...] = packets.reshape(slots.shape)

    def peer(a, b):
        return lax.rem(z + a, BEAM) * GROUP + lax.rem(y + b, GROUP)

    def source(a, b):
        return lax.rem(z + BEAM - a, BEAM) * GROUP + lax.rem(y + GROUP - b, GROUP)

    home = held.at[x, core]
    stay = pltpu.make_async_copy(slots.at[ex], home.at[ex], local.at[0])
    stay.start()
    for a in ORDER:
        for b in range(GROUP):
            if a or b:
                spot = a * GROUP + b
                move = send(slots.at[peer(a, b)], home.at[ex], d_send.at[spot], d_recv.at[spot], dp, peer(a, b))
                move.start()
                sent.append(move)

    if MID:
        for off in (1, 3):
            turn(off, EARLY, EARLY + MID, 2)

    def chunk(which, owner, j):
        zz = lax.rem(z + BEAM - ORDER[j], BEAM)
        return held.at[chip[which], owner, pl.ds(zz * GROUP, GROUP)]

    def to_sibling(which, j):
        part = chunk(which, core, j)
        move = send(part, part, t_send.at[which, j], t_recv.at[which, j], twin, ex)
        move.start()
        sent.append(move)

    def from_sibling(which):
        for j in range(4):
            part = chunk(which, 1 - core, j)
            send(part, part, t_send.at[which, j], t_recv.at[which, j], twin, ex).wait_recv()

    stay.wait()
    for j, a in enumerate(ORDER):
        for b in range(GROUP):
            if a or b:
                spot = a * GROUP + b
                there = home.at[source(a, b)]
                send(there, there, d_send.at[spot], d_recv.at[spot], dp, source(a, b)).wait_recv()
        part = chunk(OWN, core, j)
        for way, side in ((0, RIGHT), (1, LEFT)):
            move = send(part, part, g_send.at[way, j], g_recv.at[way, j], chip[side] * 2 + core, ex)
            move.start()
            sent.append(move)
        to_sibling(OWN, j)

    cells = picked.shape[0] // 2
    tile = min(1024, hidden)
    wide = min(1024, width)
    slim = min(1024, width)
    band = block // 4

    def up(which):
        for half, owner in ((0, core), (1, 1 - core)):
            picked[half * cells : (half + 1) * cells, :] = held[chip[which], owner].reshape(cells, width)

        @pl.loop(0, hidden // tile)
        def _(n):
            spot = pl.ds(pl.multiple_of(n * tile, tile), tile)
            part = jnp.dot(picked[...], first_v[:, spot], preferred_element_type=jnp.float32)
            inner[:, spot] = jnp.maximum(part, 0.0).astype(inner.dtype)

    def down(which):
        for n in range(width // wide):
            spot = slice(n * wide, (n + 1) * wide)
            part = jnp.dot(inner[...], second_v[:, spot], preferred_element_type=jnp.float32)
            total[which, :, spot] = part[:cells]
            to_twin[which, :, spot] = part[cells:].astype(to_twin.dtype)
            move = twin_half(which, n)
            move.start()
            sent.append(move)

    def twin_half(which, n):
        spot = pl.ds(n * wide, wide)
        return send(
            to_twin.at[which, :, spot], from_twin.at[which, :, spot], y_send.at[which, n], y_recv.at[which, n], twin, ex
        )

    def forward(which):
        for n in range(width // wide):
            twin_half(which, n).wait_recv()
            spot = slice(n * wide, (n + 1) * wide)
            both = total[which, :, spot] + from_twin[which, :, spot].astype(jnp.float32)
            to_chip[which - 1, :, spot] = both.astype(to_chip.dtype)

        if which == OPPOSITE:
            far_leg(0)
            far_leg(2)
        else:
            for q in (2, 3) if which == RIGHT else (0, 1):
                last_leg(which, q)

    def relay(src, dst, send_sem, recv_sem, side):
        move = send(src, dst, send_sem, recv_sem, chip[side] * 2 + core, ex)
        move.start()
        sent.append(move)

    def far_leg(q):
        rows = pl.ds(q * band, band)
        relay(to_chip.at[2, rows], far.at[rows], f_send.at[q], f_recv.at[q], RIGHT if q < 2 else LEFT)

    def last_leg(which, q):
        rows = pl.ds(q * band, band)
        spot = which - 1
        relay(to_chip.at[spot, rows], from_chip.at[spot, rows], x_send.at[spot, q], x_recv.at[spot, q], which)

    def merge(q):
        rows = pl.ds(q * band, band)
        which = RIGHT if q < 2 else LEFT
        there = far.at[rows]
        send(there, there, f_send.at[q], f_recv.at[q], dp, ex).wait_recv()
        if q in (0, 2):
            far_leg(q + 1)

        @pl.loop(0, width // slim)
        def _(n):
            spot = pl.ds(pl.multiple_of(n * slim, slim), slim)
            both = to_chip[which - 1, rows, spot].astype(jnp.float32) + far[rows, spot].astype(jnp.float32)
            to_chip[which - 1, rows, spot] = both.astype(to_chip.dtype)

        last_leg(which, q)

    def landed(way, j):
        side = LEFT if way == 0 else RIGHT
        part = chunk(side, core, j)
        send(part, part, g_send.at[way, j], g_recv.at[way, j], dp, ex).wait_recv()
        to_sibling(side, j)
        if (j < 2) == (way == 0):
            onward = RIGHT if way == 0 else LEFT
            move = send(part, part, o_send.at[j], o_recv.at[j], chip[onward] * 2 + core, ex)
            move.start()
            sent.append(move)

    for off in (1, 3, 2):
        begin = EARLY + MID if off != 2 else 0
        turn(off, begin, PAGE_CAP, 1)
    for load in loads[6:8]:
        load.wait()
    from_sibling(OWN)
    up(OWN)
    down(OWN)
    for j in range(4):
        landed(0, j)
        landed(1, j)
    from_sibling(LEFT)
    up(LEFT)
    down(LEFT)
    from_sibling(RIGHT)
    up(RIGHT)
    forward(LEFT)
    down(RIGHT)
    for j in range(4):
        part = chunk(OPPOSITE, core, j)
        send(part, part, o_send.at[j], o_recv.at[j], dp, ex).wait_recv()
        to_sibling(OPPOSITE, j)
    forward(RIGHT)
    from_sibling(OPPOSITE)
    up(OPPOSITE)
    down(OPPOSITE)
    forward(OPPOSITE)
    for q in (0, 2, 1, 3):
        merge(q)

    for n in range(width // wide):
        twin_half(OWN, n).wait_recv()
    stay = pltpu.make_async_copy(result.at[ex], returned.at[ex], local.at[1])
    for q in (0, 2, 1, 3):
        rows = pl.ds(q * band, band)
        for spot in (0, 1):
            there = from_chip.at[spot, rows]
            send(there, there, x_send.at[spot, q], x_recv.at[spot, q], dp, ex).wait_recv()

        @pl.loop(0, width // slim)
        def _(n):
            spot = pl.ds(pl.multiple_of(n * slim, slim), slim)
            whole = total[OWN, rows, spot] + from_twin[OWN, rows, spot].astype(jnp.float32)
            for side in (0, 1):
                whole = whole + from_chip[side, rows, spot].astype(jnp.float32)
            packets = whole.astype(result.dtype).reshape(GROUP, cap, slim)
            result[q * GROUP : (q + 1) * GROUP, :, spot] = packets

        for target in range(q * GROUP, (q + 1) * GROUP):
            move = send(result.at[target], returned.at[ex], r_send.at[target], r_recv.at[ex], dp, target)
            pl.when(target != ex)(move.start)
            pl.when(target == ex)(stay.start)
    for origin in range(EXPERTS):
        there = returned.at[origin]
        move = send(there, there, r_send.at[origin], r_recv.at[origin], dp, origin)
        pl.when(origin != ex)(move.wait)
    stay.wait()
    back = returned[...].reshape(block, width)
    places = real(number((row_count, block), 1))
    final = hidden_v[...]
    for k in range(2):
        taken = real(places == slot[k]).astype(kind)
        final = final + upright(gates[k : k + 1, :]) * jnp.dot(taken, back, preferred_element_type=jnp.float32)
    mixed[...] = final.astype(mixed.dtype)
    for move in sent:
        move.wait_send()
    for move in paged:
        move.wait()


def layer(*operands):
    tokens, _, _, cache, memory, first, second = operands[7:]
    row_count, width = tokens.shape
    hidden = first.shape[-1]
    kind = tokens.dtype
    cap = 4 * row_count // EXPERTS
    block = EXPERTS * cap
    quarter = row_count // BEAM

    def room(*shape, dtype=kind):
        return pltpu.VMEM(shape, dtype)

    paged = (BEAM - 1, PAGE_CAP) + cache.shape[1:]
    scratch = [
        room(*cache.shape), room(*memory.shape), room(row_count, width), room(row_count, 2 * width),
        room(1, width, dtype=jnp.float32), room(row_count, width), room(8, HEAD, dtype=jnp.int32),
        room(BEAM, PAGE_CAP, width), room(BEAM, PAGE_CAP, width), room(BEAM, 8, HEAD, dtype=jnp.int32),
        room(BEAM, quarter, width), room(2 * BEAM * PAGE_CAP, row_count * cache.shape[1], dtype=jnp.float32),
        room(2 * BEAM * quarter, quarter * memory.shape[1], dtype=jnp.float32),
        room(BEAM, PAGE_CAP, width), room(BEAM, PAGE_CAP, HEAD, dtype=jnp.float32), room(BEAM, quarter, width),
        room(BEAM, PAGE_CAP, width), room(BEAM, PAGE_CAP, HEAD, dtype=jnp.float32), room(BEAM, quarter, width),
        room(row_count, width, dtype=jnp.float32), room(*paged), room(EXPERTS, cap, width), room(EXPERTS, cap, width),
        room(CHIPS, 2, EXPERTS, cap, width), room(*first.shape), room(*second.shape),
        room(2 * block, width), room(2 * block, hidden), room(4, block, width, dtype=jnp.float32),
        room(4, block, width), room(4, block, width), room(3, block, width), room(2, block, width),
        room(block, width), room(EXPERTS, cap, width),
    ]
    sems = [
        DMA((8,)), DMA((3,)), DMA((3,)), DMA((3,)), DMA((3,)), DMA((3,)), DMA((4,)), DMA((4,)),
        DMA((3,)), DMA((3,)), DMA((3,)), DMA((3,)), DMA((4,)), DMA((4,)),
        DMA((16,)), DMA((16,)), DMA((16,)), DMA((16,)),
        DMA((2, 4)), DMA((2, 4)), DMA((4,)), DMA((4,)), DMA((4, 4)), DMA((4, 4)),
        DMA((4, 2)), DMA((4, 2)), DMA((2, 4)), DMA((2, 4)), DMA((4,)), DMA((4,)), DMA((3, 3)), DMA((3, 3)),
    ]
    return pl.pallas_call(
        layer_kernel,
        out_shape=[jax.ShapeDtypeStruct((row_count, width), kind), jax.ShapeDtypeStruct(paged, kind)],
        in_specs=[ANY] * 2 + [pl.BlockSpec(memory_space=pltpu.VMEM)] * 5 + [ANY] * 7,
        out_specs=[pl.BlockSpec(memory_space=pltpu.VMEM), ANY],
        scratch_shapes=scratch + sems,
        compiler_params=pltpu.CompilerParams(
            collective_id=0, has_side_effects=True, vmem_limit_bytes=58 * 2**20
        ),
        name="layer",
    )(*operands)


def per_device(
    tokens,
    self_query,
    new_kv,
    kv_cache,
    parents,
    dec_len,
    cross_query,
    memory,
    src_len,
    norm_gain,
    routes,
    gate_weights,
    expert_in,
    expert_out,
):
    row_count, model_width = tokens.shape
    mixed, arrived = layer(
        self_query,
        cross_query.reshape(GROUP, row_count // BEAM, model_width),
        parents[None],
        dec_len[None],
        src_len[None],
        routes.T,
        gate_weights.T,
        tokens,
        new_kv,
        norm_gain[None],
        kv_cache,
        memory,
        expert_in[0],
        expert_out[0],
    )
    fresh, mixed = unpack(parents, kv_cache, arrived, mixed)
    return (mixed, fresh)


def solution(mesh):
    placed = (
        P(("dp", "expert"), None),
        P(("dp", "expert"), None),
        P(("dp", "expert"), None),
        P(("dp", "expert"), None, None),
        P(("dp", "expert")),
        P("dp"),
        P(("dp", "expert"), None),
        P(("dp", "expert"), None, None),
        P(("dp", "expert")),
        P(),
        P(("dp", "expert"), None),
        P(("dp", "expert"), None),
        P("expert", None, "dp"),
        P("expert", "dp", None),
    )
    return jax.shard_map(
        per_device,
        mesh=mesh,
        in_specs=placed,
        out_specs=(P(("dp", "expert"), None), P(("dp", "expert"), None, None)),
        check_vma=False,
    )
```
